32 devices in a mesh: groups: 2 (over y), inner: 4 (over z), outer: 4 (over x, core).
Axes of the slice: x: 2, y: 2, z: 4, core: 2. Of those that a mesh axis runs over, the one named last changes fastest.
Arguments:
- signal: bfloat16 [4096, 1024], P(('groups', 'inner', 'outer')), parts along dimension 0, may hold values from -6 to 6
- in_coeff: bfloat16 [4096, 32], P(('groups', 'inner', 'outer')), parts along dimension 0, may hold values from -6 to 6
- out_coeff: bfloat16 [4096, 32], P(('groups', 'inner', 'outer')), parts along dimension 0, may hold values from -0.03125 to 0.03125
- cotangent: bfloat16 [4096, 1024], P(('groups', 'inner', 'outer')), parts along dimension 0, may hold values from -6 to 6
- conv_weight: float32 [2, 4, 1024], replicated, may hold values from -3 to 3
- conv_bias: float32 [2, 1024], replicated, may hold values from -3 to 3
- skip_gain: float32 [2, 16], replicated, may hold values from 0.5 to 1.5
- decay_table: float32 [2, 16, 16], replicated, as said below
- bucket: int32 [4096], P(('groups', 'inner', 'outer')), parts along dimension 0, may hold values from 0 to 15
- segment: int32 [4096], P(('groups', 'inner', 'outer')), parts along dimension 0, may hold values from 0 to 3, never falling along the last dimension, each value on 1 to 1024 neighbouring positions
Outputs:
- mixed: bfloat16 [4096, 1024], P(('groups', 'inner', 'outer')), parts along dimension 0
- grad_input: bfloat16 [4096, 1024], P(('groups', 'inner', 'outer')), parts along dimension 0
The draws below stay inside these ranges and needn't reach their ends.
There are 2 independent parts, one for each index of `groups`. The reference program is written for one: setup_inputs(seed, part) draws one part's arguments, and reference() takes and returns one part's arrays. A program takes and returns all parts, laid end to end along the dimension named above; an argument that names none is the same for every part. Nothing has to cross between parts.
Inputs may be any that keep to these rules, and one draw needn't show every extreme that they name: segment numbers never fall along the sequence. `decay_table`: entries are logarithms of decay factors.
All inputs are finite; a program needn't handle non-finite values.
Results may differ from the reference program's by a relative error of at most 0.005.
Values may be sent and summed in bfloat16 or wider, within the bound.
No kernel may reach another device: no remote copies, remote signals or barrier semaphores. Data moves between devices by JAX's collectives and lax.ppermute only.
A program may use at most 512 MiB of HBM per device.

```python
import math
import jax
import jax.numpy as jnp
import numpy as np
from jax import lax

PAIRED_CHANNELS = 16
HDIM = 64
NSTATE = 32
KW = 4
FADING_TABLE_LEN = 16
TOK_DEV = 128
SEQ = 2048


def draw_bucket(key, part):
    keyed_matrix_lines = jax.random.split(key, 3)
    blocks = SEQ // TOK_DEV
    hierarchy_depth = jax.random.randint(keyed_matrix_lines[0], (blocks,), 0, FADING_TABLE_LEN - 4)
    jitter = jax.random.randint(keyed_matrix_lines[1], (SEQ,), 0, 4)
    result = jnp.repeat(hierarchy_depth, TOK_DEV, total_repeat_length=SEQ) + jitter
    places = jax.random.randint(keyed_matrix_lines[2], (3,), 0, SEQ)
    result = result.at[places].set(FADING_TABLE_LEN - 1)
    result = result.at[0].set(0)
    return result.astype(jnp.int32)


def draw_decay_table(key, part):
    keyed_matrix_lines = jax.random.split(key, 5)
    picker = jax.random.uniform(keyed_matrix_lines[0], (2, 1, PAIRED_CHANNELS), jnp.float32)
    slow = picker < 0.5
    slow_rate = -jax.random.uniform(keyed_matrix_lines[1], (2, 1, PAIRED_CHANNELS), jnp.float32, 0.2, 0.5) * 2.0 / SEQ
    fast_rate = -jax.random.uniform(keyed_matrix_lines[2], (2, 1, PAIRED_CHANNELS), jnp.float32, 1.0 / 50.0, 1.0 / 30.0)
    base = jnp.where(slow, slow_rate, fast_rate)
    hierarchy_depth = jnp.arange(FADING_TABLE_LEN, dtype=jnp.float32)
    factor = jnp.exp2((hierarchy_depth - 7.0) / 7.0)[None, :, None]
    jitter = jax.random.uniform(keyed_matrix_lines[3], (2, FADING_TABLE_LEN, PAIRED_CHANNELS), jnp.float32, 0.8, 1.25)
    fading_factor_table = base * factor * jitter
    span_extent = jnp.log(jax.random.uniform(keyed_matrix_lines[4], (2, 1, PAIRED_CHANNELS), jnp.float32, 0.55, 0.8))
    fading_factor_table = jnp.where(hierarchy_depth[None, :, None] == FADING_TABLE_LEN - 1, span_extent, fading_factor_table)
    return fading_factor_table.astype(jnp.float32)


def block_levels(stream_key, dims, cuts, least, largest):
    def one(dim, parts):
        draws = jax.random.uniform(jax.random.fold_in(jax.random.fold_in(stream_key, 6), dim), (parts,), jnp.float32, least / len(cuts), largest / len(cuts))
        return jnp.repeat(jnp.exp(draws), dims[dim] // parts).reshape((-1,) + (1,) * (len(dims) - dim - 1))

    loudness = one(*cuts[0])
    for cut in cuts[1:]:
        loudness = loudness * one(*cut)
    return loudness


def profile(amount, total, limit, lean):
    weights = [(1 << 20) // math.isqrt(standing ** lean) + 1 for standing in range(2, amount + 1)]
    surplus, counts = total - limit - (amount - 1), [1] * (amount - 1)
    while surplus > 0:
        candidates = [i for i in range(amount - 1) if counts[i] < limit]
        whole, budget = sum([weights[i] for i in candidates]), surplus
        for i in candidates:
            extra = min(limit - counts[i], max(1, budget * weights[i] // whole), surplus)
            counts[i] = counts[i] + extra
            surplus = surplus - extra
    return np.array([limit] + counts)


def ragged_sizes(stream_key, count, total, reach, slope):
    if count == 2:
        one = jax.random.randint(stream_key, (), max(1, total - reach), min(reach, total - 1) + 1)
        return jnp.stack([one, total - one])
    lengths = jnp.asarray(profile(count, total, reach, slope), jnp.int32)
    couples = (count - 1) // 2
    giver, sink = lengths[1:1 + 2 * couples:2], lengths[2:2 + 2 * couples:2]
    room = jnp.minimum(giver - 1, reach - sink)
    shifted = jax.random.randint(jax.random.fold_in(stream_key, 1), (couples,), 0, 1 << 20) % (room + 1)
    lengths = lengths.at[1:1 + 2 * couples:2].set(giver - shifted).at[2:2 + 2 * couples:2].set(sink + shifted)
    return lengths[jax.random.permutation(jax.random.fold_in(stream_key, 2), count)]


def bell_draw(own_key, shape, scale, most, cuts=(), kind=jnp.bfloat16):
    level = block_levels(own_key, shape, cuts, -0.22, 0.18) if cuts else 1.0
    drawn = jax.random.normal(own_key, shape, jnp.float32) * scale * level
    return jnp.minimum(jnp.maximum(drawn, -most), most).astype(kind)


def setup_inputs(seed: int = 0, part: int = 0) -> dict:
    keys = jax.random.split(jax.random.key(seed), 11)
    part_splits = jax.random.split(jax.random.fold_in(keys[10], part), 11)
    return {
        "signal": bell_draw(part_splits[0], (SEQ, PAIRED_CHANNELS * HDIM), 1.0, 6.0, ((0, 16),)),
        "in_coeff": bell_draw(part_splits[1], (SEQ, NSTATE), 1.0, 6.0, ((0, 16),)),
        "out_coeff": bell_draw(part_splits[2], (SEQ, NSTATE), (NSTATE * 1024) ** -0.5, 0.03125, ((0, 16),)),
        "cotangent": bell_draw(part_splits[3], (SEQ, PAIRED_CHANNELS * HDIM), 1.0, 6.0, ((0, 16),)),
        "conv_weight": bell_draw(keys[4], (2, KW, PAIRED_CHANNELS * HDIM), 0.5, 3.0, (), jnp.float32),
        "conv_bias": bell_draw(keys[5], (2, PAIRED_CHANNELS * HDIM), 0.5, 3.0, (), jnp.float32),
        "skip_gain": jnp.clip(jax.random.uniform(keys[6], (2, PAIRED_CHANNELS), jnp.float32, 0.5, 1.5), 0.5, 1.5),
        "decay_table": draw_decay_table(jax.random.fold_in(keys[10], 71), part),
        "bucket": draw_bucket(jax.random.fold_in(jax.random.fold_in(keys[10], part), 71), part),
        "segment": jnp.searchsorted(jnp.cumsum(ragged_sizes(part_splits[9], 4, SEQ, SEQ // 2, 0)), jnp.arange(SEQ), side="right").astype(jnp.int32),
    }


EXACT = lax.Precision.HIGHEST


def local_pass(query, keyvec, values, rates, seg, exclusive):
    cumul = jnp.cumsum(rates, axis=0)
    potential = cumul - rates if exclusive else cumul
    total = cumul[-1]
    scores = jnp.dot(query, keyvec.T, precision=EXACT)
    row_ids = lax.broadcasted_iota(jnp.int32, scores.shape, 0)
    col_ids = lax.broadcasted_iota(jnp.int32, scores.shape, 1)
    allowed = (row_ids >= col_ids) & (seg[:, None] == seg[None, :])
    spread = potential.T[:, :, None] - potential.T[:, None, :]
    weights = jnp.where(allowed[None], jnp.exp(jnp.minimum(spread, 0.0)), 0.0) * scores[None]
    inner = jnp.einsum("hqk,khp->qhp", weights, values, precision=EXACT)
    tail_same = (seg == seg[-1]).astype(rates.dtype)
    fading = jnp.exp(total[None, :] - potential) * tail_same[:, None]
    weighted_keys = fading.T[:, :, None] * keyvec[None, :, :]
    summary = jnp.einsum("hkn,khp->hnp", weighted_keys, values, precision=EXACT)
    decay = jnp.exp(total) * (seg[0] == seg[-1]).astype(rates.dtype)
    return inner, jnp.exp(potential), summary, decay


def apply_carry(inner, entry_gate_weight, query, seg, state, exit_seg):
    same = (seg == exit_seg).astype(inner.dtype)
    incoming = jnp.einsum("qn,hnp->qhp", query, state, precision=EXACT)
    return inner + incoming * (entry_gate_weight * same[:, None])[:, :, None]


def run_pass(query, keyvec, values, rates, seg, exclusive):
    length = query.shape[0]
    block = min(TOK_DEV, 128)
    count = length // block
    head_count = values.shape[1]
    blocks = (query.reshape(count, block, -1), keyvec.reshape(count, block, -1),
              values.reshape(count, block, head_count, -1), rates.reshape(count, block, head_count),
              seg.reshape(count, block))

    def advance(carry, piece):
        state, last_seg = carry
        q_part, k_part, v_part, r_part, s_part = piece
        inner, entry_gate_weight, summary, decay = local_pass(q_part, k_part, v_part, r_part, s_part, exclusive)
        output = apply_carry(inner, entry_gate_weight, q_part, s_part, state, last_seg)
        keep = decay * jnp.logical_or(s_part[0] == last_seg, last_seg < 0).astype(decay.dtype)
        return (summary + keep[:, None, None] * state, s_part[-1]), output

    start = (jnp.zeros((head_count, keyvec.shape[1], values.shape[2]), jnp.float32), jnp.array(-1, jnp.int32))
    carry, outputs = lax.scan(advance, start, blocks)
    return outputs.reshape(length, head_count, -1)


def mirror(array):
    return jnp.flip(array, 0)


def silu_slope(pre):
    sigma = jax.nn.sigmoid(pre)
    return sigma * (1.0 + pre * (1.0 - sigma))


def reference(signal, in_coeff, out_coeff, cotangent, conv_weight, conv_bias, skip_gain, decay_table, bucket, segment):
    length, channels = signal.shape
    head_count = skip_gain.shape[1]
    head_size = channels // head_count
    margin = KW - 1
    source = signal.astype(jnp.float32)
    padded = jnp.pad(source, ((margin, margin), (0, 0)))
    pre_fwd = conv_bias[0] + sum(conv_weight[0, lag] * padded[margin - lag:margin - lag + length] for lag in range(KW))
    pre_rev = conv_bias[1] + sum(conv_weight[1, lag] * padded[margin + lag:margin + lag + length] for lag in range(KW))
    act_fwd = jax.nn.silu(pre_fwd).reshape(length, head_count, head_size)
    act_rev = jax.nn.silu(pre_rev).reshape(length, head_count, head_size)
    rate_fwd = decay_table[0][bucket]
    backward_speed_factor = decay_table[1][bucket]
    in_f = in_coeff.astype(jnp.float32)
    out_f = out_coeff.astype(jnp.float32)
    upstream_cotangent_input = cotangent.astype(jnp.float32).reshape(length, head_count, head_size)
    seg_back = mirror(segment)
    out_fwd = run_pass(out_f, in_f, act_fwd, rate_fwd, segment, False)
    out_rev = mirror(run_pass(mirror(out_f), mirror(in_f), mirror(act_rev), mirror(backward_speed_factor), seg_back, False))
    back_fwd = mirror(run_pass(mirror(in_f), mirror(out_f), mirror(upstream_cotangent_input), mirror(rate_fwd), seg_back, True))
    back_rev = run_pass(in_f, out_f, upstream_cotangent_input, backward_speed_factor, segment, True)
    gain_fwd = skip_gain[0][:, None]
    gain_rev = skip_gain[1][:, None]
    mixed = (out_fwd + gain_fwd * act_fwd + out_rev + gain_rev * act_rev).reshape(length, channels).astype(jnp.bfloat16)
    dpre_fwd = (back_fwd + gain_fwd * upstream_cotangent_input).reshape(length, channels) * silu_slope(pre_fwd)
    dpre_rev = (back_rev + gain_rev * upstream_cotangent_input).reshape(length, channels) * silu_slope(pre_rev)
    ext_fwd = jnp.pad(dpre_fwd, ((0, margin), (0, 0)))
    ext_rev = jnp.pad(dpre_rev, ((margin, 0), (0, 0)))
    gradient = sum(conv_weight[0, lag] * ext_fwd[lag:lag + length] + conv_weight[1, lag] * ext_rev[margin - lag:margin - lag + length] for lag in range(KW))
    return mixed, gradient.astype(jnp.bfloat16)
```

```python
import functools

import jax
import jax.numpy as jnp
from jax import lax
from jax.experimental import pallas as pl
from jax.experimental.pallas import tpu as pltpu
from jax.sharding import PartitionSpec as P

F32, BF16 = jnp.float32, jnp.bfloat16
EXACT = lax.Precision.HIGHEST
EDGE = 8
VMEM = 14 * 2**20


def mm(a, b, precision=None):
    return lax.dot_general(
        a, b, (((1,), (0,)), ((), ())), precision=precision, preferred_element_type=F32
    )


def mm_tn(a, b, precision=None):
    return lax.dot_general(
        a, b, (((0,), (0,)), ((), ())), precision=precision, preferred_element_type=F32
    )


def mm_nt(a, b, precision=None):
    return lax.dot_general(
        a, b, (((1,), (1,)), ((), ())), precision=precision, preferred_element_type=F32
    )


def iota(shape, dim):
    return lax.broadcasted_iota(jnp.int32, shape, dim)


def twice(heads):
    col = iota((heads, 2 * heads), 1)
    col = jnp.where(col < heads, col, col - heads)
    return (iota((heads, 2 * heads), 0) == col).astype(F32)


def spread(heads, lanes, hdim, start=0):
    row = iota((2 * heads, lanes), 0)
    row = jnp.where(row < heads, row, row - heads)
    low = row * hdim
    col = iota((2 * heads, lanes), 1) + start
    return ((col >= low) & (col < low + hdim)).astype(BF16)


def high_low(x):
    high = x.astype(BF16).astype(F32)
    return jnp.where(iota(x.shape, 1) < x.shape[1] // 2, high, x - high).astype(BF16)


def one_hot(column, size):
    return (column == iota((column.shape[0], size), 1).astype(column.dtype)).astype(F32)


def edges_kernel(sig_t, sig_b, cot_t, cot_b, in_t, in_b, out_t, out_b, bucket, segment, up, down):
    length = bucket.shape[1]
    channels = sig_t.shape[1]
    half = EDGE

    def put(target, column, value):
        target[:, column : column + value.shape[1]] = value.astype(BF16)

    bcol = jnp.transpose(jnp.broadcast_to(bucket[...].astype(F32), (length, length)))
    scol = jnp.transpose(jnp.broadcast_to(segment[...].astype(F32), (length, length)))
    for target, refs, lo, row in (
        (up, (sig_b, cot_b, in_b, out_b), half, length - EDGE),
        (down, (sig_t, cot_t, in_t, out_t), 0, 0),
    ):
        s, c, i, o = (r[...].astype(F32)[lo : lo + EDGE] for r in refs)
        put(target, 0, s)
        put(target, channels, c)
        put(target, 2 * channels, i)
        put(target, 2 * channels + 128, o)
        put(target, 2 * channels + 256, bcol[row : row + EDGE, :128])
        put(target, 2 * channels + 384, scol[row : row + EDGE, :128])


def edge_parts(ref, channels, state):
    x = ref[...]
    return (
        x[:, :channels].astype(F32),
        x[:, channels : 2 * channels].astype(F32),
        x[:, 2 * channels : 2 * channels + state].astype(F32),
        x[:, 2 * channels + 128 : 2 * channels + 128 + state].astype(F32),
        x[:, 2 * channels + 256 : 2 * channels + 257].astype(F32),
        x[:, 2 * channels + 384 : 2 * channels + 385].astype(F32),
    )


def conv(ext, start, rows, weight, bias, sl, step):
    total = bias
    for lag in range(weight.shape[0]):
        at = start + step * lag
        total = total + weight[lag : lag + 1, sl] * ext[at : at + rows, sl]
    return total


def begin_kernel(
    sig, cot, in_, out, bucket, segment, cw, cb, table, states, sums, sums_t, ext, edge
):
    length, channels = sig.shape
    heads = table.shape[2]
    rows = table.shape[1]
    nstate = in_.shape[1]
    hdim = channels // heads
    margin = cw.shape[1] - 1
    hot_t = (bucket[...] == iota((rows, length), 0)).astype(F32)
    tri = iota((length, length), 0) >= iota((length, length), 1)
    counts = mm_nt(tri.astype(F32), hot_t)
    strict = mm_nt((iota((length, length), 0) > iota((length, length), 1)).astype(F32), hot_t)
    upper = (iota((length, length), 0) <= iota((length, length), 1)).astype(F32)
    counts_t = mm(hot_t, upper)
    strict_t = counts_t - hot_t
    dup = twice(heads)
    table_f = mm(table[0], dup, EXACT)
    table_r = mm(table[1], dup, EXACT)
    cf = mm(counts, table_f, EXACT)
    cr = mm(strict, table_r, EXACT)
    ci = mm(counts, table_r, EXACT)
    sums[0], sums[1], sums[2] = cf, cr, ci
    sums_t[0:heads] = mm_tn(table[0], counts_t, EXACT)
    sums_t[heads : 2 * heads] = mm_tn(table[1], strict_t, EXACT)
    seg = segment[...]
    seg_col = jnp.transpose(jnp.broadcast_to(seg.astype(F32), (length, length)))[:, : 2 * heads]
    seg_row = seg.astype(F32)
    t = iota((length, 2 * heads), 0)
    last, near = length - 1, length - margin

    def fade(arg, anchor, keep):
        same = seg_col == seg_row[:, anchor : anchor + 1]
        return high_low(jnp.where(same & keep, jnp.exp(arg), 0.0))

    fade_f = fade(cf[last : last + 1] - cf, last, t >= margin)
    fade_br = fade(cr[near : near + 1] - cr, near - 1, t < near)
    fade_r = fade(cr, 0, t < near)
    fade_bf = fade(cf - cf[margin - 1 : margin], margin, t >= margin)
    ext[0:EDGE] = jnp.zeros((EDGE, channels), F32)
    ext[EDGE + length :] = jnp.zeros((EDGE, channels), F32)
    ext[EDGE : EDGE + length] = sig[...].astype(F32)
    edge[0 : 2 * heads] = spread(heads, channels, hdim)
    in_t = jnp.transpose(in_[...].astype(F32)).astype(BF16)
    out_t = jnp.transpose(out[...].astype(F32)).astype(BF16)
    wide = 256
    for c in range(0, channels, wide):
        sl = slice(c, c + wide)
        widen = edge[:, sl]
        pre = conv(ext, EDGE, length, cw[0], cb[0:1, sl], sl, -1)
        act = pre * jax.nn.sigmoid(pre)
        states[0:nstate, sl] = mm(in_t, (act * mm(fade_f, widen)).astype(BF16))
        pre = conv(ext, EDGE, length, cw[1], cb[1:2, sl], sl, 1)
        act = pre * jax.nn.sigmoid(pre)
        states[2 * nstate : 3 * nstate, sl] = mm(in_t, (act * mm(fade_r, widen)).astype(BF16))
        ct = cot[:, sl].astype(F32)
        states[nstate : 2 * nstate, sl] = mm(out_t, (ct * mm(fade_br, widen)).astype(BF16))
        states[3 * nstate :, sl] = mm(out_t, (ct * mm(fade_bf, widen)).astype(BF16))


def edge_sums(before, after, table, channels, state, heads, margin):
    dup = twice(heads)
    table_f = mm(table[0], dup, EXACT)
    table_r = mm(table[1], dup, EXACT)
    bs, bc, bi, bo, bb, bseg = edge_parts(before, channels, state)
    as_, ac, ai, ao, ab, aseg = edge_parts(after, channels, state)
    tri = (iota((EDGE, EDGE), 0) >= iota((EDGE, EDGE), 1)).astype(F32)
    rev = (iota((EDGE, EDGE), 0) <= iota((EDGE, EDGE), 1)).astype(F32)
    rows = table.shape[1]
    nf = mm(mm(tri, one_hot(ab, rows)), table_f, EXACT)
    pr = mm(mm(rev, one_hot(bb, rows)), table_r, EXACT)
    return (bs, bc, bi, bo, bseg), (as_, ac, ai, ao, aseg), nf, pr


def send_kernel(
    states, sums, sig_t, sig_b, in_t, in_b, segment, cw, cb, table, before, after, *rest, outer
):
    outs, (pay, near_f, near_r) = rest[:-3], rest[-3:]
    channels = sig_t.shape[1]
    heads = table.shape[2]
    nstate = in_t.shape[1]
    hdim = channels // heads
    margin = cw.shape[1] - 1
    length = segment.shape[1]
    prev, nxt, nf, pr = edge_sums(before, after, table, channels, nstate, heads, margin)
    bs, bc, bi, bo, bseg = prev
    as_, ac, ai, ao, aseg = nxt
    seg = segment[...].astype(F32)
    cf_l = sums[0, length - EDGE :]
    cf_0 = sums[0, 0:EDGE]
    cr_l = sums[1, length - EDGE :]
    ci_l = sums[2, length - EDGE :]
    total_f = cf_l[EDGE - 1 : EDGE]
    total_r = ci_l[EDGE - 1 : EDGE]
    j = iota((EDGE, 2 * heads), 0)
    col = jnp.transpose(jnp.broadcast_to(seg, (length, length)))[:, : 2 * heads]

    def at(t):
        return seg[:, t : t + 1]

    early = j < margin
    late = j >= EDGE - margin
    rows_f = jnp.where(early & (col[0:EDGE] == at(length - 1)), jnp.exp(total_f - cf_0), 0.0)
    rows_r = jnp.where(late & (col[length - EDGE :] == at(0)), jnp.exp(cr_l), 0.0)
    base_bf = total_f - cf_0[margin - 1 : margin]
    rows_bf = jnp.where(early & (aseg == at(margin)), jnp.exp(base_bf + nf), 0.0)
    base_br = cr_l[EDGE - margin : EDGE - margin + 1]
    rows_br = jnp.where(late & (bseg == at(length - margin - 1)), jnp.exp(base_br + pr), 0.0)
    keep_f = jnp.where(bseg[EDGE - 1 : EDGE] == at(length - 1), jnp.exp(total_f), 0.0)
    keep_r = jnp.where(aseg[0:1] == at(0), jnp.exp(total_r), 0.0)
    keep_bf = jnp.where(
        aseg[margin : margin + 1] == at(margin), jnp.exp(base_bf + nf[margin - 1 : margin]), 0.0
    )
    keep_br = jnp.where(
        bseg[EDGE - margin - 1 : EDGE - margin] == at(length - margin - 1),
        jnp.exp(base_br + pr[EDGE - margin : EDGE - margin + 1]),
        0.0,
    )
    which = j % 4
    keeps = jnp.where(
        which == 0, keep_f, jnp.where(which == 1, keep_br, jnp.where(which == 2, keep_r, keep_bf))
    )
    stack = high_low(jnp.concatenate([rows_f, rows_r, rows_bf, rows_br, keeps], axis=0))
    wide = mm(stack, spread(heads, channels, hdim))
    near_f[0:EDGE] = bs
    near_f[EDGE:] = sig_t[...].astype(F32)[0:EDGE]
    near_r[0:EDGE] = sig_b[...].astype(F32)[EDGE:]
    near_r[EDGE:] = as_
    everything = slice(0, channels)
    pre = conv(near_f, EDGE, EDGE, cw[0], cb[0:1, :], everything, -1)
    act_f = pre * jax.nn.sigmoid(pre)
    pre = conv(near_r, 0, EDGE, cw[1], cb[1:2, :], everything, 1)
    act_r = pre * jax.nn.sigmoid(pre)
    first = in_t[...].astype(F32)[0:EDGE]
    final = in_b[...].astype(F32)[EDGE:]
    for k, (left, right, row) in enumerate(
        ((first, act_f, 0), (bo, bc, 3), (final, act_r, 1), (ao, ac, 2))
    ):
        value = right * wide[row * EDGE : (row + 1) * EDGE]
        extra = mm_tn(left.astype(BF16), value.astype(BF16))
        pay[k * nstate : (k + 1) * nstate] = (
            states[k * nstate : (k + 1) * nstate] + extra
        ).astype(BF16)
    kept = wide[4 * EDGE :]
    high = kept.astype(BF16).astype(F32)
    kept = jnp.where(iota(kept.shape, 0) < 4, high, kept - high)
    pay[4 * nstate :] = jnp.concatenate([kept, jnp.zeros_like(kept)], axis=0).astype(BF16)
    width = channels // outer
    me = lax.axis_index("outer")
    for r in range(outer):
        at_ = pl.multiple_of((me ^ r) * width, 128)
        outs[r][...] = pay[:, pl.ds(at_, width)]


def read_block(block, nstate):
    x = block.astype(F32)
    keep = x[4 * nstate : 4 * nstate + 4] + x[4 * nstate + 4 : 4 * nstate + 8]
    return x, keep


def both(keep, first, nstate, width):
    row = iota((2 * nstate, width), 0)
    return jnp.where(row < nstate, keep[first : first + 1], keep[first + 1 : first + 2])


def totals_kernel(*refs, outer, inner, nstate):
    blocks, outs, held = refs[:outer], refs[outer:-1], refs[-1]
    me = lax.axis_index("outer")
    place = lax.axis_index("inner")
    width = blocks[0].shape[1]
    for r in range(outer):
        held[me ^ r] = blocks[r][...]
    n2 = 2 * nstate
    up, down = jnp.zeros((n2, width), F32), jnp.zeros((n2, width), F32)
    up_keep, down_keep = jnp.ones((2, width), F32), jnp.ones((2, width), F32)
    for k in range(outer):
        x, keep = read_block(held[k], nstate)
        up = x[0:n2] + both(keep, 0, nstate, width) * up
        up_keep = up_keep * keep[0:2]
        x, keep = read_block(held[outer - 1 - k], nstate)
        down = x[n2 : 2 * n2] + both(keep, 2, nstate, width) * down
        down_keep = down_keep * keep[2:4]
    tail = []
    for keep in (up_keep, down_keep):
        high = keep.astype(BF16).astype(F32)
        tail.append(jnp.concatenate([high, keep - high, jnp.zeros((12, width), F32)], axis=0))
    up = jnp.concatenate([up, tail[0]], axis=0).astype(BF16)
    down = jnp.concatenate([down, tail[1]], axis=0).astype(BF16)
    for r in range(1, inner):
        towards = jnp.full(up.shape, place ^ r, jnp.int32) > place
        outs[r - 1][...] = jnp.where(towards, up.astype(F32), down.astype(F32)).astype(BF16)


def entries_kernel(*refs, outer, inner, nstate):
    blocks = refs[:outer]
    others = refs[outer : outer + inner - 1]
    outs = refs[outer + inner - 1 : -3]
    held, far, entry = refs[-3:]
    me = lax.axis_index("outer")
    place = lax.axis_index("inner")
    width = blocks[0].shape[1]
    n2 = 2 * nstate
    for r in range(outer):
        held[me ^ r] = blocks[r][...]
    far[place] = jnp.zeros(far.shape[1:], BF16)
    for r in range(1, inner):
        far[place ^ r] = others[r - 1][...]

    def join(state, index, ahead):
        x = far[index].astype(F32)
        keep = x[n2 : n2 + 2] + x[n2 + 2 : n2 + 4]
        new = x[0:n2] + both(keep, 0, nstate, width) * state
        return jnp.where(jnp.full(new.shape, ahead), new, state)

    up, down = jnp.zeros((n2, width), F32), jnp.zeros((n2, width), F32)
    for k in range(inner - 1):
        up = join(up, k, k < place)
        back = inner - 1 - k
        down = join(down, back, back > place)
    for k in range(outer):
        entry[k, 0:n2] = up.astype(BF16)
        x, keep = read_block(held[k], nstate)
        up = x[0:n2] + both(keep, 0, nstate, width) * up
        back = outer - 1 - k
        entry[back, n2 : 2 * n2] = down.astype(BF16)
        x, keep = read_block(held[back], nstate)
        down = x[n2 : 2 * n2] + both(keep, 2, nstate, width) * down
    for r in range(outer):
        outs[r][...] = entry[me ^ r]


def local_kernel(
    sig, cot, in_, out, segment, cw, cb, skip, table, sums, sums_t, before, after,
    mixed, base_f, gate_f, base_r, gate_r, out_f, out_r, low, ext, widen,
    *, part, parts,
):
    length, channels = sig.shape
    heads = table.shape[2]
    nstate = in_.shape[1]
    hdim = channels // heads
    margin = cw.shape[1] - 1
    prev, nxt, nf, pr = edge_sums(before, after, table, channels, nstate, heads, margin)
    bs, bc, bi, bo, bseg = prev
    as_, ac, ai, ao, aseg = nxt
    seg = segment[...].astype(F32)
    col_full = jnp.transpose(jnp.broadcast_to(seg, (length, length)))
    col = col_full[:, : 2 * heads]
    cf, cr = sums[0], sums[1]
    total_f = cf[length - 1 : length]
    total_r = sums[2, length - EDGE :][EDGE - 1 : EDGE]
    j = iota((EDGE, 2 * heads), 0)
    early = j < margin
    late = j >= EDGE - margin
    s_first, s_last = aseg[0:1], bseg[EDGE - 1 : EDGE]
    s_beyond, s_ahead = aseg[margin : margin + 1], bseg[EDGE - margin - 1 : EDGE - margin]
    stack = [
        jnp.where(col == s_last, jnp.exp(cf), 0.0),
        jnp.where(col == s_first, jnp.exp(total_r - cr), 0.0),
        jnp.where(col == s_first, jnp.exp(total_f - cf), 0.0),
        jnp.where(col == s_last, jnp.exp(cr), 0.0),
        jnp.where(early & (aseg == s_beyond), jnp.exp(nf[margin - 1 : margin] - nf), 0.0),
        jnp.where(
            late & (bseg == s_ahead), jnp.exp(pr[EDGE - margin : EDGE - margin + 1] - pr), 0.0
        ),
        jnp.where(early & (aseg == s_first), jnp.exp(nf), 0.0),
        jnp.where(late & (bseg == s_last), jnp.exp(pr), 0.0),
        jnp.where(
            j < 4,
            jnp.where(s_first == s_beyond, jnp.exp(nf[margin - 1 : margin]), 0.0),
            jnp.where(s_last == s_ahead, jnp.exp(pr[EDGE - margin : EDGE - margin + 1]), 0.0),
        ),
    ]
    turned = []
    for d in range(margin):
        move = (EDGE - d) % EDGE
        later = pltpu.roll(nf, move, 0) if d else nf
        seg_j = jnp.broadcast_to(aseg, (EDGE, 2 * heads))
        seg_l = pltpu.roll(seg_j, move, 0) if d else seg_j
        ao_d = pltpu.roll(ao, move, 0) if d else ao
        dot = jnp.sum(ai * ao_d, axis=1, keepdims=True)
        stack.append(jnp.where((j + d < margin) & (seg_j == seg_l), jnp.exp(later - nf) * dot, 0.0))
        former = pltpu.roll(pr, d, 0) if d else pr
        seg_j = jnp.broadcast_to(bseg, (EDGE, 2 * heads))
        seg_l = pltpu.roll(seg_j, d, 0) if d else seg_j
        bo_d = pltpu.roll(bo, d, 0) if d else bo
        dot = jnp.sum(bi * bo_d, axis=1, keepdims=True)
        stack.append(
            jnp.where((j - d >= EDGE - margin) & (seg_j == seg_l), jnp.exp(former - pr) * dot, 0.0)
        )
    stack = high_low(jnp.concatenate(stack, axis=0))
    ext[0:EDGE] = bs
    ext[EDGE : EDGE + length] = sig[...].astype(F32)
    ext[EDGE + length :] = as_
    width = channels // parts
    start = part * width
    widen[...] = spread(heads, channels, hdim)
    score = mm_nt(out[...], in_[...])
    t, s = iota((length, length), 0), iota((length, length), 1)
    same = col_full == seg
    score_f = jnp.where(same & (t >= s), score, 0.0)
    score_r = jnp.where(same & (t <= s), score, 0.0)
    lower = t >= s
    wide = 128
    first = iota((length, wide), 1) < hdim
    ao_b, bo_b = ao.astype(BF16), bo.astype(BF16)
    skip2 = mm(skip[...], spread(heads, channels, hdim)[0:heads].astype(F32), EXACT)
    for c in range(0, width, wide):
        sl = slice(start + c, start + c + wide)
        to = slice(c, c + wide)
        e = mm(stack, widen[:, sl])
        skip_f, skip_r = skip2[0:1, sl], skip2[1:2, sl]
        pre = conv(ext, EDGE, length + EDGE, cw[0], cb[0:1, sl], sl, -1)
        sg = jax.nn.sigmoid(pre)
        act_f = (pre * sg)[0:length]
        slope_f = sg * (1.0 + pre * (1.0 - sg))
        pre = conv(ext, 0, length + EDGE, cw[1], cb[1:2, sl], sl, 1)
        sg = jax.nn.sigmoid(pre)
        act_r = (pre * sg)[EDGE:]
        slope_r = sg * (1.0 + pre * (1.0 - sg))
        act = jnp.concatenate([act_f.astype(BF16), act_r.astype(BF16)], axis=0)
        ct16 = cot[:, sl]
        ct = ct16.astype(F32)
        forth, back = [], []
        for k in range(wide // hdim):
            h = (start + c) // hdim + k
            up = cf[:, h : h + 1] - sums_t[h : h + 1]
            down = sums_t[heads + h : heads + h + 1] - cr[:, h : h + 1]
            x = jnp.exp(jnp.minimum(jnp.where(lower, up, down), 0.0))
            m = jnp.concatenate([(x * score_f).astype(BF16), (x * score_r).astype(BF16)], axis=1)
            forth.append(mm(m, act))
            back.append(mm_tn(m, ct16))
        mixed[:, to] = jnp.where(first, forth[0], forth[1]) + skip_f * act_f + skip_r * act_r
        here_f = jnp.where(first, back[0][0:length], back[1][0:length]) + skip_f * ct
        here_r = jnp.where(first, back[0][length:], back[1][length:]) + skip_r * ct
        at = 4 * length
        ac_c, bc_c = ac[:, sl], bc[:, sl]
        row = iota((EDGE, wide), 0)
        beyond = jnp.where(row < margin, skip_f * ac_c, 0.0)
        ahead = jnp.where(row >= EDGE - margin, skip_r * bc_c, 0.0)
        for d in range(margin):
            k = at + (5 + 2 * d) * EDGE
            moved = pltpu.roll(ac_c, (EDGE - d) % EDGE, 0) if d else ac_c
            beyond += e[k : k + EDGE] * moved
            moved = pltpu.roll(bc_c, d, 0) if d else bc_c
            ahead += e[k + EDGE : k + 2 * EDGE] * moved
        out_f[:, to] = e[0:length]
        out_r[:, to] = e[length : 2 * length]
        base_f[0:length, to] = here_f * slope_f[0:length]
        base_f[length:, to] = beyond * slope_f[length:]
        gate_f[0:length, to] = e[2 * length : 3 * length] * slope_f[0:length]
        gate_f[length:, to] = e[at : at + EDGE] * slope_f[length:]
        base_r[EDGE:, to] = here_r * slope_r[EDGE:]
        base_r[0:EDGE, to] = ahead * slope_r[0:EDGE]
        gate_r[EDGE:, to] = e[3 * length : 4 * length] * slope_r[EDGE:]
        gate_r[0:EDGE, to] = e[at + EDGE : at + 2 * EDGE] * slope_r[0:EDGE]
        low[0:nstate, to] = mm_tn(ao_b, (ac_c * e[at + 2 * EDGE : at + 3 * EDGE]).astype(BF16))
        low[nstate : 2 * nstate, to] = mm_tn(
            bo_b, (bc_c * e[at + 3 * EDGE : at + 4 * EDGE]).astype(BF16)
        )
        low[2 * nstate :, to] = e[at + 4 * EDGE : at + 5 * EDGE]


def finish_kernel(*refs, outer, parts):
    entries = refs[:outer]
    locals_ = [refs[outer + 8 * p : outer + 8 * (p + 1)] for p in range(parts)]
    in_, out, before, after, cw, mixed, grad, state, df, dr = refs[outer + 8 * parts :]
    length, channels = mixed.shape
    nstate = in_.shape[1]
    me = lax.axis_index("outer")
    width = channels // outer
    for r in range(outer):
        state[:, pl.ds(pl.multiple_of((me ^ r) * width, 128), width)] = entries[r][...]
    per = channels // parts
    query, key = out[...], in_[...]
    at = 2 * channels
    beyond, ahead = after[:, at : at + nstate], before[:, at : at + nstate]
    lags = cw.shape[1]
    wide = 256
    for c in range(0, channels, wide):
        p, off = divmod(c, per)
        loc, base_f, gate_f, base_r, gate_r, out_f, out_r, low = locals_[p]
        to = slice(off, off + wide)
        sl = slice(c, c + wide)
        s = state[:, sl]
        mixed[:, sl] = (
            loc[:, to]
            + out_f[:, to] * mm(query, s[0:nstate])
            + out_r[:, to] * mm(query, s[2 * nstate : 3 * nstate])
        ).astype(BF16)
        s_br, s_bf = s[nstate : 2 * nstate], s[3 * nstate :]
        h_f = low[0:nstate, to] + low[2 * nstate : 2 * nstate + 1, to] * s_bf.astype(F32)
        h_r = low[nstate : 2 * nstate, to] + low[2 * nstate + 4 : 2 * nstate + 5, to] * s_br.astype(F32)
        df[0:length] = base_f[0:length, to] + gate_f[0:length, to] * mm(key, h_f.astype(BF16))
        df[length:] = base_f[length:, to] + gate_f[length:, to] * mm(beyond, s_bf)
        dr[EDGE:] = base_r[EDGE:, to] + gate_r[EDGE:, to] * mm(key, h_r.astype(BF16))
        dr[0:EDGE] = base_r[0:EDGE, to] + gate_r[0:EDGE, to] * mm(ahead, s_br)
        total = jnp.zeros((length, wide), F32)
        for lag in range(lags):
            total += cw[0, lag : lag + 1, sl] * df[lag : lag + length]
            total += cw[1, lag : lag + 1, sl] * dr[EDGE - lag : EDGE - lag + length]
        grad[:, sl] = total.astype(BF16)


def params():
    return pltpu.CompilerParams(vmem_limit_bytes=VMEM)


def cost(flops, size):
    return pl.CostEstimate(flops=flops, bytes_accessed=size, transcendentals=0)


def on_device(
    signal, in_coeff, out_coeff, cotangent, conv_weight, conv_bias, skip_gain, decay_table,
    bucket, segment, *, outer, inner,
):
    length, channels = signal.shape
    heads = skip_gain.shape[1]
    nstate = in_coeff.shape[1]
    axes = ("inner", "outer")
    count = outer * inner
    bucket = bucket.reshape(1, length)
    segment = segment.reshape(1, length)
    top = lambda a: pl.BlockSpec((16, a.shape[1]), lambda i: (0, 0))
    bottom = lambda a: pl.BlockSpec((16, a.shape[1]), lambda i: (length // 16 - 1, 0))
    full = lambda a: pl.BlockSpec(a.shape, lambda i: (0,) * len(a.shape))
    sds = jax.ShapeDtypeStruct
    line = 2 * channels + 512
    up_rows, down_rows = pl.pallas_call(
        edges_kernel,
        grid=(1,),
        name="edges",
        in_specs=[s(a) for a in (signal, cotangent, in_coeff, out_coeff) for s in (top, bottom)]
        + [full(bucket), full(segment)],
        out_specs=[pl.BlockSpec((EDGE, line), lambda i: (0, 0))] * 2,
        out_shape=[sds((EDGE, line), BF16)] * 2,
        compiler_params=params(),
    )(
        signal, signal, cotangent, cotangent, in_coeff, in_coeff, out_coeff, out_coeff,
        bucket, segment,
    )
    ahead = [(i, i + 1) for i in range(count - 1)]
    before = lax.ppermute(up_rows, axes, ahead)
    after = lax.ppermute(down_rows, axes, [(j, i) for i, j in ahead])
    states, sums, sums_t = pl.pallas_call(
        begin_kernel,
        name="begin",
        out_shape=[
            sds((4 * nstate, channels), F32),
            sds((3, length, 2 * heads), F32),
            sds((2 * heads, length), F32),
        ],
        scratch_shapes=[
            pltpu.VMEM((length + 2 * EDGE, channels), F32),
            pltpu.VMEM((2 * heads, channels), BF16),
        ],
        compiler_params=params(),
        cost_estimate=cost(2 * 10**8, 2**21),
    )(
        signal, cotangent, in_coeff, out_coeff, bucket, segment, conv_weight, conv_bias,
        decay_table,
    )
    width = channels // outer
    pay = 4 * nstate + 16
    own = (states, sums)
    blocks = pl.pallas_call(
        functools.partial(send_kernel, outer=outer),
        grid=(1,),
        name="send",
        in_specs=[full(states), full(sums)]
        + [s(a) for a in (signal, in_coeff) for s in (top, bottom)]
        + [full(a) for a in (segment, conv_weight, conv_bias, decay_table, before, after)],
        out_specs=[pl.BlockSpec((pay, width), lambda i: (0, 0))] * outer,
        out_shape=[sds((pay, width), BF16)] * outer,
        scratch_shapes=[
            pltpu.VMEM((pay, channels), BF16),
            pltpu.VMEM((2 * EDGE, channels), F32),
            pltpu.VMEM((2 * EDGE, channels), F32),
        ],
        compiler_params=params(),
        cost_estimate=cost(10**6, 2**20),
    )(
        *own, signal, signal, in_coeff, in_coeff, segment, conv_weight, conv_bias, decay_table,
        before, after,
    )

    def swap(array, axis, size, r):
        return lax.ppermute(array, axis, [(i, i ^ r) for i in range(size)])

    parts = 2

    def local(part):
        per = channels // parts
        both_rows = length + EDGE
        return pl.pallas_call(
            functools.partial(local_kernel, part=part, parts=parts),
            name=f"local{part}",
            out_shape=[
                sds((length, per), F32),
                sds((both_rows, per), F32),
                sds((both_rows, per), F32),
                sds((both_rows, per), F32),
                sds((both_rows, per), F32),
                sds((length, per), F32),
                sds((length, per), F32),
                sds((2 * nstate + EDGE, per), F32),
            ],
            scratch_shapes=[
                pltpu.VMEM((length + 2 * EDGE, channels), F32),
                pltpu.VMEM((2 * heads, channels), BF16),
            ],
            compiler_params=params(),
            cost_estimate=cost(4 * 10**8, 2**22),
        )(
            signal, cotangent, in_coeff, out_coeff, segment, conv_weight, conv_bias, skip_gain,
            decay_table, sums, sums_t, before, after,
        )

    blocks = [blocks[0]] + [swap(blocks[r], "outer", outer, r) for r in range(1, outer)]
    locals_ = [local(p) for p in range(parts)]
    totals = pl.pallas_call(
        functools.partial(totals_kernel, outer=outer, inner=inner, nstate=nstate),
        name="totals",
        out_shape=[sds((2 * nstate + 16, width), BF16)] * (inner - 1),
        scratch_shapes=[pltpu.VMEM((outer, pay, width), BF16)],
        compiler_params=params(),
        cost_estimate=cost(10**6, 2**19),
    )(*blocks)
    totals = [swap(totals[r - 1], "inner", inner, r) for r in range(1, inner)]
    entries = pl.pallas_call(
        functools.partial(entries_kernel, outer=outer, inner=inner, nstate=nstate),
        name="entries",
        out_shape=[sds((4 * nstate, width), BF16)] * outer,
        scratch_shapes=[
            pltpu.VMEM((outer, pay, width), BF16),
            pltpu.VMEM((inner, 2 * nstate + 16, width), BF16),
            pltpu.VMEM((outer, 4 * nstate, width), BF16),
        ],
        compiler_params=params(),
        cost_estimate=cost(10**6, 2**19),
    )(*blocks, *totals)
    entries = [entries[0]] + [swap(entries[r], "outer", outer, r) for r in range(1, outer)]
    return pl.pallas_call(
        functools.partial(finish_kernel, outer=outer, parts=parts),
        name="finish",
        out_shape=[sds((length, channels), BF16)] * 2,
        scratch_shapes=[
            pltpu.VMEM((4 * nstate, channels), BF16),
            pltpu.VMEM((length + EDGE, 256), F32),
            pltpu.VMEM((length + EDGE, 256), F32),
        ],
        compiler_params=params(),
        cost_estimate=cost(10**8, 2**22),
    )(
        *entries, *[a for group in locals_ for a in group], in_coeff, out_coeff, before, after,
        conv_weight,
    )


def solution(mesh):
    rows = P(("groups", "inner", "outer"), None)
    flat = P(("groups", "inner", "outer"))
    return jax.shard_map(
        functools.partial(on_device, outer=mesh.shape["outer"], inner=mesh.shape["inner"]),
        mesh=mesh,
        in_specs=(rows, rows, rows, rows, P(), P(), P(), P(), flat, flat),
        out_specs=(rows, rows),
        check_vma=False,
    )
```

```python
import functools

import jax
import jax.numpy as jnp
from jax import lax
from jax.experimental import pallas as pl
from jax.experimental.pallas import tpu as pltpu
from jax.sharding import PartitionSpec as P

F32, BF16 = jnp.float32, jnp.bfloat16
EXACT = lax.Precision.HIGHEST
EDGE = 8
VMEM = 14 * 2**20


def mm(a, b, precision=None):
    return lax.dot_general(
        a, b, (((1,), (0,)), ((), ())), precision=precision, preferred_element_type=F32
    )


def mm_tn(a, b, precision=None):
    return lax.dot_general(
        a, b, (((0,), (0,)), ((), ())), precision=precision, preferred_element_type=F32
    )


def mm_nt(a, b, precision=None):
    return lax.dot_general(
        a, b, (((1,), (1,)), ((), ())), precision=precision, preferred_element_type=F32
    )


def iota(shape, dim):
    return lax.broadcasted_iota(jnp.int32, shape, dim)


def twice(heads):
    col = iota((heads, 2 * heads), 1)
    col = jnp.where(col < heads, col, col - heads)
    return (iota((heads, 2 * heads), 0) == col).astype(F32)


def spread(heads, lanes, hdim, start=0):
    row = iota((2 * heads, lanes), 0)
    row = jnp.where(row < heads, row, row - heads)
    low = row * hdim
    col = iota((2 * heads, lanes), 1) + start
    return ((col >= low) & (col < low + hdim)).astype(BF16)


def high_low(x):
    high = x.astype(BF16).astype(F32)
    return jnp.where(iota(x.shape, 1) < x.shape[1] // 2, high, x - high).astype(BF16)


def one_hot(column, size):
    return (column == iota((column.shape[0], size), 1).astype(column.dtype)).astype(F32)


def edges_kernel(sig_t, sig_b, cot_t, cot_b, in_t, out_t, bucket, segment, up, down):
    length = bucket.shape[1]
    channels = sig_t.shape[1]

    def put(target, column, value):
        target[:, column : column + value.shape[1]] = value.astype(BF16)

    bcol = jnp.transpose(jnp.broadcast_to(bucket[...].astype(F32), (length, length)))
    scol = jnp.transpose(jnp.broadcast_to(segment[...].astype(F32), (length, length)))
    j, t = iota((EDGE, length), 0), iota((EDGE, length), 1)
    for target, refs, lo, row in (
        (up, (sig_b, cot_b), EDGE, length - EDGE),
        (down, (sig_t, cot_t), 0, 0),
    ):
        pick = (t == j + row).astype(BF16)
        for k, ref in enumerate(refs):
            put(target, k * channels, ref[...].astype(F32)[lo : lo + EDGE])
        for k, ref in enumerate((in_t, out_t)):
            put(target, 2 * channels + 128 * k, mm_nt(pick, ref[...]))
        put(target, 2 * channels + 256, bcol[row : row + EDGE, :128])
        put(target, 2 * channels + 384, scol[row : row + EDGE, :128])


def edge_parts(ref, channels, state):
    x = ref[...]
    return (
        x[:, :channels].astype(F32),
        x[:, channels : 2 * channels].astype(F32),
        x[:, 2 * channels : 2 * channels + state].astype(F32),
        x[:, 2 * channels + 128 : 2 * channels + 128 + state].astype(F32),
        x[:, 2 * channels + 256 : 2 * channels + 257].astype(F32),
        x[:, 2 * channels + 384 : 2 * channels + 385].astype(F32),
    )


def conv(ext, start, rows, weight, bias, sl, step):
    total = bias
    for lag in range(weight.shape[0]):
        at = start + step * lag
        total = total + weight[lag : lag + 1, sl] * ext[at : at + rows, sl]
    return total


def begin_kernel(sig, cot, in_t, out_t, bucket, segment, cw, cb, table, sums, sums_t, *rest, outer):
    outs, (pay, ext, edge) = rest[:-3], rest[-3:]
    length, channels = sig.shape
    heads = table.shape[2]
    rows = table.shape[1]
    nstate = in_t.shape[0]
    hdim = channels // heads
    margin = cw.shape[1] - 1
    hot_t = (bucket[...] == iota((rows, length), 0)).astype(F32)
    row, col = iota((length, length), 0), iota((length, length), 1)
    counts = mm_nt((row >= col).astype(F32), hot_t)
    strict = mm_nt((row > col).astype(F32), hot_t)
    counts_t = mm(hot_t, (row <= col).astype(F32))
    strict_t = counts_t - hot_t
    dup = twice(heads)
    table_f = mm(table[0], dup, EXACT)
    table_r = mm(table[1], dup, EXACT)
    cf = mm(counts, table_f, EXACT)
    cr = mm(strict, table_r, EXACT)
    ci = mm(counts, table_r, EXACT)
    sums[0], sums[1], sums[2] = cf, cr, ci
    sums_t[0:heads] = mm_tn(table[0], counts_t, EXACT)
    sums_t[heads : 2 * heads] = mm_tn(table[1], strict_t, EXACT)
    seg = segment[...].astype(F32)
    seg_col = jnp.transpose(jnp.broadcast_to(seg, (length, length)))[:, : 2 * heads]
    t = iota((length, 2 * heads), 0)
    last, near = length - 1, length - margin

    def at(place):
        return seg[:, place : place + 1]

    def fade(arg, anchor, keep):
        return high_low(jnp.where((seg_col == at(anchor)) & keep, jnp.exp(arg), 0.0))

    fade_f = fade(cf[last:] - cf, last, t >= margin)
    fade_br = fade(cr[near : near + 1] - cr, near - 1, t < near)
    fade_r = fade(cr, 0, t < near)
    fade_bf = fade(cf - cf[margin - 1 : margin], margin, t >= margin)
    total_f, total_r = cf[last:], ci[last:]
    j = iota((EDGE, 2 * heads), 0)
    early, late = j < margin, j >= EDGE - margin
    keeps = jnp.zeros((EDGE, 2 * heads), F32)
    for k, value in enumerate(
        (
            jnp.exp(total_f),
            jnp.exp(cr[near : near + 1]),
            jnp.where(at(near - 1) == at(last), jnp.exp(total_r - cr[near : near + 1]), 0.0),
            jnp.exp(total_r),
            jnp.exp(total_f - cf[margin - 1 : margin]),
            jnp.where(at(0) == at(margin), jnp.exp(cf[margin - 1 : margin]), 0.0),
        )
    ):
        keeps = jnp.where(j == k, value, keeps)
    cf_0, cr_l = cf[0:EDGE], cr[length - EDGE :]
    seg_0, seg_l = seg_col[0:EDGE], seg_col[length - EDGE :]
    act_fade = jnp.where(
        early & (seg_0 == at(last)),
        jnp.exp(total_f - cf_0),
        jnp.where(late & (seg_l == at(0)), jnp.exp(cr_l), 0.0),
    )
    cot_fade = jnp.where(
        early & (seg_0 == at(0)),
        jnp.exp(cf_0),
        jnp.where(late & (seg_l == at(last)), jnp.exp(total_r - cr_l), 0.0),
    )
    small = high_low(jnp.concatenate([keeps, act_fade, cot_fade], axis=0))
    ext[0:EDGE] = jnp.zeros((EDGE, channels), F32)
    ext[EDGE + length :] = jnp.zeros((EDGE, channels), F32)
    ext[EDGE : EDGE + length] = sig[...].astype(F32)
    edge[...] = spread(heads, channels, hdim)
    keys, queries = in_t[...], out_t[...]
    wide = 256
    for c in range(0, channels, wide):
        sl = slice(c, c + wide)
        widen = edge[:, sl]
        pre = conv(ext, EDGE, length, cw[0], cb[0:1, sl], sl, -1)
        act = pre * jax.nn.sigmoid(pre)
        pay[0:nstate, sl] = mm(keys, (act * mm(fade_f, widen)).astype(BF16)).astype(BF16)
        pre = conv(ext, EDGE, length, cw[1], cb[1:2, sl], sl, 1)
        act = pre * jax.nn.sigmoid(pre)
        pay[2 * nstate : 3 * nstate, sl] = mm(keys, (act * mm(fade_r, widen)).astype(BF16)).astype(
            BF16
        )
        ct = cot[:, sl].astype(F32)
        pay[nstate : 2 * nstate, sl] = mm(queries, (ct * mm(fade_br, widen)).astype(BF16)).astype(
            BF16
        )
        pay[3 * nstate : 4 * nstate, sl] = mm(
            queries, (ct * mm(fade_bf, widen)).astype(BF16)
        ).astype(BF16)
    e = mm(small, edge[...])
    row = iota((EDGE, channels), 0)

    def tile(ref):
        top = ref[0:16].astype(F32)[0:EDGE]
        return jnp.where(row < 4, top, ref[length - 16 :].astype(F32)[EDGE:])

    high = e[0:EDGE].astype(BF16).astype(F32)
    head = jnp.where(row == 6, at(0), jnp.where(row == 7, at(margin), high))
    foot = jnp.where(
        row == 6, at(near - 1), jnp.where(row == 7, at(last), e[0:EDGE] - high)
    )
    k, s = iota((EDGE, length), 0), iota((EDGE, length), 1)
    lines = jnp.concatenate([keys, keys, queries, queries], axis=0)
    firsts = mm_nt(((k < margin) & (s == k)).astype(BF16), lines)
    finals = mm_nt(((k >= EDGE - margin) & (s == k + length - EDGE)).astype(BF16), lines)
    group = iota(firsts.shape, 1) // nstate
    coeff = jnp.where(group % 2 == 0, firsts, finals)
    width = channels // outer
    if width > coeff.shape[1]:
        coeff = jnp.concatenate(
            [coeff, jnp.zeros((EDGE, width - coeff.shape[1]), F32)], axis=1
        )
    coeff = jnp.concatenate([coeff] * outer, axis=1)
    base = 4 * nstate
    pay[base : base + 16] = jnp.concatenate([head, foot], axis=0).astype(BF16)
    pay[base + 16 : base + 32] = jnp.concatenate([tile(sig), e[EDGE : 2 * EDGE]], axis=0).astype(
        BF16
    )
    pay[base + 32 : base + 48] = jnp.concatenate(
        [tile(cot) * e[2 * EDGE :], coeff], axis=0
    ).astype(BF16)
    me = lax.axis_index("outer")
    for r in range(outer):
        outs[r][...] = pay[:, pl.ds(pl.multiple_of((me ^ r) * width, 128), width)]


def edge_sums(before, after, table, channels, state, heads, margin):
    dup = twice(heads)
    table_f = mm(table[0], dup, EXACT)
    table_r = mm(table[1], dup, EXACT)
    bs, bc, bi, bo, bb, bseg = edge_parts(before, channels, state)
    as_, ac, ai, ao, ab, aseg = edge_parts(after, channels, state)
    tri = (iota((EDGE, EDGE), 0) >= iota((EDGE, EDGE), 1)).astype(F32)
    rev = (iota((EDGE, EDGE), 0) <= iota((EDGE, EDGE), 1)).astype(F32)
    rows = table.shape[1]
    nf = mm(mm(tri, one_hot(ab, rows)), table_f, EXACT)
    pr = mm(mm(rev, one_hot(bb, rows)), table_r, EXACT)
    return (bs, bc, bi, bo, bseg), (as_, ac, ai, ao, aseg), nf, pr


class Block:
    def __init__(self, ref, nstate):
        x = ref.astype(F32)
        h = 4 * nstate
        self.f, self.br = x[0:nstate], x[nstate : 2 * nstate]
        self.r, self.bf = x[2 * nstate : 3 * nstate], x[3 * nstate : h]
        keep = x[h : h + 8] + x[h + 8 : h + 16]
        self.keep_f, self.near_br, self.far_br = keep[0:1], keep[1:2], keep[2:3]
        self.keep_r, self.near_bf, self.far_bf = keep[3:4], keep[4:5], keep[5:6]
        self.seg_first, self.seg_early = x[h + 6 : h + 7], x[h + 7 : h + 8]
        self.seg_late, self.seg_last = x[h + 14 : h + 15], x[h + 15 : h + 16]
        self.sig, self.fade = x[h + 16 : h + 24], x[h + 24 : h + 32]
        self.cot, self.coeff = x[h + 32 : h + 40], x[h + 40 : h + 48]


def alike(a, b):
    return jnp.where(a == b, 1.0, 0.0)


def act_rows(before, here, after, cw, cb, lanes):
    row = iota(here.shape, 0)
    pre_f = cb[0:1, lanes] + cw[0, 0:1, lanes] * here
    pre_r = cb[1:2, lanes] + cw[1, 0:1, lanes] * here
    for lag in range(1, cw.shape[1]):
        moved = pltpu.roll(jnp.where(row >= EDGE - lag, before, here), lag, 0)
        pre_f += cw[0, lag : lag + 1, lanes] * moved
        moved = pltpu.roll(jnp.where(row < lag, after, here), EDGE - lag, 0)
        pre_r += cw[1, lag : lag + 1, lanes] * moved
    pre = jnp.where(row < 4, pre_f, pre_r)
    return pre * jax.nn.sigmoid(pre)


def edge_states(act, fade, cot, coeff, nstate):
    coeff = coeff.astype(BF16)
    a = mm_tn(coeff[:, : 2 * nstate], (act * fade).astype(BF16))
    b = mm_tn(coeff[:, 2 * nstate : 4 * nstate], cot.astype(BF16))
    return a[:nstate], a[nstate:], b[:nstate], b[nstate:]


def totals_kernel(*refs, outer, inner, nstate):
    blocks, (cw, cb), outs, held = refs[:outer], refs[outer : outer + 2], refs[outer + 2 : -1], refs[-1]
    me = lax.axis_index("outer")
    place = lax.axis_index("inner")
    width = blocks[0].shape[1]
    lanes = pl.ds(pl.multiple_of(me * width, 128), width)
    for r in range(outer):
        held[me ^ r] = blocks[r][...]
    b = [Block(held[k], nstate) for k in range(outer)]
    none = jnp.zeros((EDGE, width), F32)
    low = []
    for k in range(outer):
        before = b[k - 1].sig if k else none
        after = b[k + 1].sig if k < outer - 1 else none
        act = act_rows(before, b[k].sig, after, cw, cb, lanes)
        low.append(edge_states(act, b[k].fade, b[k].cot, b[k].coeff, nstate))
    end = outer - 1
    f, x = b[0].f, b[0].br
    keep_f, keep_br = jnp.ones((1, width), F32), b[0].near_br
    for k in range(1, outer):
        y = low[k - 1][3] + b[k - 1].far_br * x
        factor = b[k].near_br * alike(b[k - 1].seg_last, b[k].seg_late)
        x = b[k].br + factor * y
        keep_br = keep_br * b[k - 1].far_br * factor
        factor = b[k].keep_f * alike(b[k - 1].seg_last, b[k].seg_last)
        f = b[k].f + low[k][0] + factor * f
        keep_f = keep_f * factor
    r, z = b[end].r, b[end].bf
    keep_r, keep_bf = jnp.ones((1, width), F32), b[end].near_bf
    for k in range(end - 1, -1, -1):
        y = low[k + 1][2] + b[k + 1].far_bf * z
        factor = b[k].near_bf * alike(b[k + 1].seg_first, b[k].seg_early)
        z = b[k].bf + factor * y
        keep_bf = keep_bf * b[k + 1].far_bf * factor
        factor = b[k].keep_r * alike(b[k + 1].seg_first, b[k].seg_first)
        r = b[k].r + low[k][1] + factor * r
        keep_r = keep_r * factor
    row = iota((EDGE, width), 0)
    half = row < 4

    def header(rows):
        tile = jnp.zeros((EDGE, width), F32)
        for k, value in enumerate(rows):
            tile = jnp.where(row == k, value, tile)
        high = tile.astype(BF16).astype(F32)
        return jnp.concatenate([high, tile - high], axis=0)

    up = (
        keep_f, b[0].keep_f, keep_br, b[end].far_br,
        b[0].seg_last, b[0].seg_late, b[end].seg_last,
    )
    down = (
        keep_r, b[end].keep_r, keep_bf, b[0].far_bf,
        b[end].seg_first, b[end].seg_early, b[0].seg_first,
    )
    sig = jnp.where(half, b[0].sig, b[end].sig)
    coeff = jnp.where(half, b[0].coeff, b[end].coeff)
    up_rows = jnp.where(half, b[0].fade, b[end].cot)
    down_rows = jnp.where(half, b[0].cot, b[end].fade)
    pad = jnp.zeros((EDGE, width), F32)
    up = jnp.concatenate([f, x, header(up), sig, coeff, up_rows, pad], axis=0)
    down = jnp.concatenate([r, z, header(down), sig, coeff, down_rows, pad], axis=0)
    for r in range(1, inner):
        towards = jnp.full(up.shape, place ^ r, jnp.int32) > place
        outs[r - 1][...] = jnp.where(towards, up, down).astype(BF16)


def entries_kernel(*refs, outer, inner, nstate):
    blocks = refs[:outer]
    others = refs[outer : outer + inner - 1]
    cw, cb = refs[outer + inner - 1 : outer + inner + 1]
    outs = refs[outer + inner + 1 : -3]
    held, far, entry = refs[-3:]
    me = lax.axis_index("outer")
    place = lax.axis_index("inner")
    width = blocks[0].shape[1]
    lanes = pl.ds(pl.multiple_of(me * width, 128), width)
    for r in range(outer):
        held[me ^ r] = blocks[r][...]
    far[place] = jnp.zeros(far.shape[1:], BF16)
    for r in range(1, inner):
        far[place ^ r] = others[r - 1][...]
    n, h = nstate, 2 * nstate
    zero = jnp.zeros((n, width), F32)
    none = jnp.zeros((EDGE, width), F32)
    line = jnp.zeros((1, width), F32)

    def step(carry, index, wanted, upward):
        state, x, y, edge, seg = carry
        p = far[index].astype(F32)
        keep = p[h : h + 8] + p[h + 8 : h + 16]
        sig, coeff, rows = (p[h + k : h + k + EDGE] for k in (16, 24, 32))
        if upward:
            act = act_rows(edge, sig, none, cw, cb, lanes)
            first, _, _, second = edge_states(act, rows, rows, coeff, n)
        else:
            act = act_rows(none, sig, edge, cw, cb, lanes)
            _, first, second, _ = edge_states(act, rows, rows, coeff, n)
        new = p[0:n] + keep[0:1] * (first + keep[1:2] * alike(seg, keep[4:5]) * state)
        new_x = p[n:h] + keep[2:3] * alike(seg, keep[5:6]) * y
        new_y = second + keep[3:4] * new_x
        return tuple(
            jnp.where(jnp.full(b.shape, wanted), b, a)
            for a, b in zip(carry, (new, new_x, new_y, sig, keep[6:7]))
        )

    up = down = (zero, zero, zero, none, line)
    for k in range(inner - 1):
        up = step(up, k, k < place, True)
        back = inner - 1 - k
        down = step(down, back, back > place, False)
    f, x, y, edge_up, seg_up = up
    r, z, w, edge_down, seg_down = down
    b = [Block(held[k], nstate) for k in range(outer)]
    low = []
    for k in range(outer):
        before = b[k - 1].sig if k else edge_up
        after = b[k + 1].sig if k < outer - 1 else edge_down
        act = act_rows(before, b[k].sig, after, cw, cb, lanes)
        low.append(edge_states(act, b[k].fade, b[k].cot, b[k].coeff, nstate))
    for k in range(outer):
        entry[k, 0:h] = jnp.concatenate([f, x], axis=0).astype(BF16)
        if k == outer - 1:
            break
        before = b[k - 1].seg_last if k else seg_up
        f = b[k].f + low[k][0] + b[k].keep_f * alike(before, b[k].seg_last) * f
        x = b[k].br + b[k].near_br * alike(before, b[k].seg_late) * y
        y = low[k][3] + b[k].far_br * x
    for k in range(outer - 1, -1, -1):
        entry[k, h : 2 * h] = jnp.concatenate([r, z], axis=0).astype(BF16)
        if k == 0:
            break
        after = b[k + 1].seg_first if k < outer - 1 else seg_down
        r = b[k].r + low[k][1] + b[k].keep_r * alike(after, b[k].seg_first) * r
        z = b[k].bf + b[k].near_bf * alike(after, b[k].seg_early) * w
        w = low[k][2] + b[k].far_bf * z
    for r_ in range(outer):
        outs[r_][...] = entry[me ^ r_]


def local_kernel(
    sig, cot, in_, out, segment, cw, cb, skip, table, sums, sums_t, before, after,
    mixed, base_f, gate_f, base_r, gate_r, out_f, out_r, low, ext, widen,
    *, part, parts,
):
    length, channels = sig.shape
    heads = table.shape[2]
    nstate = in_.shape[0]
    hdim = channels // heads
    margin = cw.shape[1] - 1
    prev, nxt, nf, pr = edge_sums(before, after, table, channels, nstate, heads, margin)
    bs, bc, bi, bo, bseg = prev
    as_, ac, ai, ao, aseg = nxt
    seg = segment[...].astype(F32)
    col_full = jnp.transpose(jnp.broadcast_to(seg, (length, length)))
    col = col_full[:, : 2 * heads]
    cf, cr = sums[0], sums[1]
    total_f = cf[length - 1 : length]
    total_r = sums[2, length - EDGE :][EDGE - 1 : EDGE]
    j = iota((EDGE, 2 * heads), 0)
    early = j < margin
    late = j >= EDGE - margin
    s_first, s_last = aseg[0:1], bseg[EDGE - 1 : EDGE]
    s_beyond, s_ahead = aseg[margin : margin + 1], bseg[EDGE - margin - 1 : EDGE - margin]
    stack = [
        jnp.where(col == s_last, jnp.exp(cf), 0.0),
        jnp.where(col == s_first, jnp.exp(total_r - cr), 0.0),
        jnp.where(col == s_first, jnp.exp(total_f - cf), 0.0),
        jnp.where(col == s_last, jnp.exp(cr), 0.0),
        jnp.where(early & (aseg == s_beyond), jnp.exp(nf[margin - 1 : margin] - nf), 0.0),
        jnp.where(
            late & (bseg == s_ahead), jnp.exp(pr[EDGE - margin : EDGE - margin + 1] - pr), 0.0
        ),
        jnp.where(early & (aseg == s_first), jnp.exp(nf), 0.0),
        jnp.where(late & (bseg == s_last), jnp.exp(pr), 0.0),
        jnp.where(
            j < 4,
            jnp.where(s_first == s_beyond, jnp.exp(nf[margin - 1 : margin]), 0.0),
            jnp.where(s_last == s_ahead, jnp.exp(pr[EDGE - margin : EDGE - margin + 1]), 0.0),
        ),
    ]
    turned = []
    for d in range(margin):
        move = (EDGE - d) % EDGE
        later = pltpu.roll(nf, move, 0) if d else nf
        seg_j = jnp.broadcast_to(aseg, (EDGE, 2 * heads))
        seg_l = pltpu.roll(seg_j, move, 0) if d else seg_j
        ao_d = pltpu.roll(ao, move, 0) if d else ao
        dot = jnp.sum(ai * ao_d, axis=1, keepdims=True)
        stack.append(jnp.where((j + d < margin) & (seg_j == seg_l), jnp.exp(later - nf) * dot, 0.0))
        former = pltpu.roll(pr, d, 0) if d else pr
        seg_j = jnp.broadcast_to(bseg, (EDGE, 2 * heads))
        seg_l = pltpu.roll(seg_j, d, 0) if d else seg_j
        bo_d = pltpu.roll(bo, d, 0) if d else bo
        dot = jnp.sum(bi * bo_d, axis=1, keepdims=True)
        stack.append(
            jnp.where((j - d >= EDGE - margin) & (seg_j == seg_l), jnp.exp(former - pr) * dot, 0.0)
        )
    stack = high_low(jnp.concatenate(stack, axis=0))
    ext[0:EDGE] = bs
    ext[EDGE : EDGE + length] = sig[...].astype(F32)
    ext[EDGE + length :] = as_
    width = channels // parts
    start = part * width
    widen[...] = spread(heads, channels, hdim)
    score = mm_tn(out[...], in_[...])
    t, s = iota((length, length), 0), iota((length, length), 1)
    same = col_full == seg
    score_f = jnp.where(same & (t >= s), score, 0.0)
    score_r = jnp.where(same & (t <= s), score, 0.0)
    lower = t >= s
    wide = 128
    first = iota((length, wide), 1) < hdim
    ao_b, bo_b = ao.astype(BF16), bo.astype(BF16)
    skip2 = mm(skip[...], spread(heads, channels, hdim)[0:heads].astype(F32), EXACT)
    for c in range(0, width, wide):
        sl = slice(start + c, start + c + wide)
        to = slice(c, c + wide)
        e = mm(stack, widen[:, sl])
        skip_f, skip_r = skip2[0:1, sl], skip2[1:2, sl]
        pre = conv(ext, EDGE, length + EDGE, cw[0], cb[0:1, sl], sl, -1)
        sg = jax.nn.sigmoid(pre)
        act_f = (pre * sg)[0:length]
        slope_f = sg * (1.0 + pre * (1.0 - sg))
        pre = conv(ext, 0, length + EDGE, cw[1], cb[1:2, sl], sl, 1)
        sg = jax.nn.sigmoid(pre)
        act_r = (pre * sg)[EDGE:]
        slope_r = sg * (1.0 + pre * (1.0 - sg))
        act = jnp.concatenate([act_f.astype(BF16), act_r.astype(BF16)], axis=0)
        ct16 = cot[:, sl]
        ct = ct16.astype(F32)
        forth, back = [], []
        for k in range(wide // hdim):
            h = (start + c) // hdim + k
            up = cf[:, h : h + 1] - sums_t[h : h + 1]
            down = sums_t[heads + h : heads + h + 1] - cr[:, h : h + 1]
            x = jnp.exp(jnp.minimum(jnp.where(lower, up, down), 0.0))
            m = jnp.concatenate([(x * score_f).astype(BF16), (x * score_r).astype(BF16)], axis=1)
            forth.append(mm(m, act))
            back.append(mm_tn(m, ct16))
        mixed[:, to] = jnp.where(first, forth[0], forth[1]) + skip_f * act_f + skip_r * act_r
        here_f = jnp.where(first, back[0][0:length], back[1][0:length]) + skip_f * ct
        here_r = jnp.where(first, back[0][length:], back[1][length:]) + skip_r * ct
        at = 4 * length
        ac_c, bc_c = ac[:, sl], bc[:, sl]
        row = iota((EDGE, wide), 0)
        beyond = jnp.where(row < margin, skip_f * ac_c, 0.0)
        ahead = jnp.where(row >= EDGE - margin, skip_r * bc_c, 0.0)
        for d in range(margin):
            k = at + (5 + 2 * d) * EDGE
            moved = pltpu.roll(ac_c, (EDGE - d) % EDGE, 0) if d else ac_c
            beyond += e[k : k + EDGE] * moved
            moved = pltpu.roll(bc_c, d, 0) if d else bc_c
            ahead += e[k + EDGE : k + 2 * EDGE] * moved
        out_f[:, to] = e[0:length]
        out_r[:, to] = e[length : 2 * length]
        base_f[0:length, to] = here_f * slope_f[0:length]
        base_f[length:, to] = beyond * slope_f[length:]
        gate_f[0:length, to] = e[2 * length : 3 * length] * slope_f[0:length]
        gate_f[length:, to] = e[at : at + EDGE] * slope_f[length:]
        base_r[EDGE:, to] = here_r * slope_r[EDGE:]
        base_r[0:EDGE, to] = ahead * slope_r[0:EDGE]
        gate_r[EDGE:, to] = e[3 * length : 4 * length] * slope_r[EDGE:]
        gate_r[0:EDGE, to] = e[at + EDGE : at + 2 * EDGE] * slope_r[0:EDGE]
        low[0:nstate, to] = mm_tn(ao_b, (ac_c * e[at + 2 * EDGE : at + 3 * EDGE]).astype(BF16))
        low[nstate : 2 * nstate, to] = mm_tn(
            bo_b, (bc_c * e[at + 3 * EDGE : at + 4 * EDGE]).astype(BF16)
        )
        low[2 * nstate :, to] = e[at + 4 * EDGE : at + 5 * EDGE]


def finish_kernel(*refs, outer, parts):
    entries = refs[:outer]
    locals_ = [refs[outer + 8 * p : outer + 8 * (p + 1)] for p in range(parts)]
    in_, out, before, after, cw, mixed, grad, state, df, dr = refs[outer + 8 * parts :]
    length, channels = mixed.shape
    nstate = in_.shape[0]
    me = lax.axis_index("outer")
    width = channels // outer
    for r in range(outer):
        state[:, pl.ds(pl.multiple_of((me ^ r) * width, 128), width)] = entries[r][...]
    per = channels // parts
    query, key = out[...], in_[...]
    at = 2 * channels
    beyond, ahead = after[:, at : at + nstate], before[:, at : at + nstate]
    lags = cw.shape[1]
    wide = 256
    for c in range(0, channels, wide):
        p, off = divmod(c, per)
        loc, base_f, gate_f, base_r, gate_r, out_f, out_r, low = locals_[p]
        to = slice(off, off + wide)
        sl = slice(c, c + wide)
        s = state[:, sl]
        mixed[:, sl] = (
            loc[:, to]
            + out_f[:, to] * mm_tn(query, s[0:nstate])
            + out_r[:, to] * mm_tn(query, s[2 * nstate : 3 * nstate])
        ).astype(BF16)
        s_br, s_bf = s[nstate : 2 * nstate], s[3 * nstate :]
        h_f = low[0:nstate, to] + low[2 * nstate : 2 * nstate + 1, to] * s_bf.astype(F32)
        h_r = low[nstate : 2 * nstate, to] + low[2 * nstate + 4 : 2 * nstate + 5, to] * s_br.astype(F32)
        df[0:length] = base_f[0:length, to] + gate_f[0:length, to] * mm_tn(key, h_f.astype(BF16))
        df[length:] = base_f[length:, to] + gate_f[length:, to] * mm(beyond, s_bf)
        dr[EDGE:] = base_r[EDGE:, to] + gate_r[EDGE:, to] * mm_tn(key, h_r.astype(BF16))
        dr[0:EDGE] = base_r[0:EDGE, to] + gate_r[0:EDGE, to] * mm(ahead, s_br)
        total = jnp.zeros((length, wide), F32)
        for lag in range(lags):
            total += cw[0, lag : lag + 1, sl] * df[lag : lag + length]
            total += cw[1, lag : lag + 1, sl] * dr[EDGE - lag : EDGE - lag + length]
        grad[:, sl] = total.astype(BF16)


def params():
    return pltpu.CompilerParams(vmem_limit_bytes=VMEM)


def cost(flops, size):
    return pl.CostEstimate(flops=flops, bytes_accessed=size, transcendentals=0)


def on_device(
    signal, in_coeff, out_coeff, cotangent, conv_weight, conv_bias, skip_gain, decay_table,
    bucket, segment, *, outer, inner,
):
    length, channels = signal.shape
    heads = skip_gain.shape[1]
    nstate = in_coeff.shape[1]
    axes = ("inner", "outer")
    count = outer * inner
    bucket = bucket.reshape(1, length)
    segment = segment.reshape(1, length)
    in_t, out_t = in_coeff.T, out_coeff.T
    top = lambda a: pl.BlockSpec((16, a.shape[1]), lambda i: (0, 0))
    bottom = lambda a: pl.BlockSpec((16, a.shape[1]), lambda i: (length // 16 - 1, 0))
    full = lambda a: pl.BlockSpec(a.shape, lambda i: (0,) * len(a.shape))
    sds = jax.ShapeDtypeStruct
    width = channels // outer
    pay = 4 * nstate + 48
    far = 2 * nstate + 48
    sums, sums_t, *blocks = pl.pallas_call(
        functools.partial(begin_kernel, outer=outer),
        name="begin",
        out_shape=[sds((3, length, 2 * heads), F32), sds((2 * heads, length), F32)]
        + [sds((pay, width), BF16)] * outer,
        scratch_shapes=[
            pltpu.VMEM((pay, channels), BF16),
            pltpu.VMEM((length + 2 * EDGE, channels), F32),
            pltpu.VMEM((2 * heads, channels), BF16),
        ],
        compiler_params=params(),
        cost_estimate=cost(2 * 10**8, 2**21),
    )(signal, cotangent, in_t, out_t, bucket, segment, conv_weight, conv_bias, decay_table)

    def swap(array, axis, size, r):
        return lax.ppermute(array, axis, [(i, i ^ r) for i in range(size)])

    blocks = [blocks[0]] + [swap(blocks[r], "outer", outer, r) for r in range(1, outer)]
    line = 2 * channels + 512
    late_bucket, _ = lax.optimization_barrier((bucket, sums))
    up_rows, down_rows = pl.pallas_call(
        edges_kernel,
        grid=(1,),
        name="edges",
        in_specs=[s(a) for a in (signal, cotangent) for s in (top, bottom)]
        + [full(a) for a in (in_t, out_t, bucket, segment)],
        out_specs=[pl.BlockSpec((EDGE, line), lambda i: (0, 0))] * 2,
        out_shape=[sds((EDGE, line), BF16)] * 2,
        compiler_params=params(),
    )(signal, signal, cotangent, cotangent, in_t, out_t, late_bucket, segment)
    ahead = [(i, i + 1) for i in range(count - 1)]
    before = lax.ppermute(up_rows, axes, ahead)
    after = lax.ppermute(down_rows, axes, [(j, i) for i, j in ahead])
    parts = 2

    def local(part):
        per = channels // parts
        both_rows = length + EDGE
        return pl.pallas_call(
            functools.partial(local_kernel, part=part, parts=parts),
            name=f"local{part}",
            out_shape=[
                sds((length, per), F32),
                sds((both_rows, per), F32),
                sds((both_rows, per), F32),
                sds((both_rows, per), F32),
                sds((both_rows, per), F32),
                sds((length, per), F32),
                sds((length, per), F32),
                sds((2 * nstate + EDGE, per), F32),
            ],
            scratch_shapes=[
                pltpu.VMEM((length + 2 * EDGE, channels), F32),
                pltpu.VMEM((2 * heads, channels), BF16),
            ],
            compiler_params=params(),
            cost_estimate=cost(4 * 10**8, 2**22),
        )(
            signal, cotangent, in_t, out_t, segment, conv_weight, conv_bias, skip_gain,
            decay_table, sums, sums_t, before, after,
        )

    locals_ = [local(p) for p in range(parts)]
    totals = pl.pallas_call(
        functools.partial(totals_kernel, outer=outer, inner=inner, nstate=nstate),
        name="totals",
        out_shape=[sds((far, width), BF16)] * (inner - 1),
        scratch_shapes=[pltpu.VMEM((outer, pay, width), BF16)],
        compiler_params=params(),
        cost_estimate=cost(10**6, 2**19),
    )(*blocks, conv_weight, conv_bias)
    totals = [swap(totals[r - 1], "inner", inner, r) for r in range(1, inner)]
    entries = pl.pallas_call(
        functools.partial(entries_kernel, outer=outer, inner=inner, nstate=nstate),
        name="entries",
        out_shape=[sds((4 * nstate, width), BF16)] * outer,
        scratch_shapes=[
            pltpu.VMEM((outer, pay, width), BF16),
            pltpu.VMEM((inner, far, width), BF16),
            pltpu.VMEM((outer, 4 * nstate, width), BF16),
        ],
        compiler_params=params(),
        cost_estimate=cost(10**6, 2**19),
    )(*blocks, *totals, conv_weight, conv_bias)
    entries = [entries[0]] + [swap(entries[r], "outer", outer, r) for r in range(1, outer)]
    return pl.pallas_call(
        functools.partial(finish_kernel, outer=outer, parts=parts),
        name="finish",
        out_shape=[sds((length, channels), BF16)] * 2,
        scratch_shapes=[
            pltpu.VMEM((4 * nstate, channels), BF16),
            pltpu.VMEM((length + EDGE, 256), F32),
            pltpu.VMEM((length + EDGE, 256), F32),
        ],
        compiler_params=params(),
        cost_estimate=cost(10**8, 2**22),
    )(*entries, *[a for group in locals_ for a in group], in_t, out_t, before, after, conv_weight)


def solution(mesh):
    rows = P(("groups", "inner", "outer"), None)
    flat = P(("groups", "inner", "outer"))
    return jax.shard_map(
        functools.partial(on_device, outer=mesh.shape["outer"], inner=mesh.shape["inner"]),
        mesh=mesh,
        in_specs=(rows, rows, rows, rows, P(), P(), P(), P(), flat, flat),
        out_specs=(rows, rows),
        check_vma=False,
    )
```

```python
import functools

import jax
import jax.numpy as jnp
from jax import lax
from jax.experimental import pallas as pl
from jax.experimental.pallas import tpu as pltpu
from jax.sharding import PartitionSpec as P

F32, BF16 = jnp.float32, jnp.bfloat16
EXACT = lax.Precision.HIGHEST
EDGE = 8
VMEM = 14 * 2**20
BEGIN_VMEM = 58 * 2**20


def mm(a, b, precision=None):
    return lax.dot_general(
        a, b, (((1,), (0,)), ((), ())), precision=precision, preferred_element_type=F32
    )


def mm_tn(a, b, precision=None):
    return lax.dot_general(
        a, b, (((0,), (0,)), ((), ())), precision=precision, preferred_element_type=F32
    )


def mm_nt(a, b, precision=None):
    return lax.dot_general(
        a, b, (((1,), (1,)), ((), ())), precision=precision, preferred_element_type=F32
    )


def iota(shape, dim):
    return lax.broadcasted_iota(jnp.int32, shape, dim)


def twice(heads):
    col = iota((heads, 2 * heads), 1)
    col = jnp.where(col < heads, col, col - heads)
    return (iota((heads, 2 * heads), 0) == col).astype(F32)


def spread(heads, lanes, hdim, start=0):
    row = iota((2 * heads, lanes), 0)
    row = jnp.where(row < heads, row, row - heads)
    low = row * hdim
    col = iota((2 * heads, lanes), 1) + start
    return ((col >= low) & (col < low + hdim)).astype(BF16)


def high_low(x):
    high = x.astype(BF16).astype(F32)
    return jnp.where(iota(x.shape, 1) < x.shape[1] // 2, high, x - high).astype(BF16)


def one_hot(column, size):
    return (column == iota((column.shape[0], size), 1).astype(column.dtype)).astype(F32)


def edges_kernel(sig, cot, in_t, out_t, bucket, segment, up, down):
    length = bucket.shape[1]
    channels = sig.shape[1]

    def put(target, column, value):
        target[:, column : column + value.shape[1]] = value.astype(BF16)

    bcol = jnp.transpose(jnp.broadcast_to(bucket[...].astype(F32), (length, length)))
    scol = jnp.transpose(jnp.broadcast_to(segment[...].astype(F32), (length, length)))
    j, t = iota((EDGE, length), 0), iota((EDGE, length), 1)
    for target, start, lo, row in ((up, length - 16, EDGE, length - EDGE), (down, 0, 0, 0)):
        pick = (t == j + row).astype(BF16)
        for k, ref in enumerate((sig, cot)):
            put(target, k * channels, ref[start : start + 16].astype(F32)[lo : lo + EDGE])
        for k, ref in enumerate((in_t, out_t)):
            put(target, 2 * channels + 128 * k, mm_nt(pick, ref[...]))
        put(target, 2 * channels + 256, bcol[row : row + EDGE, :128])
        put(target, 2 * channels + 384, scol[row : row + EDGE, :128])


def edge_parts(ref, channels, state):
    x = ref[...]
    return (
        x[:, :channels].astype(F32),
        x[:, channels : 2 * channels].astype(F32),
        x[:, 2 * channels : 2 * channels + state].astype(F32),
        x[:, 2 * channels + 128 : 2 * channels + 128 + state].astype(F32),
        x[:, 2 * channels + 256 : 2 * channels + 257].astype(F32),
        x[:, 2 * channels + 384 : 2 * channels + 385].astype(F32),
    )


def conv(ext, start, rows, weight, bias, sl, step):
    total = bias
    for lag in range(weight.shape[0]):
        at = start + step * lag
        total = total + weight[lag : lag + 1, sl] * ext[at : at + rows, sl]
    return total


def begin_kernel(*refs, outer, count):
    far, near = refs[:count], refs[-count:]
    sums, sums_t, *outs = refs[count : -count - 4]
    pay, ext, edge, sems = refs[-count - 4 : -count]
    copies = [pltpu.make_async_copy(a, b, sems.at[k]) for k, (a, b) in enumerate(zip(far, near))]
    for copy in copies:
        copy.start()
    bucket, segment, table, sig, cw, cb, in_t, cot, out_t = near
    for copy in copies[:3]:
        copy.wait()
    length, channels = sig.shape
    heads = table.shape[2]
    rows = table.shape[1]
    nstate = in_t.shape[0]
    hdim = channels // heads
    margin = cw.shape[1] - 1
    hot_t = (bucket[...] == iota((rows, length), 0)).astype(F32)
    row, col = iota((length, length), 0), iota((length, length), 1)
    counts = mm_nt((row >= col).astype(F32), hot_t)
    strict = mm_nt((row > col).astype(F32), hot_t)
    counts_t = mm(hot_t, (row <= col).astype(F32))
    strict_t = counts_t - hot_t
    dup = twice(heads)
    table_f = mm(table[0], dup, EXACT)
    table_r = mm(table[1], dup, EXACT)
    cf = mm(counts, table_f, EXACT)
    cr = mm(strict, table_r, EXACT)
    ci = mm(counts, table_r, EXACT)
    sums[0], sums[1], sums[2] = cf, cr, ci
    sums_t[0:heads] = mm_tn(table[0], counts_t, EXACT)
    sums_t[heads : 2 * heads] = mm_tn(table[1], strict_t, EXACT)
    seg = segment[...].astype(F32)
    seg_col = jnp.transpose(jnp.broadcast_to(seg, (length, length)))[:, : 2 * heads]
    t = iota((length, 2 * heads), 0)
    last, tail = length - 1, length - margin

    def at(place):
        return seg[:, place : place + 1]

    def fade(arg, anchor, keep):
        return high_low(jnp.where((seg_col == at(anchor)) & keep, jnp.exp(arg), 0.0))

    fade_f = fade(cf[last:] - cf, last, t >= margin)
    fade_br = fade(cr[tail : tail + 1] - cr, tail - 1, t < tail)
    fade_r = fade(cr, 0, t < tail)
    fade_bf = fade(cf - cf[margin - 1 : margin], margin, t >= margin)
    total_f, total_r = cf[last:], ci[last:]
    j = iota((EDGE, 2 * heads), 0)
    early, late = j < margin, j >= EDGE - margin
    keeps = jnp.zeros((EDGE, 2 * heads), F32)
    for k, value in enumerate(
        (
            jnp.exp(total_f),
            jnp.exp(cr[tail : tail + 1]),
            jnp.where(at(tail - 1) == at(last), jnp.exp(total_r - cr[tail : tail + 1]), 0.0),
            jnp.exp(total_r),
            jnp.exp(total_f - cf[margin - 1 : margin]),
            jnp.where(at(0) == at(margin), jnp.exp(cf[margin - 1 : margin]), 0.0),
        )
    ):
        keeps = jnp.where(j == k, value, keeps)
    cf_0, cr_l = cf[0:EDGE], cr[length - EDGE :]
    seg_0, seg_l = seg_col[0:EDGE], seg_col[length - EDGE :]
    act_fade = jnp.where(
        early & (seg_0 == at(last)),
        jnp.exp(total_f - cf_0),
        jnp.where(late & (seg_l == at(0)), jnp.exp(cr_l), 0.0),
    )
    cot_fade = jnp.where(
        early & (seg_0 == at(0)),
        jnp.exp(cf_0),
        jnp.where(late & (seg_l == at(last)), jnp.exp(total_r - cr_l), 0.0),
    )
    small = high_low(jnp.concatenate([keeps, act_fade, cot_fade], axis=0))
    ext[0:EDGE] = jnp.zeros((EDGE, channels), F32)
    ext[EDGE + length :] = jnp.zeros((EDGE, channels), F32)
    edge[...] = spread(heads, channels, hdim)
    for copy in copies[3:]:
        copy.wait()
    ext[EDGE : EDGE + length] = sig[...].astype(F32)
    keys, queries = in_t[...], out_t[...]
    wide = 256
    for c in range(0, channels, wide):
        sl = slice(c, c + wide)
        widen = edge[:, sl]
        pre = conv(ext, EDGE, length, cw[0], cb[0:1, sl], sl, -1)
        act = pre * jax.nn.sigmoid(pre)
        pay[0:nstate, sl] = mm(keys, (act * mm(fade_f, widen)).astype(BF16)).astype(BF16)
        pre = conv(ext, EDGE, length, cw[1], cb[1:2, sl], sl, 1)
        act = pre * jax.nn.sigmoid(pre)
        pay[2 * nstate : 3 * nstate, sl] = mm(keys, (act * mm(fade_r, widen)).astype(BF16)).astype(
            BF16
        )
        ct = cot[:, sl].astype(F32)
        pay[nstate : 2 * nstate, sl] = mm(queries, (ct * mm(fade_br, widen)).astype(BF16)).astype(
            BF16
        )
        pay[3 * nstate : 4 * nstate, sl] = mm(
            queries, (ct * mm(fade_bf, widen)).astype(BF16)
        ).astype(BF16)
    e = mm(small, edge[...])
    row = iota((EDGE, channels), 0)

    def tile(ref):
        top = ref[0:16].astype(F32)[0:EDGE]
        return jnp.where(row < 4, top, ref[length - 16 :].astype(F32)[EDGE:])

    high = e[0:EDGE].astype(BF16).astype(F32)
    head = jnp.where(row == 6, at(0), jnp.where(row == 7, at(margin), high))
    foot = jnp.where(
        row == 6, at(tail - 1), jnp.where(row == 7, at(last), e[0:EDGE] - high)
    )
    k, s = iota((EDGE, length), 0), iota((EDGE, length), 1)
    lines = jnp.concatenate([keys, keys, queries, queries], axis=0)
    firsts = mm_nt(((k < margin) & (s == k)).astype(BF16), lines)
    finals = mm_nt(((k >= EDGE - margin) & (s == k + length - EDGE)).astype(BF16), lines)
    group = iota(firsts.shape, 1) // nstate
    coeff = jnp.where(group % 2 == 0, firsts, finals)
    width = channels // outer
    if width > coeff.shape[1]:
        coeff = jnp.concatenate(
            [coeff, jnp.zeros((EDGE, width - coeff.shape[1]), F32)], axis=1
        )
    coeff = jnp.concatenate([coeff] * outer, axis=1)
    base = 4 * nstate
    pay[base : base + 16] = jnp.concatenate([head, foot], axis=0).astype(BF16)
    pay[base + 16 : base + 32] = jnp.concatenate([tile(sig), e[EDGE : 2 * EDGE]], axis=0).astype(
        BF16
    )
    pay[base + 32 : base + 48] = jnp.concatenate(
        [tile(cot) * e[2 * EDGE :], coeff], axis=0
    ).astype(BF16)
    me = lax.axis_index("outer")
    for r in range(outer):
        outs[r][...] = pay[:, pl.ds(pl.multiple_of((me ^ r) * width, 128), width)]


def edge_sums(before, after, table, channels, state, heads, margin):
    dup = twice(heads)
    table_f = mm(table[0], dup, EXACT)
    table_r = mm(table[1], dup, EXACT)
    bs, bc, bi, bo, bb, bseg = edge_parts(before, channels, state)
    as_, ac, ai, ao, ab, aseg = edge_parts(after, channels, state)
    tri = (iota((EDGE, EDGE), 0) >= iota((EDGE, EDGE), 1)).astype(F32)
    rev = (iota((EDGE, EDGE), 0) <= iota((EDGE, EDGE), 1)).astype(F32)
    rows = table.shape[1]
    nf = mm(mm(tri, one_hot(ab, rows)), table_f, EXACT)
    pr = mm(mm(rev, one_hot(bb, rows)), table_r, EXACT)
    return (bs, bc, bi, bo, bseg), (as_, ac, ai, ao, aseg), nf, pr


class Block:
    def __init__(self, ref, nstate):
        x = ref.astype(F32)
        h = 4 * nstate
        self.f, self.br = x[0:nstate], x[nstate : 2 * nstate]
        self.r, self.bf = x[2 * nstate : 3 * nstate], x[3 * nstate : h]
        keep = x[h : h + 8] + x[h + 8 : h + 16]
        self.keep_f, self.near_br, self.far_br = keep[0:1], keep[1:2], keep[2:3]
        self.keep_r, self.near_bf, self.far_bf = keep[3:4], keep[4:5], keep[5:6]
        self.seg_first, self.seg_early = x[h + 6 : h + 7], x[h + 7 : h + 8]
        self.seg_late, self.seg_last = x[h + 14 : h + 15], x[h + 15 : h + 16]
        self.sig, self.fade = x[h + 16 : h + 24], x[h + 24 : h + 32]
        self.cot, self.coeff = x[h + 32 : h + 40], x[h + 40 : h + 48]


def alike(a, b):
    return jnp.where(a == b, 1.0, 0.0)


def act_rows(before, here, after, cw, cb, lanes):
    row = iota(here.shape, 0)
    pre_f = cb[0:1, lanes] + cw[0, 0:1, lanes] * here
    pre_r = cb[1:2, lanes] + cw[1, 0:1, lanes] * here
    for lag in range(1, cw.shape[1]):
        moved = pltpu.roll(jnp.where(row >= EDGE - lag, before, here), lag, 0)
        pre_f += cw[0, lag : lag + 1, lanes] * moved
        moved = pltpu.roll(jnp.where(row < lag, after, here), EDGE - lag, 0)
        pre_r += cw[1, lag : lag + 1, lanes] * moved
    pre = jnp.where(row < 4, pre_f, pre_r)
    return pre * jax.nn.sigmoid(pre)


def edge_states(act, fade, cot, coeff, nstate):
    coeff = coeff.astype(BF16)
    a = mm_tn(coeff[:, : 2 * nstate], (act * fade).astype(BF16))
    b = mm_tn(coeff[:, 2 * nstate : 4 * nstate], cot.astype(BF16))
    return a[:nstate], a[nstate:], b[:nstate], b[nstate:]


def totals_kernel(*refs, outer, inner, nstate):
    blocks, (cw, cb), outs, held = refs[:outer], refs[outer : outer + 2], refs[outer + 2 : -1], refs[-1]
    me = lax.axis_index("outer")
    place = lax.axis_index("inner")
    width = blocks[0].shape[1]
    lanes = pl.ds(pl.multiple_of(me * width, 128), width)
    for r in range(outer):
        held[me ^ r] = blocks[r][...]
    b = [Block(held[k], nstate) for k in range(outer)]
    none = jnp.zeros((EDGE, width), F32)
    low = []
    for k in range(outer):
        before = b[k - 1].sig if k else none
        after = b[k + 1].sig if k < outer - 1 else none
        act = act_rows(before, b[k].sig, after, cw, cb, lanes)
        low.append(edge_states(act, b[k].fade, b[k].cot, b[k].coeff, nstate))
    end = outer - 1
    f, x = b[0].f, b[0].br
    keep_f, keep_br = jnp.ones((1, width), F32), b[0].near_br
    for k in range(1, outer):
        y = low[k - 1][3] + b[k - 1].far_br * x
        factor = b[k].near_br * alike(b[k - 1].seg_last, b[k].seg_late)
        x = b[k].br + factor * y
        keep_br = keep_br * b[k - 1].far_br * factor
        factor = b[k].keep_f * alike(b[k - 1].seg_last, b[k].seg_last)
        f = b[k].f + low[k][0] + factor * f
        keep_f = keep_f * factor
    r, z = b[end].r, b[end].bf
    keep_r, keep_bf = jnp.ones((1, width), F32), b[end].near_bf
    for k in range(end - 1, -1, -1):
        y = low[k + 1][2] + b[k + 1].far_bf * z
        factor = b[k].near_bf * alike(b[k + 1].seg_first, b[k].seg_early)
        z = b[k].bf + factor * y
        keep_bf = keep_bf * b[k + 1].far_bf * factor
        factor = b[k].keep_r * alike(b[k + 1].seg_first, b[k].seg_first)
        r = b[k].r + low[k][1] + factor * r
        keep_r = keep_r * factor
    row = iota((EDGE, width), 0)
    half = row < 4

    def header(rows):
        tile = jnp.zeros((EDGE, width), F32)
        for k, value in enumerate(rows):
            tile = jnp.where(row == k, value, tile)
        high = tile.astype(BF16).astype(F32)
        return jnp.concatenate([high, tile - high], axis=0)

    up = (
        keep_f, b[0].keep_f, keep_br, b[end].far_br,
        b[0].seg_last, b[0].seg_late, b[end].seg_last,
    )
    down = (
        keep_r, b[end].keep_r, keep_bf, b[0].far_bf,
        b[end].seg_first, b[end].seg_early, b[0].seg_first,
    )
    sig = jnp.where(half, b[0].sig, b[end].sig)
    coeff = jnp.where(half, b[0].coeff, b[end].coeff)
    up_rows = jnp.where(half, b[0].fade, b[end].cot)
    down_rows = jnp.where(half, b[0].cot, b[end].fade)
    pad = jnp.zeros((EDGE, width), F32)
    up = jnp.concatenate([f, x, header(up), sig, coeff, up_rows, pad], axis=0)
    down = jnp.concatenate([r, z, header(down), sig, coeff, down_rows, pad], axis=0)
    for r in range(1, inner):
        towards = jnp.full(up.shape, place ^ r, jnp.int32) > place
        outs[r - 1][...] = jnp.where(towards, up, down).astype(BF16)


def entries_kernel(*refs, outer, inner, nstate):
    blocks = refs[:outer]
    others = refs[outer : outer + inner - 1]
    cw, cb = refs[outer + inner - 1 : outer + inner + 1]
    outs = refs[outer + inner + 1 : -3]
    held, far, entry = refs[-3:]
    me = lax.axis_index("outer")
    place = lax.axis_index("inner")
    width = blocks[0].shape[1]
    lanes = pl.ds(pl.multiple_of(me * width, 128), width)
    for r in range(outer):
        held[me ^ r] = blocks[r][...]
    far[place] = jnp.zeros(far.shape[1:], BF16)
    for r in range(1, inner):
        far[place ^ r] = others[r - 1][...]
    n, h = nstate, 2 * nstate
    zero = jnp.zeros((n, width), F32)
    none = jnp.zeros((EDGE, width), F32)
    line = jnp.zeros((1, width), F32)

    def step(carry, index, wanted, upward):
        state, x, y, edge, seg = carry
        p = far[index].astype(F32)
        keep = p[h : h + 8] + p[h + 8 : h + 16]
        sig, coeff, rows = (p[h + k : h + k + EDGE] for k in (16, 24, 32))
        if upward:
            act = act_rows(edge, sig, none, cw, cb, lanes)
            first, _, _, second = edge_states(act, rows, rows, coeff, n)
        else:
            act = act_rows(none, sig, edge, cw, cb, lanes)
            _, first, second, _ = edge_states(act, rows, rows, coeff, n)
        new = p[0:n] + keep[0:1] * (first + keep[1:2] * alike(seg, keep[4:5]) * state)
        new_x = p[n:h] + keep[2:3] * alike(seg, keep[5:6]) * y
        new_y = second + keep[3:4] * new_x
        return tuple(
            jnp.where(jnp.full(b.shape, wanted), b, a)
            for a, b in zip(carry, (new, new_x, new_y, sig, keep[6:7]))
        )

    up = down = (zero, zero, zero, none, line)
    for k in range(inner - 1):
        up = step(up, k, k < place, True)
        back = inner - 1 - k
        down = step(down, back, back > place, False)
    f, x, y, edge_up, seg_up = up
    r, z, w, edge_down, seg_down = down
    b = [Block(held[k], nstate) for k in range(outer)]
    low = []
    for k in range(outer):
        before = b[k - 1].sig if k else edge_up
        after = b[k + 1].sig if k < outer - 1 else edge_down
        act = act_rows(before, b[k].sig, after, cw, cb, lanes)
        low.append(edge_states(act, b[k].fade, b[k].cot, b[k].coeff, nstate))
    for k in range(outer):
        entry[k, 0:h] = jnp.concatenate([f, x], axis=0).astype(BF16)
        if k == outer - 1:
            break
        before = b[k - 1].seg_last if k else seg_up
        f = b[k].f + low[k][0] + b[k].keep_f * alike(before, b[k].seg_last) * f
        x = b[k].br + b[k].near_br * alike(before, b[k].seg_late) * y
        y = low[k][3] + b[k].far_br * x
    for k in range(outer - 1, -1, -1):
        entry[k, h : 2 * h] = jnp.concatenate([r, z], axis=0).astype(BF16)
        if k == 0:
            break
        after = b[k + 1].seg_first if k < outer - 1 else seg_down
        r = b[k].r + low[k][1] + b[k].keep_r * alike(after, b[k].seg_first) * r
        z = b[k].bf + b[k].near_bf * alike(after, b[k].seg_early) * w
        w = low[k][2] + b[k].far_bf * z
    for r_ in range(outer):
        outs[r_][...] = entry[me ^ r_]


def local_kernel(
    sig, cot, in_, out, segment, cw, cb, skip, table, sums, sums_t, before, after,
    mixed, base_f, gate_f, base_r, gate_r, out_f, out_r, low, ext, widen,
    *, part, parts,
):
    length, channels = sig.shape
    heads = table.shape[2]
    nstate = in_.shape[0]
    hdim = channels // heads
    margin = cw.shape[1] - 1
    prev, nxt, nf, pr = edge_sums(before, after, table, channels, nstate, heads, margin)
    bs, bc, bi, bo, bseg = prev
    as_, ac, ai, ao, aseg = nxt
    seg = segment[...].astype(F32)
    col_full = jnp.transpose(jnp.broadcast_to(seg, (length, length)))
    col = col_full[:, : 2 * heads]
    cf, cr = sums[0], sums[1]
    total_f = cf[length - 1 : length]
    total_r = sums[2, length - EDGE :][EDGE - 1 : EDGE]
    j = iota((EDGE, 2 * heads), 0)
    early = j < margin
    late = j >= EDGE - margin
    s_first, s_last = aseg[0:1], bseg[EDGE - 1 : EDGE]
    s_beyond, s_ahead = aseg[margin : margin + 1], bseg[EDGE - margin - 1 : EDGE - margin]
    stack = [
        jnp.where(col == s_last, jnp.exp(cf), 0.0),
        jnp.where(col == s_first, jnp.exp(total_r - cr), 0.0),
        jnp.where(col == s_first, jnp.exp(total_f - cf), 0.0),
        jnp.where(col == s_last, jnp.exp(cr), 0.0),
        jnp.where(early & (aseg == s_beyond), jnp.exp(nf[margin - 1 : margin] - nf), 0.0),
        jnp.where(
            late & (bseg == s_ahead), jnp.exp(pr[EDGE - margin : EDGE - margin + 1] - pr), 0.0
        ),
        jnp.where(early & (aseg == s_first), jnp.exp(nf), 0.0),
        jnp.where(late & (bseg == s_last), jnp.exp(pr), 0.0),
        jnp.where(
            j < 4,
            jnp.where(s_first == s_beyond, jnp.exp(nf[margin - 1 : margin]), 0.0),
            jnp.where(s_last == s_ahead, jnp.exp(pr[EDGE - margin : EDGE - margin + 1]), 0.0),
        ),
    ]
    turned = []
    for d in range(margin):
        move = (EDGE - d) % EDGE
        later = pltpu.roll(nf, move, 0) if d else nf
        seg_j = jnp.broadcast_to(aseg, (EDGE, 2 * heads))
        seg_l = pltpu.roll(seg_j, move, 0) if d else seg_j
        ao_d = pltpu.roll(ao, move, 0) if d else ao
        dot = jnp.sum(ai * ao_d, axis=1, keepdims=True)
        stack.append(jnp.where((j + d < margin) & (seg_j == seg_l), jnp.exp(later - nf) * dot, 0.0))
        former = pltpu.roll(pr, d, 0) if d else pr
        seg_j = jnp.broadcast_to(bseg, (EDGE, 2 * heads))
        seg_l = pltpu.roll(seg_j, d, 0) if d else seg_j
        bo_d = pltpu.roll(bo, d, 0) if d else bo
        dot = jnp.sum(bi * bo_d, axis=1, keepdims=True)
        stack.append(
            jnp.where((j - d >= EDGE - margin) & (seg_j == seg_l), jnp.exp(former - pr) * dot, 0.0)
        )
    stack = high_low(jnp.concatenate(stack, axis=0))
    ext[0:EDGE] = bs
    ext[EDGE : EDGE + length] = sig[...].astype(F32)
    ext[EDGE + length :] = as_
    width = channels // parts
    start = part * width
    widen[...] = spread(heads, channels, hdim)
    score = mm_tn(out[...], in_[...])
    t, s = iota((length, length), 0), iota((length, length), 1)
    same = col_full == seg
    score_f = jnp.where(same & (t >= s), score, 0.0)
    score_r = jnp.where(same & (t <= s), score, 0.0)
    lower = t >= s
    wide = 128
    first = iota((length, wide), 1) < hdim
    ao_b, bo_b = ao.astype(BF16), bo.astype(BF16)
    skip2 = mm(skip[...], spread(heads, channels, hdim)[0:heads].astype(F32), EXACT)
    for c in range(0, width, wide):
        sl = slice(start + c, start + c + wide)
        to = slice(c, c + wide)
        e = mm(stack, widen[:, sl])
        skip_f, skip_r = skip2[0:1, sl], skip2[1:2, sl]
        pre = conv(ext, EDGE, length + EDGE, cw[0], cb[0:1, sl], sl, -1)
        sg = jax.nn.sigmoid(pre)
        act_f = (pre * sg)[0:length]
        slope_f = sg * (1.0 + pre * (1.0 - sg))
        pre = conv(ext, 0, length + EDGE, cw[1], cb[1:2, sl], sl, 1)
        sg = jax.nn.sigmoid(pre)
        act_r = (pre * sg)[EDGE:]
        slope_r = sg * (1.0 + pre * (1.0 - sg))
        act = jnp.concatenate([act_f.astype(BF16), act_r.astype(BF16)], axis=0)
        ct16 = cot[:, sl]
        ct = ct16.astype(F32)
        forth, back = [], []
        for k in range(wide // hdim):
            h = (start + c) // hdim + k
            up = cf[:, h : h + 1] - sums_t[h : h + 1]
            down = sums_t[heads + h : heads + h + 1] - cr[:, h : h + 1]
            x = jnp.exp(jnp.minimum(jnp.where(lower, up, down), 0.0))
            m = jnp.concatenate([(x * score_f).astype(BF16), (x * score_r).astype(BF16)], axis=1)
            forth.append(mm(m, act))
            back.append(mm_tn(m, ct16))
        mixed[:, to] = jnp.where(first, forth[0], forth[1]) + skip_f * act_f + skip_r * act_r
        here_f = jnp.where(first, back[0][0:length], back[1][0:length]) + skip_f * ct
        here_r = jnp.where(first, back[0][length:], back[1][length:]) + skip_r * ct
        at = 4 * length
        ac_c, bc_c = ac[:, sl], bc[:, sl]
        row = iota((EDGE, wide), 0)
        beyond = jnp.where(row < margin, skip_f * ac_c, 0.0)
        ahead = jnp.where(row >= EDGE - margin, skip_r * bc_c, 0.0)
        for d in range(margin):
            k = at + (5 + 2 * d) * EDGE
            moved = pltpu.roll(ac_c, (EDGE - d) % EDGE, 0) if d else ac_c
            beyond += e[k : k + EDGE] * moved
            moved = pltpu.roll(bc_c, d, 0) if d else bc_c
            ahead += e[k + EDGE : k + 2 * EDGE] * moved
        out_f[:, to] = e[0:length]
        out_r[:, to] = e[length : 2 * length]
        base_f[0:length, to] = here_f * slope_f[0:length]
        base_f[length:, to] = beyond * slope_f[length:]
        gate_f[0:length, to] = e[2 * length : 3 * length] * slope_f[0:length]
        gate_f[length:, to] = e[at : at + EDGE] * slope_f[length:]
        base_r[EDGE:, to] = here_r * slope_r[EDGE:]
        base_r[0:EDGE, to] = ahead * slope_r[0:EDGE]
        gate_r[EDGE:, to] = e[3 * length : 4 * length] * slope_r[EDGE:]
        gate_r[0:EDGE, to] = e[at + EDGE : at + 2 * EDGE] * slope_r[0:EDGE]
        low[0:nstate, to] = mm_tn(ao_b, (ac_c * e[at + 2 * EDGE : at + 3 * EDGE]).astype(BF16))
        low[nstate : 2 * nstate, to] = mm_tn(
            bo_b, (bc_c * e[at + 3 * EDGE : at + 4 * EDGE]).astype(BF16)
        )
        low[2 * nstate :, to] = e[at + 4 * EDGE : at + 5 * EDGE]


def finish_kernel(*refs, outer, parts):
    entries = refs[:outer]
    locals_ = [refs[outer + 8 * p : outer + 8 * (p + 1)] for p in range(parts)]
    in_, out, before, after, cw, mixed, grad, state, df, dr = refs[outer + 8 * parts :]
    length, channels = mixed.shape
    nstate = in_.shape[0]
    me = lax.axis_index("outer")
    width = channels // outer
    for r in range(outer):
        state[:, pl.ds(pl.multiple_of((me ^ r) * width, 128), width)] = entries[r][...]
    per = channels // parts
    query, key = out[...], in_[...]
    at = 2 * channels
    beyond, ahead = after[:, at : at + nstate], before[:, at : at + nstate]
    lags = cw.shape[1]
    wide = 256
    for c in range(0, channels, wide):
        p, off = divmod(c, per)
        loc, base_f, gate_f, base_r, gate_r, out_f, out_r, low = locals_[p]
        to = slice(off, off + wide)
        sl = slice(c, c + wide)
        s = state[:, sl]
        mixed[:, sl] = (
            loc[:, to]
            + out_f[:, to] * mm_tn(query, s[0:nstate])
            + out_r[:, to] * mm_tn(query, s[2 * nstate : 3 * nstate])
        ).astype(BF16)
        s_br, s_bf = s[nstate : 2 * nstate], s[3 * nstate :]
        h_f = low[0:nstate, to] + low[2 * nstate : 2 * nstate + 1, to] * s_bf.astype(F32)
        h_r = low[nstate : 2 * nstate, to] + low[2 * nstate + 4 : 2 * nstate + 5, to] * s_br.astype(F32)
        df[0:length] = base_f[0:length, to] + gate_f[0:length, to] * mm_tn(key, h_f.astype(BF16))
        df[length:] = base_f[length:, to] + gate_f[length:, to] * mm(beyond, s_bf)
        dr[EDGE:] = base_r[EDGE:, to] + gate_r[EDGE:, to] * mm_tn(key, h_r.astype(BF16))
        dr[0:EDGE] = base_r[0:EDGE, to] + gate_r[0:EDGE, to] * mm(ahead, s_br)
        total = jnp.zeros((length, wide), F32)
        for lag in range(lags):
            total += cw[0, lag : lag + 1, sl] * df[lag : lag + length]
            total += cw[1, lag : lag + 1, sl] * dr[EDGE - lag : EDGE - lag + length]
        grad[:, sl] = total.astype(BF16)


def params():
    return pltpu.CompilerParams(vmem_limit_bytes=VMEM)


def cost(flops, size):
    return pl.CostEstimate(flops=flops, bytes_accessed=size, transcendentals=0)


def on_device(
    signal, in_coeff, out_coeff, cotangent, conv_weight, conv_bias, skip_gain, decay_table,
    bucket, segment, *, outer, inner,
):
    length, channels = signal.shape
    heads = skip_gain.shape[1]
    nstate = in_coeff.shape[1]
    axes = ("inner", "outer")
    count = outer * inner
    bucket = bucket.reshape(1, length)
    segment = segment.reshape(1, length)
    sds = jax.ShapeDtypeStruct
    width = channels // outer
    pay = 4 * nstate + 48
    far = 2 * nstate + 48
    arrays = (
        bucket, segment, decay_table, signal, conv_weight, conv_bias, in_coeff.T, cotangent,
        out_coeff.T,
    )
    whole = pl.BlockSpec(memory_space=pltpu.VMEM)
    in_t, out_t = in_coeff.T, out_coeff.T
    sums, sums_t, *blocks = pl.pallas_call(
        functools.partial(begin_kernel, outer=outer, count=len(arrays)),
        name="begin",
        in_specs=[pl.BlockSpec(memory_space=pltpu.HBM)] * len(arrays),
        out_shape=[sds((3, length, 2 * heads), F32), sds((2 * heads, length), F32)]
        + [sds((pay, width), BF16)] * outer,
        scratch_shapes=[
            pltpu.VMEM((pay, channels), BF16),
            pltpu.VMEM((length + 2 * EDGE, channels), F32),
            pltpu.VMEM((2 * heads, channels), BF16),
            pltpu.SemaphoreType.DMA((len(arrays),)),
        ]
        + [pltpu.VMEM(a.shape, a.dtype) for a in arrays],
        compiler_params=pltpu.CompilerParams(vmem_limit_bytes=BEGIN_VMEM),
        cost_estimate=cost(2 * 10**8, 2**21),
    )(*arrays)

    def swap(array, axis, size, r):
        return lax.ppermute(array, axis, [(i, i ^ r) for i in range(size)])

    blocks = [blocks[0]] + [swap(blocks[r], "outer", outer, r) for r in range(1, outer)]
    line = 2 * channels + 512
    late_bucket, _ = lax.optimization_barrier((bucket, sums))
    up_rows, down_rows = pl.pallas_call(
        edges_kernel,
        name="edges",
        out_shape=[sds((EDGE, line), BF16)] * 2,
        compiler_params=params(),
    )(signal, cotangent, in_t, out_t, late_bucket, segment)
    ahead = [(i, i + 1) for i in range(count - 1)]
    before = lax.ppermute(up_rows, axes, ahead)
    after = lax.ppermute(down_rows, axes, [(j, i) for i, j in ahead])
    parts = 2

    def local(part):
        per = channels // parts
        both_rows = length + EDGE
        return pl.pallas_call(
            functools.partial(local_kernel, part=part, parts=parts),
            name=f"local{part}",
            out_shape=[
                sds((length, per), F32),
                sds((both_rows, per), F32),
                sds((both_rows, per), F32),
                sds((both_rows, per), F32),
                sds((both_rows, per), F32),
                sds((length, per), F32),
                sds((length, per), F32),
                sds((2 * nstate + EDGE, per), F32),
            ],
            scratch_shapes=[
                pltpu.VMEM((length + 2 * EDGE, channels), F32),
                pltpu.VMEM((2 * heads, channels), BF16),
            ],
            compiler_params=params(),
            cost_estimate=cost(4 * 10**8, 2**22),
        )(
            signal, cotangent, in_t, out_t, segment, conv_weight, conv_bias, skip_gain,
            decay_table, sums, sums_t, before, after,
        )

    locals_ = [local(p) for p in range(parts)]
    totals = pl.pallas_call(
        functools.partial(totals_kernel, outer=outer, inner=inner, nstate=nstate),
        name="totals",
        out_shape=[sds((far, width), BF16)] * (inner - 1),
        scratch_shapes=[pltpu.VMEM((outer, pay, width), BF16)],
        compiler_params=params(),
        cost_estimate=cost(10**6, 2**19),
    )(*blocks, conv_weight, conv_bias)
    totals = [swap(totals[r - 1], "inner", inner, r) for r in range(1, inner)]
    entries = pl.pallas_call(
        functools.partial(entries_kernel, outer=outer, inner=inner, nstate=nstate),
        name="entries",
        out_shape=[sds((4 * nstate, width), BF16)] * outer,
        scratch_shapes=[
            pltpu.VMEM((outer, pay, width), BF16),
            pltpu.VMEM((inner, far, width), BF16),
            pltpu.VMEM((outer, 4 * nstate, width), BF16),
        ],
        compiler_params=params(),
        cost_estimate=cost(10**6, 2**19),
    )(*blocks, *totals, conv_weight, conv_bias)
    entries = [entries[0]] + [swap(entries[r], "outer", outer, r) for r in range(1, outer)]
    return pl.pallas_call(
        functools.partial(finish_kernel, outer=outer, parts=parts),
        name="finish",
        out_shape=[sds((length, channels), BF16)] * 2,
        scratch_shapes=[
            pltpu.VMEM((4 * nstate, channels), BF16),
            pltpu.VMEM((length + EDGE, 256), F32),
            pltpu.VMEM((length + EDGE, 256), F32),
        ],
        compiler_params=params(),
        cost_estimate=cost(10**8, 2**22),
    )(*entries, *[a for group in locals_ for a in group], in_t, out_t, before, after, conv_weight)


def solution(mesh):
    rows = P(("groups", "inner", "outer"), None)
    flat = P(("groups", "inner", "outer"))
    return jax.shard_map(
        functools.partial(on_device, outer=mesh.shape["outer"], inner=mesh.shape["inner"]),
        mesh=mesh,
        in_specs=(rows, rows, rows, rows, P(), P(), P(), P(), flat, flat),
        out_specs=(rows, rows),
        check_vma=False,
    )
```

```python
import functools

import jax
import jax.numpy as jnp
from jax import lax
from jax.experimental import pallas as pl
from jax.experimental.pallas import tpu as pltpu
from jax.sharding import PartitionSpec as P

F32, BF16 = jnp.float32, jnp.bfloat16
EXACT = lax.Precision.HIGHEST
EDGE = 8
VMEM = 14 * 2**20
NEVER = -1e4
BEGIN_VMEM = 58 * 2**20


def mm(a, b, precision=None):
    return lax.dot_general(
        a, b, (((1,), (0,)), ((), ())), precision=precision, preferred_element_type=F32
    )


def mm_tn(a, b, precision=None):
    return lax.dot_general(
        a, b, (((0,), (0,)), ((), ())), precision=precision, preferred_element_type=F32
    )


def mm_nt(a, b, precision=None):
    return lax.dot_general(
        a, b, (((1,), (1,)), ((), ())), precision=precision, preferred_element_type=F32
    )


def iota(shape, dim):
    return lax.broadcasted_iota(jnp.int32, shape, dim)


def twice(heads):
    col = iota((heads, 2 * heads), 1)
    col = jnp.where(col < heads, col, col - heads)
    return (iota((heads, 2 * heads), 0) == col).astype(F32)


def spread(heads, lanes, hdim, start=0):
    row = iota((2 * heads, lanes), 0)
    row = jnp.where(row < heads, row, row - heads)
    low = row * hdim
    col = iota((2 * heads, lanes), 1) + start
    return ((col >= low) & (col < low + hdim)).astype(BF16)


def high_low(x):
    high = x.astype(BF16).astype(F32)
    return jnp.where(iota(x.shape, 1) < x.shape[1] // 2, high, x - high).astype(BF16)


def one_hot(column, size):
    return (column == iota((column.shape[0], size), 1).astype(column.dtype)).astype(F32)


def edges_kernel(sig, cot, in_t, out_t, bucket, segment, mine, near, next_, own, sem):
    copy = pltpu.make_async_copy(mine, own, sem)
    copy.start()
    length = bucket.shape[1]
    channels = sig.shape[1]

    bcol = jnp.transpose(jnp.broadcast_to(bucket[...].astype(F32), (length, length)))
    scol = jnp.transpose(jnp.broadcast_to(segment[...].astype(F32), (length, length)))
    j, t = iota((EDGE, length), 0), iota((EDGE, length), 1)
    even = lax.axis_index("outer") % 2 == 0

    def ends(place, value):
        final, first = value(length - EDGE), value(0)
        here = jnp.full(final.shape, even)
        columns = slice(place, place + final.shape[1])
        near[:, columns] = jnp.where(here, final, first).astype(BF16)
        next_[:, columns] = jnp.where(here, first, final).astype(BF16)

    def rows_of(ref):
        def get(row):
            start = row // 16 * 16
            return ref[start : start + 16].astype(F32)[row - start : row - start + EDGE]

        return get

    for k, ref in enumerate((sig, cot)):
        ends(k * channels, rows_of(ref))
    for k, ref in enumerate((in_t, out_t)):
        ends(2 * channels + 128 * k, lambda row: mm_nt((t == j + row).astype(BF16), ref[...]))
    for k, full in enumerate((bcol, scol)):
        ends(2 * channels + 256 + 128 * k, lambda row: full[row : row + EDGE, :128])
    copy.wait()


def neighbours(near, next_):
    a, b = near[...].astype(F32), next_[...].astype(F32)
    even = jnp.full(a.shape, lax.axis_index("outer") % 2 == 0)
    return jnp.where(even, b, a), jnp.where(even, a, b)


def edge_parts(x, channels, state):
    return (
        x[:, :channels].astype(F32),
        x[:, channels : 2 * channels].astype(F32),
        x[:, 2 * channels : 2 * channels + state].astype(F32),
        x[:, 2 * channels + 128 : 2 * channels + 128 + state].astype(F32),
        x[:, 2 * channels + 256 : 2 * channels + 257].astype(F32),
        x[:, 2 * channels + 384 : 2 * channels + 385].astype(F32),
    )


def conv(ext, start, rows, weight, bias, sl, step):
    total = bias
    for lag in range(weight.shape[0]):
        at = start + step * lag
        total = total + weight[lag : lag + 1, sl] * ext[at : at + rows, sl]
    return total


def begin_kernel(*refs, outer, count):
    far, near = refs[:count], refs[-count:]
    sums, sums_t, *outs = refs[count : -count - 4]
    pay, ext, edge, sems = refs[-count - 4 : -count]
    copies = [pltpu.make_async_copy(a, b, sems.at[k]) for k, (a, b) in enumerate(zip(far, near))]
    for copy in copies:
        copy.start()
    bucket, segment, table, sig, cw, cb, in_t, cot, out_t = near
    for copy in copies[:3]:
        copy.wait()
    length, channels = sig.shape
    heads = table.shape[2]
    rows = table.shape[1]
    nstate = in_t.shape[0]
    hdim = channels // heads
    margin = cw.shape[1] - 1
    hot_t = (bucket[...] == iota((rows, length), 0)).astype(F32)
    row, col = iota((length, length), 0), iota((length, length), 1)
    counts = mm_nt((row >= col).astype(F32), hot_t)
    strict = mm_nt((row > col).astype(F32), hot_t)
    counts_t = mm(hot_t, (row <= col).astype(F32))
    strict_t = counts_t - hot_t
    dup = twice(heads)
    table_f = mm(table[0], dup, EXACT)
    table_r = mm(table[1], dup, EXACT)
    cf = mm(counts, table_f, EXACT)
    cr = mm(strict, table_r, EXACT)
    ci = mm(counts, table_r, EXACT)
    sums[0], sums[1], sums[2] = cf, cr, ci
    sums_t[0:heads] = mm_tn(table[0], counts_t, EXACT)
    sums_t[heads : 2 * heads] = mm_tn(table[1], strict_t, EXACT)
    seg = segment[...].astype(F32)
    seg_col = jnp.transpose(jnp.broadcast_to(seg, (length, length)))[:, : 2 * heads]
    t = iota((length, 2 * heads), 0)
    last, tail = length - 1, length - margin

    def at(place):
        return seg[:, place : place + 1]

    def fade(arg, anchor, keep):
        return high_low(jnp.where((seg_col == at(anchor)) & keep, jnp.exp(arg), 0.0))

    fade_f = fade(cf[last:] - cf, last, t >= margin)
    fade_br = fade(cr[tail : tail + 1] - cr, tail - 1, t < tail)
    fade_r = fade(cr, 0, t < tail)
    fade_bf = fade(cf - cf[margin - 1 : margin], margin, t >= margin)
    total_f, total_r = cf[last:], ci[last:]
    j = iota((EDGE, 2 * heads), 0)
    early, late = j < margin, j >= EDGE - margin
    at_tail = cr[tail : tail + 1]
    logs = (
        total_f,
        at_tail,
        jnp.where(at(tail - 1) == at(last), total_r - at_tail, NEVER),
        total_r,
        total_f - cf[margin - 1 : margin],
        jnp.where(at(0) == at(margin), cf[margin - 1 : margin], NEVER),
    )
    keeps = jnp.zeros((EDGE, 2 * heads), F32)
    for k, value in enumerate(logs):
        keeps = jnp.where(j == k, value, keeps)
    cf_0, cr_l = cf[0:EDGE], cr[length - EDGE :]
    seg_0, seg_l = seg_col[0:EDGE], seg_col[length - EDGE :]
    act_fade = jnp.where(
        early & (seg_0 == at(last)),
        jnp.exp(total_f - cf_0),
        jnp.where(late & (seg_l == at(0)), jnp.exp(cr_l), 0.0),
    )
    cot_fade = jnp.where(
        early & (seg_0 == at(0)),
        jnp.exp(cf_0),
        jnp.where(late & (seg_l == at(last)), jnp.exp(total_r - cr_l), 0.0),
    )
    small = high_low(jnp.concatenate([keeps, act_fade, cot_fade], axis=0))
    ext[0:EDGE] = jnp.zeros((EDGE, channels), F32)
    ext[EDGE + length :] = jnp.zeros((EDGE, channels), F32)
    edge[...] = spread(heads, channels, hdim)
    for copy in copies[3:]:
        copy.wait()
    ext[EDGE : EDGE + length] = sig[...].astype(F32)
    keys, queries = in_t[...], out_t[...]
    wide = 256
    for c in range(0, channels, wide):
        sl = slice(c, c + wide)
        widen = edge[:, sl]
        pre = conv(ext, EDGE, length, cw[0], cb[0:1, sl], sl, -1)
        act = pre * jax.nn.sigmoid(pre)
        pay[0:nstate, sl] = mm(keys, (act * mm(fade_f, widen)).astype(BF16)).astype(BF16)
        pre = conv(ext, EDGE, length, cw[1], cb[1:2, sl], sl, 1)
        act = pre * jax.nn.sigmoid(pre)
        pay[2 * nstate : 3 * nstate, sl] = mm(keys, (act * mm(fade_r, widen)).astype(BF16)).astype(
            BF16
        )
        ct = cot[:, sl].astype(F32)
        pay[nstate : 2 * nstate, sl] = mm(queries, (ct * mm(fade_br, widen)).astype(BF16)).astype(
            BF16
        )
        pay[3 * nstate : 4 * nstate, sl] = mm(
            queries, (ct * mm(fade_bf, widen)).astype(BF16)
        ).astype(BF16)
    e = mm(small, edge[...])
    row = iota((EDGE, channels), 0)

    def tile(ref):
        top = ref[0:16].astype(F32)[0:EDGE]
        return jnp.where(row < 4, top, ref[length - 16 :].astype(F32)[EDGE:])

    def spare(rows, first):
        filled = jnp.where(row == 3, e[first : first + 1], rows)
        return jnp.where(row == 4, e[first + 1 : first + 2], filled)

    k, s = iota((EDGE, length), 0), iota((EDGE, length), 1)
    lines = jnp.concatenate([keys, keys, queries, queries], axis=0)
    firsts = mm_nt(((k < margin) & (s == k)).astype(BF16), lines)
    finals = mm_nt(((k >= EDGE - margin) & (s == k + length - EDGE)).astype(BF16), lines)
    group = iota(firsts.shape, 1) // nstate
    coeff = jnp.where(group % 2 == 0, firsts, finals)
    coeff = jnp.where(
        k == 3,
        jnp.where(
            group == 0,
            at(0),
            jnp.where(group == 1, at(margin), jnp.where(group == 2, at(tail - 1), at(last))),
        ),
        coeff,
    )
    width = channels // outer
    if width > coeff.shape[1]:
        coeff = jnp.concatenate(
            [coeff, jnp.zeros((EDGE, width - coeff.shape[1]), F32)], axis=1
        )
    coeff = jnp.concatenate([coeff] * outer, axis=1)
    base = 4 * nstate
    pay[base : base + 16] = jnp.concatenate(
        [spare(tile(sig), 0), spare(e[EDGE : 2 * EDGE], 2)], axis=0
    ).astype(BF16)
    pay[base + 16 : base + 32] = jnp.concatenate(
        [spare(tile(cot) * e[2 * EDGE :], 4), coeff], axis=0
    ).astype(BF16)
    me = lax.axis_index("outer")
    for r in range(outer):
        outs[r][...] = pay[:, pl.ds(pl.multiple_of((me ^ r) * width, 128), width)]


def edge_sums(before, after, table, channels, state, heads, margin):
    dup = twice(heads)
    table_f = mm(table[0], dup, EXACT)
    table_r = mm(table[1], dup, EXACT)
    bs, bc, bi, bo, bb, bseg = edge_parts(before, channels, state)
    as_, ac, ai, ao, ab, aseg = edge_parts(after, channels, state)
    tri = (iota((EDGE, EDGE), 0) >= iota((EDGE, EDGE), 1)).astype(F32)
    rev = (iota((EDGE, EDGE), 0) <= iota((EDGE, EDGE), 1)).astype(F32)
    rows = table.shape[1]
    nf = mm(mm(tri, one_hot(ab, rows)), table_f, EXACT)
    pr = mm(mm(rev, one_hot(bb, rows)), table_r, EXACT)
    return (bs, bc, bi, bo, bseg), (as_, ac, ai, ao, aseg), nf, pr


class Block:
    def __init__(self, ref, nstate):
        x = ref.astype(F32)
        h = 4 * nstate
        self.f, self.br = x[0:nstate], x[nstate : 2 * nstate]
        self.r, self.bf = x[2 * nstate : 3 * nstate], x[3 * nstate : h]
        self.sig, self.fade = x[h : h + 8], x[h + 8 : h + 16]
        self.cot, self.coeff = x[h + 16 : h + 24], x[h + 24 : h + 32]
        self.keep_f, self.near_br = self.sig[3:4], self.sig[4:5]
        self.far_br, self.keep_r = self.fade[3:4], self.fade[4:5]
        self.near_bf, self.far_bf = self.cot[3:4], self.cot[4:5]
        self.seg_first, self.seg_early = self.coeff[3:4, 0:1], self.coeff[3:4, nstate : nstate + 1]
        self.seg_late = self.coeff[3:4, 2 * nstate : 2 * nstate + 1]
        self.seg_last = self.coeff[3:4, 3 * nstate : 3 * nstate + 1]


def alike(a, b):
    return jnp.where(a == b, 0.0, NEVER)


def act_rows(before, here, after, cw, cb, lanes):
    row = iota(here.shape, 0)
    pre_f = cb[0:1, lanes] + cw[0, 0:1, lanes] * here
    pre_r = cb[1:2, lanes] + cw[1, 0:1, lanes] * here
    for lag in range(1, cw.shape[1]):
        moved = pltpu.roll(jnp.where(row >= EDGE - lag, before, here), lag, 0)
        pre_f += cw[0, lag : lag + 1, lanes] * moved
        moved = pltpu.roll(jnp.where(row < lag, after, here), EDGE - lag, 0)
        pre_r += cw[1, lag : lag + 1, lanes] * moved
    pre = jnp.where(row < 4, pre_f, pre_r)
    return pre * jax.nn.sigmoid(pre)


def edge_states(act, fade, cot, coeff, nstate):
    coeff = coeff.astype(BF16)
    row = iota(cot.shape, 0)
    edge = (row < 3) | (row > 4)
    a = mm_tn(coeff[:, : 2 * nstate], jnp.where(edge, act * fade, 0.0).astype(BF16))
    b = mm_tn(coeff[:, 2 * nstate : 4 * nstate], jnp.where(edge, cot, 0.0).astype(BF16))
    return a[:nstate], a[nstate:], b[:nstate], b[nstate:]


def totals_kernel(*refs, outer, inner, nstate):
    blocks, (cw, cb), outs, held = refs[:outer], refs[outer : outer + 2], refs[outer + 2 : -1], refs[-1]
    me = lax.axis_index("outer")
    place = lax.axis_index("inner")
    width = blocks[0].shape[1]
    lanes = pl.ds(pl.multiple_of(me * width, 128), width)
    for r in range(outer):
        held[me ^ r] = blocks[r][...]
    b = [Block(held[k], nstate) for k in range(outer)]
    none = jnp.zeros((EDGE, width), F32)
    low = []
    for k in range(outer):
        before = b[k - 1].sig if k else none
        after = b[k + 1].sig if k < outer - 1 else none
        act = act_rows(before, b[k].sig, after, cw, cb, lanes)
        low.append(edge_states(act, b[k].fade, b[k].cot, b[k].coeff, nstate))
    end = outer - 1
    f, x = b[0].f, b[0].br
    keep_f, keep_br = jnp.zeros((1, width), F32), b[0].near_br
    for k in range(1, outer):
        y = low[k - 1][3] + jnp.exp(b[k - 1].far_br) * x
        factor = b[k].near_br + alike(b[k - 1].seg_last, b[k].seg_late)
        x = b[k].br + jnp.exp(factor) * y
        keep_br = keep_br + b[k - 1].far_br + factor
        factor = b[k].keep_f + alike(b[k - 1].seg_last, b[k].seg_last)
        f = b[k].f + low[k][0] + jnp.exp(factor) * f
        keep_f = keep_f + factor
    r, z = b[end].r, b[end].bf
    keep_r, keep_bf = jnp.zeros((1, width), F32), b[end].near_bf
    for k in range(end - 1, -1, -1):
        y = low[k + 1][2] + jnp.exp(b[k + 1].far_bf) * z
        factor = b[k].near_bf + alike(b[k + 1].seg_first, b[k].seg_early)
        z = b[k].bf + jnp.exp(factor) * y
        keep_bf = keep_bf + b[k + 1].far_bf + factor
        factor = b[k].keep_r + alike(b[k + 1].seg_first, b[k].seg_first)
        r = b[k].r + low[k][1] + jnp.exp(factor) * r
        keep_r = keep_r + factor
    row = iota((EDGE, width), 0)
    half = row < 4

    def spare(rows, first, second):
        return jnp.where(row == 3, first, jnp.where(row == 4, second, rows))

    def named(rows, *values):
        group = iota(rows.shape, 1) // nstate
        for k, value in enumerate(values):
            rows = jnp.where((row == 3) & (group == k), value, rows)
        return rows

    sig = jnp.where(half, b[0].sig, b[end].sig)
    coeff = jnp.where(half, b[0].coeff, b[end].coeff)
    up = jnp.concatenate(
        [
            f,
            x,
            spare(sig, keep_f, b[0].keep_f),
            named(coeff, b[0].seg_last, b[0].seg_late, b[end].seg_last),
            spare(jnp.where(half, b[0].fade, b[end].cot), keep_br, b[end].far_br),
        ],
        axis=0,
    )
    down = jnp.concatenate(
        [
            r,
            z,
            spare(sig, keep_r, b[end].keep_r),
            named(coeff, b[end].seg_first, b[end].seg_early, b[0].seg_first),
            spare(jnp.where(half, b[0].cot, b[end].fade), keep_bf, b[0].far_bf),
        ],
        axis=0,
    )
    for r in range(1, inner):
        towards = jnp.full(up.shape, place ^ r, jnp.int32) > place
        outs[r - 1][...] = jnp.where(towards, up, down).astype(BF16)


def entries_kernel(*refs, outer, inner, nstate):
    blocks = refs[:outer]
    others = refs[outer : outer + inner - 1]
    cw, cb = refs[outer + inner - 1 : outer + inner + 1]
    outs = refs[outer + inner + 1 : -3]
    held, far, entry = refs[-3:]
    me = lax.axis_index("outer")
    place = lax.axis_index("inner")
    width = blocks[0].shape[1]
    lanes = pl.ds(pl.multiple_of(me * width, 128), width)
    for r in range(outer):
        held[me ^ r] = blocks[r][...]
    n, h = nstate, 2 * nstate
    far[place] = jnp.zeros(far.shape[1:], F32)
    for r in range(1, inner):
        far[place ^ r] = others[r - 1][...].astype(F32)
    zero = jnp.zeros((n, width), F32)
    none = jnp.zeros((EDGE, width), F32)
    line = jnp.zeros((1, 1), F32)

    def step(carry, index, wanted, upward):
        state, x, y, edge, seg = carry
        p = far[index]
        sig, coeff, rows = (p[h + k : h + k + EDGE] for k in (0, EDGE, 2 * EDGE))
        segs = [coeff[3:4, k * n : k * n + 1] for k in range(3)]
        if upward:
            act = act_rows(edge, sig, none, cw, cb, lanes)
            first, _, _, second = edge_states(act, rows, rows, coeff, n)
        else:
            act = act_rows(none, sig, edge, cw, cb, lanes)
            _, first, second, _ = edge_states(act, rows, rows, coeff, n)
        inside = jnp.exp(sig[4:5] + alike(seg, segs[0]))
        new = p[0:n] + jnp.exp(sig[3:4]) * (first + inside * state)
        new_x = p[n:h] + jnp.exp(rows[3:4] + alike(seg, segs[1])) * y
        new_y = second + jnp.exp(rows[4:5]) * new_x
        return tuple(
            jnp.where(jnp.full(b.shape, wanted), b, a)
            for a, b in zip(carry, (new, new_x, new_y, sig, segs[2]))
        )

    up = down = (zero, zero, zero, none, line)
    for k in range(inner - 1):
        up = step(up, k, k < place, True)
        back = inner - 1 - k
        down = step(down, back, back > place, False)
    f, x, y, edge_up, seg_up = up
    r, z, w, edge_down, seg_down = down
    b = [Block(held[k], nstate) for k in range(outer)]
    low = []
    for k in range(outer):
        before = b[k - 1].sig if k else edge_up
        after = b[k + 1].sig if k < outer - 1 else edge_down
        act = act_rows(before, b[k].sig, after, cw, cb, lanes)
        low.append(edge_states(act, b[k].fade, b[k].cot, b[k].coeff, nstate))
    for k in range(outer):
        entry[k, 0:h] = jnp.concatenate([f, x], axis=0).astype(BF16)
        if k == outer - 1:
            break
        before = b[k - 1].seg_last if k else seg_up
        f = b[k].f + low[k][0] + jnp.exp(b[k].keep_f + alike(before, b[k].seg_last)) * f
        x = b[k].br + jnp.exp(b[k].near_br + alike(before, b[k].seg_late)) * y
        y = low[k][3] + jnp.exp(b[k].far_br) * x
    for k in range(outer - 1, -1, -1):
        entry[k, h : 2 * h] = jnp.concatenate([r, z], axis=0).astype(BF16)
        if k == 0:
            break
        after = b[k + 1].seg_first if k < outer - 1 else seg_down
        r = b[k].r + low[k][1] + jnp.exp(b[k].keep_r + alike(after, b[k].seg_first)) * r
        z = b[k].bf + jnp.exp(b[k].near_bf + alike(after, b[k].seg_early)) * w
        w = low[k][2] + jnp.exp(b[k].far_bf) * z
    for r_ in range(outer):
        outs[r_][...] = entry[me ^ r_]


def local_kernel(
    sig, cot, in_, out, segment, cw, cb, skip, table, sums, sums_t, before, after,
    mixed, base_f, gate_f, base_r, gate_r, out_f, out_r, low, ext, widen,
    *, part, parts,
):
    length, channels = sig.shape
    heads = table.shape[2]
    nstate = in_.shape[0]
    hdim = channels // heads
    margin = cw.shape[1] - 1
    prev, nxt, nf, pr = edge_sums(*neighbours(before, after), table, channels, nstate, heads, margin)
    bs, bc, bi, bo, bseg = prev
    as_, ac, ai, ao, aseg = nxt
    seg = segment[...].astype(F32)
    col_full = jnp.transpose(jnp.broadcast_to(seg, (length, length)))
    col = col_full[:, : 2 * heads]
    cf, cr = sums[0], sums[1]
    total_f = cf[length - 1 : length]
    total_r = sums[2, length - EDGE :][EDGE - 1 : EDGE]
    j = iota((EDGE, 2 * heads), 0)
    early = j < margin
    late = j >= EDGE - margin
    s_first, s_last = aseg[0:1], bseg[EDGE - 1 : EDGE]
    s_beyond, s_ahead = aseg[margin : margin + 1], bseg[EDGE - margin - 1 : EDGE - margin]
    stack = [
        jnp.where(col == s_last, jnp.exp(cf), 0.0),
        jnp.where(col == s_first, jnp.exp(total_r - cr), 0.0),
        jnp.where(col == s_first, jnp.exp(total_f - cf), 0.0),
        jnp.where(col == s_last, jnp.exp(cr), 0.0),
        jnp.where(early & (aseg == s_beyond), jnp.exp(nf[margin - 1 : margin] - nf), 0.0),
        jnp.where(
            late & (bseg == s_ahead), jnp.exp(pr[EDGE - margin : EDGE - margin + 1] - pr), 0.0
        ),
        jnp.where(early & (aseg == s_first), jnp.exp(nf), 0.0),
        jnp.where(late & (bseg == s_last), jnp.exp(pr), 0.0),
        jnp.where(
            j < 4,
            jnp.where(s_first == s_beyond, jnp.exp(nf[margin - 1 : margin]), 0.0),
            jnp.where(s_last == s_ahead, jnp.exp(pr[EDGE - margin : EDGE - margin + 1]), 0.0),
        ),
    ]
    turned = []
    for d in range(margin):
        move = (EDGE - d) % EDGE
        later = pltpu.roll(nf, move, 0) if d else nf
        seg_j = jnp.broadcast_to(aseg, (EDGE, 2 * heads))
        seg_l = pltpu.roll(seg_j, move, 0) if d else seg_j
        ao_d = pltpu.roll(ao, move, 0) if d else ao
        dot = jnp.sum(ai * ao_d, axis=1, keepdims=True)
        stack.append(jnp.where((j + d < margin) & (seg_j == seg_l), jnp.exp(later - nf) * dot, 0.0))
        former = pltpu.roll(pr, d, 0) if d else pr
        seg_j = jnp.broadcast_to(bseg, (EDGE, 2 * heads))
        seg_l = pltpu.roll(seg_j, d, 0) if d else seg_j
        bo_d = pltpu.roll(bo, d, 0) if d else bo
        dot = jnp.sum(bi * bo_d, axis=1, keepdims=True)
        stack.append(
            jnp.where((j - d >= EDGE - margin) & (seg_j == seg_l), jnp.exp(former - pr) * dot, 0.0)
        )
    stack = high_low(jnp.concatenate(stack, axis=0))
    ext[0:EDGE] = bs
    ext[EDGE : EDGE + length] = sig[...].astype(F32)
    ext[EDGE + length :] = as_
    width = channels // parts
    start = part * width
    widen[...] = spread(heads, channels, hdim)
    score = mm_tn(out[...], in_[...])
    t, s = iota((length, length), 0), iota((length, length), 1)
    same = col_full == seg
    score_f = jnp.where(same & (t >= s), score, 0.0)
    score_r = jnp.where(same & (t <= s), score, 0.0)
    lower = t >= s
    wide = 128
    first = iota((length, wide), 1) < hdim
    ao_b, bo_b = ao.astype(BF16), bo.astype(BF16)
    skip2 = mm(skip[...], spread(heads, channels, hdim)[0:heads].astype(F32), EXACT)
    for c in range(0, width, wide):
        sl = slice(start + c, start + c + wide)
        to = slice(c, c + wide)
        e = mm(stack, widen[:, sl])
        skip_f, skip_r = skip2[0:1, sl], skip2[1:2, sl]
        pre = conv(ext, EDGE, length + EDGE, cw[0], cb[0:1, sl], sl, -1)
        sg = jax.nn.sigmoid(pre)
        act_f = (pre * sg)[0:length]
        slope_f = sg * (1.0 + pre * (1.0 - sg))
        pre = conv(ext, 0, length + EDGE, cw[1], cb[1:2, sl], sl, 1)
        sg = jax.nn.sigmoid(pre)
        act_r = (pre * sg)[EDGE:]
        slope_r = sg * (1.0 + pre * (1.0 - sg))
        act = jnp.concatenate([act_f.astype(BF16), act_r.astype(BF16)], axis=0)
        ct16 = cot[:, sl]
        ct = ct16.astype(F32)
        forth, back = [], []
        for k in range(wide // hdim):
            h = (start + c) // hdim + k
            up = cf[:, h : h + 1] - sums_t[h : h + 1]
            down = sums_t[heads + h : heads + h + 1] - cr[:, h : h + 1]
            x = jnp.exp(jnp.minimum(jnp.where(lower, up, down), 0.0))
            m = jnp.concatenate([(x * score_f).astype(BF16), (x * score_r).astype(BF16)], axis=1)
            forth.append(mm(m, act))
            back.append(mm_tn(m, ct16))
        mixed[:, to] = jnp.where(first, forth[0], forth[1]) + skip_f * act_f + skip_r * act_r
        here_f = jnp.where(first, back[0][0:length], back[1][0:length]) + skip_f * ct
        here_r = jnp.where(first, back[0][length:], back[1][length:]) + skip_r * ct
        at = 4 * length
        ac_c, bc_c = ac[:, sl], bc[:, sl]
        row = iota((EDGE, wide), 0)
        beyond = jnp.where(row < margin, skip_f * ac_c, 0.0)
        ahead = jnp.where(row >= EDGE - margin, skip_r * bc_c, 0.0)
        for d in range(margin):
            k = at + (5 + 2 * d) * EDGE
            moved = pltpu.roll(ac_c, (EDGE - d) % EDGE, 0) if d else ac_c
            beyond += e[k : k + EDGE] * moved
            moved = pltpu.roll(bc_c, d, 0) if d else bc_c
            ahead += e[k + EDGE : k + 2 * EDGE] * moved
        out_f[:, to] = e[0:length]
        out_r[:, to] = e[length : 2 * length]
        base_f[0:length, to] = here_f * slope_f[0:length]
        base_f[length:, to] = beyond * slope_f[length:]
        gate_f[0:length, to] = e[2 * length : 3 * length] * slope_f[0:length]
        gate_f[length:, to] = e[at : at + EDGE] * slope_f[length:]
        base_r[EDGE:, to] = here_r * slope_r[EDGE:]
        base_r[0:EDGE, to] = ahead * slope_r[0:EDGE]
        gate_r[EDGE:, to] = e[3 * length : 4 * length] * slope_r[EDGE:]
        gate_r[0:EDGE, to] = e[at + EDGE : at + 2 * EDGE] * slope_r[0:EDGE]
        low[0:nstate, to] = mm_tn(ao_b, (ac_c * e[at + 2 * EDGE : at + 3 * EDGE]).astype(BF16))
        low[nstate : 2 * nstate, to] = mm_tn(
            bo_b, (bc_c * e[at + 3 * EDGE : at + 4 * EDGE]).astype(BF16)
        )
        low[2 * nstate :, to] = e[at + 4 * EDGE : at + 5 * EDGE]


def finish_kernel(*refs, outer, parts):
    entries = refs[:outer]
    locals_ = [refs[outer + 8 * p : outer + 8 * (p + 1)] for p in range(parts)]
    in_, out, before, after, cw, mixed, grad, state, df, dr = refs[outer + 8 * parts :]
    length, channels = mixed.shape
    nstate = in_.shape[0]
    me = lax.axis_index("outer")
    width = channels // outer
    for r in range(outer):
        state[:, pl.ds(pl.multiple_of((me ^ r) * width, 128), width)] = entries[r][...]
    per = channels // parts
    query, key = out[...], in_[...]
    at = 2 * channels
    ahead, beyond = neighbours(before.at[:, at : at + 128], after.at[:, at : at + 128])
    ahead, beyond = ahead[:, :nstate].astype(BF16), beyond[:, :nstate].astype(BF16)
    lags = cw.shape[1]
    wide = 256
    for c in range(0, channels, wide):
        p, off = divmod(c, per)
        loc, base_f, gate_f, base_r, gate_r, out_f, out_r, low = locals_[p]
        to = slice(off, off + wide)
        sl = slice(c, c + wide)
        s = state[:, sl]
        mixed[:, sl] = (
            loc[:, to]
            + out_f[:, to] * mm_tn(query, s[0:nstate])
            + out_r[:, to] * mm_tn(query, s[2 * nstate : 3 * nstate])
        ).astype(BF16)
        s_br, s_bf = s[nstate : 2 * nstate], s[3 * nstate :]
        h_f = low[0:nstate, to] + low[2 * nstate : 2 * nstate + 1, to] * s_bf.astype(F32)
        h_r = low[nstate : 2 * nstate, to] + low[2 * nstate + 4 : 2 * nstate + 5, to] * s_br.astype(F32)
        df[0:length] = base_f[0:length, to] + gate_f[0:length, to] * mm_tn(key, h_f.astype(BF16))
        df[length:] = base_f[length:, to] + gate_f[length:, to] * mm(beyond, s_bf)
        dr[EDGE:] = base_r[EDGE:, to] + gate_r[EDGE:, to] * mm_tn(key, h_r.astype(BF16))
        dr[0:EDGE] = base_r[0:EDGE, to] + gate_r[0:EDGE, to] * mm(ahead, s_br)
        total = jnp.zeros((length, wide), F32)
        for lag in range(lags):
            total += cw[0, lag : lag + 1, sl] * df[lag : lag + length]
            total += cw[1, lag : lag + 1, sl] * dr[EDGE - lag : EDGE - lag + length]
        grad[:, sl] = total.astype(BF16)


def params():
    return pltpu.CompilerParams(vmem_limit_bytes=VMEM)


def cost(flops, size):
    return pl.CostEstimate(flops=flops, bytes_accessed=size, transcendentals=0)


def on_device(
    signal, in_coeff, out_coeff, cotangent, conv_weight, conv_bias, skip_gain, decay_table,
    bucket, segment, *, outer, inner,
):
    length, channels = signal.shape
    heads = skip_gain.shape[1]
    nstate = in_coeff.shape[1]
    axes = ("inner", "outer")
    count = outer * inner
    bucket = bucket.reshape(1, length)
    segment = segment.reshape(1, length)
    sds = jax.ShapeDtypeStruct
    width = channels // outer
    pay = 4 * nstate + 4 * EDGE
    far = 2 * nstate + 3 * EDGE
    in_t, out_t = in_coeff.T, out_coeff.T
    arrays = (
        bucket, segment, decay_table, signal, conv_weight, conv_bias, in_coeff.T, cotangent,
        out_coeff.T,
    )
    whole = pl.BlockSpec(memory_space=pltpu.VMEM)
    sums, sums_t, *blocks = pl.pallas_call(
        functools.partial(begin_kernel, outer=outer, count=len(arrays)),
        name="begin",
        in_specs=[pl.BlockSpec(memory_space=pltpu.HBM)] * len(arrays),
        out_shape=[sds((3, length, 2 * heads), F32), sds((2 * heads, length), F32)]
        + [sds((pay, width), BF16)] * outer,
        scratch_shapes=[
            pltpu.VMEM((pay, channels), BF16),
            pltpu.VMEM((length + 2 * EDGE, channels), F32),
            pltpu.VMEM((2 * heads, channels), BF16),
            pltpu.SemaphoreType.DMA((len(arrays),)),
        ]
        + [pltpu.VMEM(a.shape, a.dtype) for a in arrays],
        compiler_params=pltpu.CompilerParams(vmem_limit_bytes=BEGIN_VMEM),
        cost_estimate=cost(2 * 10**8, 2**21),
    )(*arrays)

    def swap(array, axis, size, r):
        return lax.ppermute(array, axis, [(i, i ^ r) for i in range(size)])

    def exchange(arrays, axis, size):
        got = {r: swap(arrays[r], axis, size, r) for r in reversed(range(1, size))}
        return [got[r] for r in range(1, size)]

    blocks = [blocks[0], *exchange(blocks, "outer", outer)]
    line = 2 * channels + 512
    whole = pl.BlockSpec(memory_space=pltpu.VMEM)
    near_rows, next_rows, blocks[0] = pl.pallas_call(
        edges_kernel,
        name="edges",
        in_specs=[whole] * 6 + [pl.BlockSpec(memory_space=pltpu.HBM)],
        out_specs=[whole] * 3,
        out_shape=[sds((EDGE, line), BF16)] * 2 + [sds((pay, width), BF16)],
        scratch_shapes=[pltpu.SemaphoreType.DMA],
        compiler_params=params(),
        cost_estimate=cost(10**6, 2**18),
    )(signal, cotangent, in_t, out_t, bucket, segment, blocks[0])
    before = lax.ppermute(near_rows, "outer", [(i, i ^ 1) for i in range(outer)])
    pairs = [(i, i + 1) for i in range(1, count - 1, 2)]
    after = lax.ppermute(next_rows, axes, pairs + [(j, i) for i, j in pairs])
    parts = 2

    def local(part):
        per = channels // parts
        both_rows = length + EDGE
        return pl.pallas_call(
            functools.partial(local_kernel, part=part, parts=parts),
            name=f"local{part}",
            out_shape=[
                sds((length, per), F32),
                sds((both_rows, per), F32),
                sds((both_rows, per), F32),
                sds((both_rows, per), F32),
                sds((both_rows, per), F32),
                sds((length, per), F32),
                sds((length, per), F32),
                sds((2 * nstate + EDGE, per), F32),
            ],
            scratch_shapes=[
                pltpu.VMEM((length + 2 * EDGE, channels), F32),
                pltpu.VMEM((2 * heads, channels), BF16),
            ],
            compiler_params=params(),
            cost_estimate=cost(4 * 10**8, 2**22),
        )(
            signal, cotangent, in_t, out_t, segment, conv_weight, conv_bias, skip_gain,
            decay_table, sums, sums_t, before, after,
        )

    locals_ = [local(p) for p in range(parts)]
    totals = pl.pallas_call(
        functools.partial(totals_kernel, outer=outer, inner=inner, nstate=nstate),
        name="totals",
        out_shape=[sds((far, width), BF16)] * (inner - 1),
        scratch_shapes=[pltpu.VMEM((outer, pay, width), BF16)],
        compiler_params=params(),
        cost_estimate=cost(10**6, 2**19),
    )(*blocks, conv_weight, conv_bias)
    totals = exchange([None, *totals], "inner", inner)
    entries = pl.pallas_call(
        functools.partial(entries_kernel, outer=outer, inner=inner, nstate=nstate),
        name="entries",
        out_shape=[sds((4 * nstate, width), BF16)] * outer,
        scratch_shapes=[
            pltpu.VMEM((outer, pay, width), BF16),
            pltpu.VMEM((inner, far, width), F32),
            pltpu.VMEM((outer, 4 * nstate, width), BF16),
        ],
        compiler_params=params(),
        cost_estimate=cost(10**6, 2**19),
    )(*blocks, *totals, conv_weight, conv_bias)
    entries = [entries[0], *exchange(entries, "outer", outer)]
    return pl.pallas_call(
        functools.partial(finish_kernel, outer=outer, parts=parts),
        name="finish",
        out_shape=[sds((length, channels), BF16)] * 2,
        scratch_shapes=[
            pltpu.VMEM((4 * nstate, channels), BF16),
            pltpu.VMEM((length + EDGE, 256), F32),
            pltpu.VMEM((length + EDGE, 256), F32),
        ],
        compiler_params=params(),
        cost_estimate=cost(10**8, 2**22),
    )(*entries, *[a for group in locals_ for a in group], in_t, out_t, before, after, conv_weight)


def solution(mesh):
    rows = P(("groups", "inner", "outer"), None)
    flat = P(("groups", "inner", "outer"))
    return jax.shard_map(
        functools.partial(on_device, outer=mesh.shape["outer"], inner=mesh.shape["inner"]),
        mesh=mesh,
        in_specs=(rows, rows, rows, rows, P(), P(), P(), P(), flat, flat),
        out_specs=(rows, rows),
        check_vma=False,
    )
```

```python
import functools

import jax
import jax.numpy as jnp
from jax import lax
from jax.experimental import pallas as pl
from jax.experimental.pallas import tpu as pltpu
from jax.sharding import PartitionSpec as P

F32, BF16 = jnp.float32, jnp.bfloat16
EXACT = lax.Precision.HIGHEST
EDGE = 8
VMEM = 14 * 2**20
NEVER = -1e4


def mm(a, b, precision=None):
    return lax.dot_general(
        a, b, (((1,), (0,)), ((), ())), precision=precision, preferred_element_type=F32
    )


def mm_tn(a, b, precision=None):
    return lax.dot_general(
        a, b, (((0,), (0,)), ((), ())), precision=precision, preferred_element_type=F32
    )


def mm_nt(a, b, precision=None):
    return lax.dot_general(
        a, b, (((1,), (1,)), ((), ())), precision=precision, preferred_element_type=F32
    )


def iota(shape, dim):
    return lax.broadcasted_iota(jnp.int32, shape, dim)


def twice(heads):
    col = iota((heads, 2 * heads), 1)
    col = jnp.where(col < heads, col, col - heads)
    return (iota((heads, 2 * heads), 0) == col).astype(F32)


def spread(heads, lanes, hdim, start=0):
    row = iota((2 * heads, lanes), 0)
    row = jnp.where(row < heads, row, row - heads)
    low = row * hdim
    col = iota((2 * heads, lanes), 1) + start
    return ((col >= low) & (col < low + hdim)).astype(BF16)


def high_low(x):
    high = x.astype(BF16).astype(F32)
    return jnp.where(iota(x.shape, 1) < x.shape[1] // 2, high, x - high).astype(BF16)


def three(x):
    high = x.astype(BF16)
    rest = x - high.astype(F32)
    mid = rest.astype(BF16)
    return jnp.concatenate([high, mid, (rest - mid.astype(F32)).astype(BF16)], axis=0)


def one_hot(column, size):
    return (column == iota((column.shape[0], size), 1).astype(column.dtype)).astype(F32)


def edges_kernel(sig, cot, in_t, out_t, bucket, segment, near, next_):
    length = bucket.shape[1]
    channels = sig.shape[1]

    bcol = jnp.transpose(jnp.broadcast_to(bucket[...].astype(F32), (length, length)))
    scol = jnp.transpose(jnp.broadcast_to(segment[...].astype(F32), (length, length)))
    j, t = iota((EDGE, length), 0), iota((EDGE, length), 1)
    even = lax.axis_index("outer") % 2 == 0

    def ends(place, value):
        final, first = value(length - EDGE), value(0)
        here = jnp.full(final.shape, even)
        columns = slice(place, place + final.shape[1])
        near[:, columns] = jnp.where(here, final, first).astype(BF16)
        next_[:, columns] = jnp.where(here, first, final).astype(BF16)

    def rows_of(ref):
        def get(row):
            start = row // 16 * 16
            return ref[start : start + 16].astype(F32)[row - start : row - start + EDGE]

        return get

    for k, ref in enumerate((sig, cot)):
        ends(k * channels, rows_of(ref))
    for k, ref in enumerate((in_t, out_t)):
        ends(2 * channels + 128 * k, lambda row: mm_nt((t == j + row).astype(BF16), ref[...]))
    for k, full in enumerate((bcol, scol)):
        ends(2 * channels + 256 + 128 * k, lambda row: full[row : row + EDGE, :128])


def neighbours(near, next_):
    a, b = near[...].astype(F32), next_[...].astype(F32)
    even = jnp.full(a.shape, lax.axis_index("outer") % 2 == 0)
    return jnp.where(even, b, a), jnp.where(even, a, b)


def edge_parts(x, channels, state):
    return (
        x[:, :channels].astype(F32),
        x[:, channels : 2 * channels].astype(F32),
        x[:, 2 * channels : 2 * channels + state].astype(F32),
        x[:, 2 * channels + 128 : 2 * channels + 128 + state].astype(F32),
        x[:, 2 * channels + 256 : 2 * channels + 257].astype(F32),
        x[:, 2 * channels + 384 : 2 * channels + 385].astype(F32),
    )


def conv(ext, start, rows, weight, bias, sl, step):
    total = bias
    for lag in range(weight.shape[0]):
        at = start + step * lag
        total = total + weight[lag : lag + 1, sl] * ext[at : at + rows, sl]
    return total


def begin_kernel(*refs, outer, steps):
    bucket_h, segment_h, table_h, cw_h, cb_h, in_h, out_h, sig_h, cot_h = refs[:9]
    count = len(steps)
    outs = refs[9 : 9 + count]
    sums, sums_t = refs[9 + count : 11 + count]
    bucket, segment, table, cw, cb, in_t, out_t, sig, cot, ext, sems = refs[11 + count :]
    near = (bucket, segment, table, cw, cb, in_t, out_t)
    me = lax.axis_index("outer")
    length = segment.shape[1]
    heads = table.shape[2]
    rows = table.shape[1]
    nstate = in_t.shape[0]
    width = sig.shape[2]
    channels = width * outer
    hdim = channels // heads
    margin = cw.shape[1] - 1
    starts = [pl.multiple_of((me ^ r) * width, 128) for r in steps]
    small_in = [
        pltpu.make_async_copy(a, b, sems.at[k]) for k, (a, b) in enumerate(zip(refs[:7], near))
    ]
    large_in = []
    for k, start in enumerate(starts):
        for n, (a, b) in enumerate(((sig_h, sig), (cot_h, cot))):
            large_in.append(
                pltpu.make_async_copy(
                    a.at[:, pl.ds(start, width)], b.at[k], sems.at[7 + 2 * k + n]
                )
            )
    for copy in small_in + large_in:
        copy.start()
    for copy in small_in[:3]:
        copy.wait()
    last, tail = length - 1, length - margin
    hot = (bucket[...] == iota((rows, length), 0)).astype(BF16)
    hot = jnp.concatenate([hot, hot, hot], axis=0)
    row, col = iota((length, length), 0), iota((length, length), 1)
    counts = mm_nt((row >= col).astype(BF16), hot).astype(BF16)
    parts_f, parts_r = three(table[0]), three(table[1])
    dup = twice(heads).astype(BF16)
    cf = mm(counts, mm(parts_f, dup).astype(BF16))
    ci = mm(counts, mm(parts_r, dup).astype(BF16))
    lanes4 = 8 * heads
    kind = iota((heads, lanes4), 1) // (2 * heads)
    same_head = iota((heads, lanes4), 0) == iota((heads, lanes4), 1) % heads
    sign = jnp.where(kind < 2, -1.0, 1.0)
    pick_f = jnp.where(same_head & ((kind == 0) | (kind == 3)), sign, 0.0).astype(BF16)
    pick_r = jnp.where(same_head & ((kind == 1) | (kind == 2)), sign, 0.0).astype(BF16)
    quad = mm(counts, (mm(parts_f, pick_f) + mm(parts_r, pick_r)).astype(BF16))
    t, kind = iota((length, lanes4), 0), iota((length, lanes4), 1) // (2 * heads)
    reverse = (kind == 1) | (kind == 2)
    before = jnp.where(t == 0, 0.0, pltpu.roll(quad, 1, 0))
    quad = jnp.where(reverse, before, quad)
    cr = jnp.where(iota(ci.shape, 0) == 0, 0.0, pltpu.roll(ci, 1, 0))
    sums[0], sums[1], sums[2] = cf, cr, ci
    counts_t = mm(hot, (row <= col).astype(BF16))
    sums_t[0:heads] = mm_tn(parts_f, counts_t.astype(BF16))
    sums_t[heads : 2 * heads] = mm_tn(parts_r, (counts_t - hot.astype(F32)).astype(BF16))
    seg = segment[...].astype(F32)
    seg_full = jnp.transpose(jnp.broadcast_to(seg, (length, length)))
    seg_col = seg_full[:, : 2 * heads]

    def at(place):
        return seg[:, place : place + 1]

    def by_kind(a, b, c, d, like):
        k = kind[: like.shape[0]] if like.shape[0] > 1 else kind[0:1]
        return jnp.where(k == 0, a, jnp.where(k == 1, b, jnp.where(k == 2, c, d)))

    line = quad[0:1]
    anchor = by_kind(quad[last:], quad[tail : tail + 1], line, quad[margin - 1 : margin], line)
    owner = by_kind(at(last), at(tail - 1), at(0), at(margin), line)
    first, end = jnp.where(reverse, 0, margin), jnp.where(reverse, tail, length)
    inside = (t >= first) & (t < end) & (seg_full[:, :lanes4] == owner)
    fades = jnp.where(inside, jnp.exp(quad - anchor), 0.0)
    high = fades.astype(BF16).astype(F32)
    upper_half = iota(fades.shape, 1) % (2 * heads) < heads
    fades = jnp.where(upper_half, high, fades - high).astype(BF16)
    total_f, total_r = cf[last:], ci[last:]
    j = iota((EDGE, 2 * heads), 0)
    early, late = j < margin, j >= EDGE - margin
    at_tail = cr[tail : tail + 1]
    logs = (
        total_f,
        at_tail,
        jnp.where(at(tail - 1) == at(last), total_r - at_tail, NEVER),
        total_r,
        total_f - cf[margin - 1 : margin],
        jnp.where(at(0) == at(margin), cf[margin - 1 : margin], NEVER),
    )
    keeps = jnp.zeros((EDGE, 2 * heads), F32)
    for k, value in enumerate(logs):
        keeps = jnp.where(j == k, value, keeps)
    cf_0, cr_l = cf[0:EDGE], cr[length - EDGE :]
    seg_0, seg_l = seg_col[0:EDGE], seg_col[length - EDGE :]
    act_fade = jnp.where(
        early & (seg_0 == at(last)),
        jnp.exp(total_f - cf_0),
        jnp.where(late & (seg_l == at(0)), jnp.exp(cr_l), 0.0),
    )
    cot_fade = jnp.where(
        early & (seg_0 == at(0)),
        jnp.exp(cf_0),
        jnp.where(late & (seg_l == at(last)), jnp.exp(total_r - cr_l), 0.0),
    )
    small = high_low(jnp.concatenate([keeps, act_fade, cot_fade], axis=0))
    for copy in small_in[3:]:
        copy.wait()
    keys, queries = in_t[...], out_t[...]
    k, s = iota((EDGE, length), 0), iota((EDGE, length), 1)
    lines = jnp.concatenate([keys, keys, queries, queries], axis=0)
    firsts = mm_nt(((k < margin) & (s == k)).astype(BF16), lines)
    finals = mm_nt(((k >= EDGE - margin) & (s == k + length - EDGE)).astype(BF16), lines)
    group = iota(firsts.shape, 1) // nstate
    coeff = jnp.where(group % 2 == 0, firsts, finals)
    coeff = jnp.where(
        k == 3,
        jnp.where(
            group == 0,
            at(0),
            jnp.where(group == 1, at(margin), jnp.where(group == 2, at(tail - 1), at(last))),
        ),
        coeff,
    )
    if width > coeff.shape[1]:
        coeff = jnp.concatenate(
            [coeff, jnp.zeros((EDGE, width - coeff.shape[1]), F32)], axis=1
        )
    ext[0:EDGE] = jnp.zeros((EDGE, width), F32)
    ext[EDGE + length :] = jnp.zeros((EDGE, width), F32)
    row = iota((EDGE, width), 0)
    base = 4 * nstate
    for n, start in enumerate(starts):
        lanes = pl.ds(start, width)
        widen = spread(heads, width, hdim, start)
        none = jnp.zeros_like(widen)
        factor = [
            mm(fades, jnp.concatenate([none] * k + [widen] + [none] * (3 - k), axis=0))
            for k in range(4)
        ]
        large_in[2 * n].wait()
        ext[EDGE : EDGE + length] = sig[n].astype(F32)
        for side in range(2):
            pre = cb[side : side + 1, lanes]
            for lag in range(margin + 1):
                first = EDGE + (lag if side else -lag)
                pre = pre + cw[side, lag : lag + 1, lanes] * ext[first : first + length]
            act = pre * jax.nn.sigmoid(pre)
            value = (act * factor[2 * side]).astype(BF16)
            to = 2 * side * nstate
            outs[n][to : to + nstate] = mm(keys, value).astype(BF16)
        large_in[2 * n + 1].wait()
        ct = cot[n].astype(F32)
        for side in range(2):
            value = (ct * factor[2 * side + 1]).astype(BF16)
            to = (2 * side + 1) * nstate
            outs[n][to : to + nstate] = mm(queries, value).astype(BF16)
        e = mm(small, widen)

        def tile(ref):
            top = ref[n, 0:16].astype(F32)[0:EDGE]
            return jnp.where(row < 4, top, ref[n, length - 16 :].astype(F32)[EDGE:])

        def spare(rows, first):
            filled = jnp.where(row == 3, e[first : first + 1], rows)
            return jnp.where(row == 4, e[first + 1 : first + 2], filled)

        outs[n][base : base + 16] = jnp.concatenate(
            [spare(tile(sig), 0), spare(e[EDGE : 2 * EDGE], 2)], axis=0
        ).astype(BF16)
        outs[n][base + 16 : base + 32] = jnp.concatenate(
            [spare(tile(cot) * e[2 * EDGE :], 4), coeff], axis=0
        ).astype(BF16)


def edge_sums(before, after, table, channels, state, heads, margin):
    dup = twice(heads)
    table_f = mm(table[0], dup, EXACT)
    table_r = mm(table[1], dup, EXACT)
    bs, bc, bi, bo, bb, bseg = edge_parts(before, channels, state)
    as_, ac, ai, ao, ab, aseg = edge_parts(after, channels, state)
    tri = (iota((EDGE, EDGE), 0) >= iota((EDGE, EDGE), 1)).astype(F32)
    rev = (iota((EDGE, EDGE), 0) <= iota((EDGE, EDGE), 1)).astype(F32)
    rows = table.shape[1]
    nf = mm(mm(tri, one_hot(ab, rows)), table_f, EXACT)
    pr = mm(mm(rev, one_hot(bb, rows)), table_r, EXACT)
    return (bs, bc, bi, bo, bseg), (as_, ac, ai, ao, aseg), nf, pr


class Block:
    def __init__(self, ref, nstate):
        x = ref.astype(F32)
        h = 4 * nstate
        self.f, self.br = x[0:nstate], x[nstate : 2 * nstate]
        self.r, self.bf = x[2 * nstate : 3 * nstate], x[3 * nstate : h]
        self.sig, self.fade = x[h : h + 8], x[h + 8 : h + 16]
        self.cot, self.coeff = x[h + 16 : h + 24], x[h + 24 : h + 32]
        self.keep_f, self.near_br = self.sig[3:4], self.sig[4:5]
        self.far_br, self.keep_r = self.fade[3:4], self.fade[4:5]
        self.near_bf, self.far_bf = self.cot[3:4], self.cot[4:5]
        self.seg_first, self.seg_early = self.coeff[3:4, 0:1], self.coeff[3:4, nstate : nstate + 1]
        self.seg_late = self.coeff[3:4, 2 * nstate : 2 * nstate + 1]
        self.seg_last = self.coeff[3:4, 3 * nstate : 3 * nstate + 1]


def alike(a, b):
    return jnp.where(a == b, 0.0, NEVER)


def act_rows(before, here, after, cw, cb, lanes):
    row = iota(here.shape, 0)
    pre_f = cb[0:1, lanes] + cw[0, 0:1, lanes] * here
    pre_r = cb[1:2, lanes] + cw[1, 0:1, lanes] * here
    for lag in range(1, cw.shape[1]):
        moved = pltpu.roll(jnp.where(row >= EDGE - lag, before, here), lag, 0)
        pre_f += cw[0, lag : lag + 1, lanes] * moved
        moved = pltpu.roll(jnp.where(row < lag, after, here), EDGE - lag, 0)
        pre_r += cw[1, lag : lag + 1, lanes] * moved
    pre = jnp.where(row < 4, pre_f, pre_r)
    return pre * jax.nn.sigmoid(pre)


def edge_states(act, fade, cot, coeff, nstate):
    coeff = coeff.astype(BF16)
    row = iota(cot.shape, 0)
    edge = (row < 3) | (row > 4)
    a = mm_tn(coeff[:, : 2 * nstate], jnp.where(edge, act * fade, 0.0).astype(BF16))
    b = mm_tn(coeff[:, 2 * nstate : 4 * nstate], jnp.where(edge, cot, 0.0).astype(BF16))
    return a[:nstate], a[nstate:], b[:nstate], b[nstate:]


def totals_kernel(*refs, outer, inner, nstate):
    blocks, (cw, cb), outs, held = refs[:outer], refs[outer : outer + 2], refs[outer + 2 : -1], refs[-1]
    me = lax.axis_index("outer")
    place = lax.axis_index("inner")
    width = blocks[0].shape[1]
    lanes = pl.ds(pl.multiple_of(me * width, 128), width)
    for r in range(outer):
        held[me ^ r] = blocks[r][...]
    b = [Block(held[k], nstate) for k in range(outer)]
    none = jnp.zeros((EDGE, width), F32)
    low = []
    for k in range(outer):
        before = b[k - 1].sig if k else none
        after = b[k + 1].sig if k < outer - 1 else none
        act = act_rows(before, b[k].sig, after, cw, cb, lanes)
        low.append(edge_states(act, b[k].fade, b[k].cot, b[k].coeff, nstate))
    end = outer - 1
    f, x = b[0].f, b[0].br
    keep_f, keep_br = jnp.zeros((1, width), F32), b[0].near_br
    for k in range(1, outer):
        y = low[k - 1][3] + jnp.exp(b[k - 1].far_br) * x
        factor = b[k].near_br + alike(b[k - 1].seg_last, b[k].seg_late)
        x = b[k].br + jnp.exp(factor) * y
        keep_br = keep_br + b[k - 1].far_br + factor
        factor = b[k].keep_f + alike(b[k - 1].seg_last, b[k].seg_last)
        f = b[k].f + low[k][0] + jnp.exp(factor) * f
        keep_f = keep_f + factor
    r, z = b[end].r, b[end].bf
    keep_r, keep_bf = jnp.zeros((1, width), F32), b[end].near_bf
    for k in range(end - 1, -1, -1):
        y = low[k + 1][2] + jnp.exp(b[k + 1].far_bf) * z
        factor = b[k].near_bf + alike(b[k + 1].seg_first, b[k].seg_early)
        z = b[k].bf + jnp.exp(factor) * y
        keep_bf = keep_bf + b[k + 1].far_bf + factor
        factor = b[k].keep_r + alike(b[k + 1].seg_first, b[k].seg_first)
        r = b[k].r + low[k][1] + jnp.exp(factor) * r
        keep_r = keep_r + factor
    row = iota((EDGE, width), 0)
    half = row < 4

    def spare(rows, first, second):
        return jnp.where(row == 3, first, jnp.where(row == 4, second, rows))

    def named(rows, *values):
        group = iota(rows.shape, 1) // nstate
        for k, value in enumerate(values):
            rows = jnp.where((row == 3) & (group == k), value, rows)
        return rows

    sig = jnp.where(half, b[0].sig, b[end].sig)
    coeff = jnp.where(half, b[0].coeff, b[end].coeff)
    up = jnp.concatenate(
        [
            f,
            x,
            spare(sig, keep_f, b[0].keep_f),
            named(coeff, b[0].seg_last, b[0].seg_late, b[end].seg_last),
            spare(jnp.where(half, b[0].fade, b[end].cot), keep_br, b[end].far_br),
        ],
        axis=0,
    )
    down = jnp.concatenate(
        [
            r,
            z,
            spare(sig, keep_r, b[end].keep_r),
            named(coeff, b[end].seg_first, b[end].seg_early, b[0].seg_first),
            spare(jnp.where(half, b[0].cot, b[end].fade), keep_bf, b[0].far_bf),
        ],
        axis=0,
    )
    for r in range(1, inner):
        towards = jnp.full(up.shape, place ^ r, jnp.int32) > place
        outs[r - 1][...] = jnp.where(towards, up, down).astype(BF16)


def entries_kernel(*refs, outer, inner, nstate):
    blocks = refs[:outer]
    others = refs[outer : outer + inner - 1]
    cw, cb = refs[outer + inner - 1 : outer + inner + 1]
    outs = refs[outer + inner + 1 : -3]
    held, far, entry = refs[-3:]
    me = lax.axis_index("outer")
    place = lax.axis_index("inner")
    width = blocks[0].shape[1]
    lanes = pl.ds(pl.multiple_of(me * width, 128), width)
    for r in range(outer):
        held[me ^ r] = blocks[r][...]
    n, h = nstate, 2 * nstate
    far[place] = jnp.zeros(far.shape[1:], F32)
    for r in range(1, inner):
        far[place ^ r] = others[r - 1][...].astype(F32)
    zero = jnp.zeros((n, width), F32)
    none = jnp.zeros((EDGE, width), F32)
    line = jnp.zeros((1, 1), F32)

    def step(carry, index, wanted, upward):
        state, x, y, edge, seg = carry
        p = far[index]
        sig, coeff, rows = (p[h + k : h + k + EDGE] for k in (0, EDGE, 2 * EDGE))
        segs = [coeff[3:4, k * n : k * n + 1] for k in range(3)]
        if upward:
            act = act_rows(edge, sig, none, cw, cb, lanes)
            first, _, _, second = edge_states(act, rows, rows, coeff, n)
        else:
            act = act_rows(none, sig, edge, cw, cb, lanes)
            _, first, second, _ = edge_states(act, rows, rows, coeff, n)
        inside = jnp.exp(sig[4:5] + alike(seg, segs[0]))
        new = p[0:n] + jnp.exp(sig[3:4]) * (first + inside * state)
        new_x = p[n:h] + jnp.exp(rows[3:4] + alike(seg, segs[1])) * y
        new_y = second + jnp.exp(rows[4:5]) * new_x
        return tuple(
            jnp.where(jnp.full(b.shape, wanted), b, a)
            for a, b in zip(carry, (new, new_x, new_y, sig, segs[2]))
        )

    up = down = (zero, zero, zero, none, line)
    for k in range(inner - 1):
        up = step(up, k, k < place, True)
        back = inner - 1 - k
        down = step(down, back, back > place, False)
    f, x, y, edge_up, seg_up = up
    r, z, w, edge_down, seg_down = down
    b = [Block(held[k], nstate) for k in range(outer)]
    low = []
    for k in range(outer):
        before = b[k - 1].sig if k else edge_up
        after = b[k + 1].sig if k < outer - 1 else edge_down
        act = act_rows(before, b[k].sig, after, cw, cb, lanes)
        low.append(edge_states(act, b[k].fade, b[k].cot, b[k].coeff, nstate))
    for k in range(outer):
        entry[k, 0:h] = jnp.concatenate([f, x], axis=0).astype(BF16)
        if k == outer - 1:
            break
        before = b[k - 1].seg_last if k else seg_up
        f = b[k].f + low[k][0] + jnp.exp(b[k].keep_f + alike(before, b[k].seg_last)) * f
        x = b[k].br + jnp.exp(b[k].near_br + alike(before, b[k].seg_late)) * y
        y = low[k][3] + jnp.exp(b[k].far_br) * x
    for k in range(outer - 1, -1, -1):
        entry[k, h : 2 * h] = jnp.concatenate([r, z], axis=0).astype(BF16)
        if k == 0:
            break
        after = b[k + 1].seg_first if k < outer - 1 else seg_down
        r = b[k].r + low[k][1] + jnp.exp(b[k].keep_r + alike(after, b[k].seg_first)) * r
        z = b[k].bf + jnp.exp(b[k].near_bf + alike(after, b[k].seg_early)) * w
        w = low[k][2] + jnp.exp(b[k].far_bf) * z
    for r_ in range(outer):
        outs[r_][...] = entry[me ^ r_]


def weights_kernel(in_, out, segment, skip, sums, sums_t, weights, skips):
    length = segment.shape[1]
    heads = skip.shape[1]
    channels = skips.shape[1]
    seg = segment[...].astype(F32)
    same = jnp.transpose(jnp.broadcast_to(seg, (length, length))) == seg
    score = mm_tn(out[...], in_[...])
    t, s = iota((length, length), 0), iota((length, length), 1)
    score_f = jnp.where(same & (t >= s), score, 0.0)
    score_r = jnp.where(same & (t <= s), score, 0.0)
    lower = t >= s
    cf, cr = sums[0], sums[1]
    for h in range(heads):
        up = cf[:, h : h + 1] - sums_t[h : h + 1]
        down = sums_t[heads + h : heads + h + 1] - cr[:, h : h + 1]
        x = jnp.exp(jnp.minimum(jnp.where(lower, up, down), 0.0))
        weights[h, :, 0:length] = (x * score_f).astype(BF16)
        weights[h, :, length:] = (x * score_r).astype(BF16)
    wide = spread(heads, channels, channels // heads)[0:heads].astype(F32)
    skips[...] = mm(skip[...], wide, EXACT)


def local_kernel(
    sig, cot, in_, out, segment, cw, cb, table, sums, weights, skips, before, after,
    mixed, base_f, gate_f, base_r, gate_r, out_f, out_r, low, ext, widen,
    *, part, parts,
):
    length, channels = sig.shape
    heads = table.shape[2]
    nstate = in_.shape[0]
    hdim = channels // heads
    margin = cw.shape[1] - 1
    prev, nxt, nf, pr = edge_sums(*neighbours(before, after), table, channels, nstate, heads, margin)
    bs, bc, bi, bo, bseg = prev
    as_, ac, ai, ao, aseg = nxt
    seg = segment[...].astype(F32)
    col_full = jnp.transpose(jnp.broadcast_to(seg, (length, length)))
    col = col_full[:, : 2 * heads]
    cf, cr = sums[0], sums[1]
    total_f = cf[length - 1 : length]
    total_r = sums[2, length - EDGE :][EDGE - 1 : EDGE]
    j = iota((EDGE, 2 * heads), 0)
    early = j < margin
    late = j >= EDGE - margin
    s_first, s_last = aseg[0:1], bseg[EDGE - 1 : EDGE]
    s_beyond, s_ahead = aseg[margin : margin + 1], bseg[EDGE - margin - 1 : EDGE - margin]
    stack = [
        jnp.where(col == s_last, jnp.exp(cf), 0.0),
        jnp.where(col == s_first, jnp.exp(total_r - cr), 0.0),
        jnp.where(col == s_first, jnp.exp(total_f - cf), 0.0),
        jnp.where(col == s_last, jnp.exp(cr), 0.0),
        jnp.where(early & (aseg == s_beyond), jnp.exp(nf[margin - 1 : margin] - nf), 0.0),
        jnp.where(
            late & (bseg == s_ahead), jnp.exp(pr[EDGE - margin : EDGE - margin + 1] - pr), 0.0
        ),
        jnp.where(early & (aseg == s_first), jnp.exp(nf), 0.0),
        jnp.where(late & (bseg == s_last), jnp.exp(pr), 0.0),
        jnp.where(
            j < 4,
            jnp.where(s_first == s_beyond, jnp.exp(nf[margin - 1 : margin]), 0.0),
            jnp.where(s_last == s_ahead, jnp.exp(pr[EDGE - margin : EDGE - margin + 1]), 0.0),
        ),
    ]
    turned = []
    for d in range(margin):
        move = (EDGE - d) % EDGE
        later = pltpu.roll(nf, move, 0) if d else nf
        seg_j = jnp.broadcast_to(aseg, (EDGE, 2 * heads))
        seg_l = pltpu.roll(seg_j, move, 0) if d else seg_j
        ao_d = pltpu.roll(ao, move, 0) if d else ao
        dot = jnp.sum(ai * ao_d, axis=1, keepdims=True)
        stack.append(jnp.where((j + d < margin) & (seg_j == seg_l), jnp.exp(later - nf) * dot, 0.0))
        former = pltpu.roll(pr, d, 0) if d else pr
        seg_j = jnp.broadcast_to(bseg, (EDGE, 2 * heads))
        seg_l = pltpu.roll(seg_j, d, 0) if d else seg_j
        bo_d = pltpu.roll(bo, d, 0) if d else bo
        dot = jnp.sum(bi * bo_d, axis=1, keepdims=True)
        stack.append(
            jnp.where((j - d >= EDGE - margin) & (seg_j == seg_l), jnp.exp(former - pr) * dot, 0.0)
        )
    stack = high_low(jnp.concatenate(stack, axis=0))
    ext[0:EDGE] = bs
    ext[EDGE : EDGE + length] = sig[...].astype(F32)
    ext[EDGE + length :] = as_
    width = channels // parts
    start = part * width
    widen[...] = spread(heads, channels, hdim)
    wide = 128
    first = iota((length, wide), 1) < hdim
    ao_b, bo_b = ao.astype(BF16), bo.astype(BF16)
    for c in range(0, width, wide):
        sl = slice(start + c, start + c + wide)
        to = slice(c, c + wide)
        e = mm(stack, widen[:, sl])
        skip_f, skip_r = skips[0:1, sl], skips[1:2, sl]
        pre = conv(ext, EDGE, length + EDGE, cw[0], cb[0:1, sl], sl, -1)
        sg = jax.nn.sigmoid(pre)
        act_f = (pre * sg)[0:length]
        slope_f = sg * (1.0 + pre * (1.0 - sg))
        pre = conv(ext, 0, length + EDGE, cw[1], cb[1:2, sl], sl, 1)
        sg = jax.nn.sigmoid(pre)
        act_r = (pre * sg)[EDGE:]
        slope_r = sg * (1.0 + pre * (1.0 - sg))
        act = jnp.concatenate([act_f.astype(BF16), act_r.astype(BF16)], axis=0)
        ct16 = cot[:, sl]
        ct = ct16.astype(F32)
        forth, back = [], []
        for k in range(wide // hdim):
            h = (start + c) // hdim + k
            m = weights[h]
            forth.append(mm(m, act))
            back.append(mm_tn(m, ct16))
        mixed[:, to] = jnp.where(first, forth[0], forth[1]) + skip_f * act_f + skip_r * act_r
        here_f = jnp.where(first, back[0][0:length], back[1][0:length]) + skip_f * ct
        here_r = jnp.where(first, back[0][length:], back[1][length:]) + skip_r * ct
        at = 4 * length
        ac_c, bc_c = ac[:, sl], bc[:, sl]
        row = iota((EDGE, wide), 0)
        beyond = jnp.where(row < margin, skip_f * ac_c, 0.0)
        ahead = jnp.where(row >= EDGE - margin, skip_r * bc_c, 0.0)
        for d in range(margin):
            k = at + (5 + 2 * d) * EDGE
            moved = pltpu.roll(ac_c, (EDGE - d) % EDGE, 0) if d else ac_c
            beyond += e[k : k + EDGE] * moved
            moved = pltpu.roll(bc_c, d, 0) if d else bc_c
            ahead += e[k + EDGE : k + 2 * EDGE] * moved
        out_f[:, to] = e[0:length]
        out_r[:, to] = e[length : 2 * length]
        base_f[0:length, to] = here_f * slope_f[0:length]
        base_f[length:, to] = beyond * slope_f[length:]
        gate_f[0:length, to] = e[2 * length : 3 * length] * slope_f[0:length]
        gate_f[length:, to] = e[at : at + EDGE] * slope_f[length:]
        base_r[EDGE:, to] = here_r * slope_r[EDGE:]
        base_r[0:EDGE, to] = ahead * slope_r[0:EDGE]
        gate_r[EDGE:, to] = e[3 * length : 4 * length] * slope_r[EDGE:]
        gate_r[0:EDGE, to] = e[at + EDGE : at + 2 * EDGE] * slope_r[0:EDGE]
        low[0:nstate, to] = mm_tn(ao_b, (ac_c * e[at + 2 * EDGE : at + 3 * EDGE]).astype(BF16))
        low[nstate : 2 * nstate, to] = mm_tn(
            bo_b, (bc_c * e[at + 3 * EDGE : at + 4 * EDGE]).astype(BF16)
        )
        low[2 * nstate :, to] = e[at + 4 * EDGE : at + 5 * EDGE]


def finish_kernel(*refs, outer, parts):
    entries = refs[:outer]
    locals_ = [refs[outer + 8 * p : outer + 8 * (p + 1)] for p in range(parts)]
    in_, out, before, after, cw, mixed, grad, state, df, dr = refs[outer + 8 * parts :]
    length, channels = mixed.shape
    nstate = in_.shape[0]
    me = lax.axis_index("outer")
    width = channels // outer
    for r in range(outer):
        state[:, pl.ds(pl.multiple_of((me ^ r) * width, 128), width)] = entries[r][...]
    per = channels // parts
    query, key = out[...], in_[...]
    at = 2 * channels
    ahead, beyond = neighbours(before.at[:, at : at + 128], after.at[:, at : at + 128])
    ahead, beyond = ahead[:, :nstate].astype(BF16), beyond[:, :nstate].astype(BF16)
    lags = cw.shape[1]
    wide = 256
    for c in range(0, channels, wide):
        p, off = divmod(c, per)
        loc, base_f, gate_f, base_r, gate_r, out_f, out_r, low = locals_[p]
        to = slice(off, off + wide)
        sl = slice(c, c + wide)
        s = state[:, sl]
        mixed[:, sl] = (
            loc[:, to]
            + out_f[:, to] * mm_tn(query, s[0:nstate])
            + out_r[:, to] * mm_tn(query, s[2 * nstate : 3 * nstate])
        ).astype(BF16)
        s_br, s_bf = s[nstate : 2 * nstate], s[3 * nstate :]
        h_f = low[0:nstate, to] + low[2 * nstate : 2 * nstate + 1, to] * s_bf.astype(F32)
        h_r = low[nstate : 2 * nstate, to] + low[2 * nstate + 4 : 2 * nstate + 5, to] * s_br.astype(F32)
        df[0:length] = base_f[0:length, to] + gate_f[0:length, to] * mm_tn(key, h_f.astype(BF16))
        df[length:] = base_f[length:, to] + gate_f[length:, to] * mm(beyond, s_bf)
        dr[EDGE:] = base_r[EDGE:, to] + gate_r[EDGE:, to] * mm_tn(key, h_r.astype(BF16))
        dr[0:EDGE] = base_r[0:EDGE, to] + gate_r[0:EDGE, to] * mm(ahead, s_br)
        total = jnp.zeros((length, wide), F32)
        for lag in range(lags):
            total += cw[0, lag : lag + 1, sl] * df[lag : lag + length]
            total += cw[1, lag : lag + 1, sl] * dr[EDGE - lag : EDGE - lag + length]
        grad[:, sl] = total.astype(BF16)


def params():
    return pltpu.CompilerParams(vmem_limit_bytes=VMEM)


def cost(flops, size):
    return pl.CostEstimate(flops=flops, bytes_accessed=size, transcendentals=0)


def on_device(
    signal, in_coeff, out_coeff, cotangent, conv_weight, conv_bias, skip_gain, decay_table,
    bucket, segment, *, outer, inner,
):
    length, channels = signal.shape
    heads = skip_gain.shape[1]
    nstate = in_coeff.shape[1]
    axes = ("inner", "outer")
    count = outer * inner
    bucket = bucket.reshape(1, length)
    segment = segment.reshape(1, length)
    sds = jax.ShapeDtypeStruct
    width = channels // outer
    pay = 4 * nstate + 4 * EDGE
    far = 2 * nstate + 3 * EDGE
    in_t, out_t = in_coeff.T, out_coeff.T
    steps = tuple(reversed(range(outer)))
    small = (bucket, segment, decay_table, conv_weight, conv_bias, in_t, out_t)
    operands = [
        pltpu.with_memory_space_constraint(a, pltpu.HBM) for a in (*small, signal, cotangent)
    ]
    *blocks, sums, sums_t = pl.pallas_call(
        functools.partial(begin_kernel, outer=outer, steps=steps),
        name="begin",
        in_specs=[pl.BlockSpec(memory_space=pltpu.HBM)] * len(operands),
        out_shape=[sds((pay, width), BF16)] * outer
        + [sds((3, length, 2 * heads), F32), sds((2 * heads, length), F32)],
        scratch_shapes=[pltpu.VMEM(a.shape, a.dtype) for a in small]
        + [pltpu.VMEM((outer, length, width), BF16)] * 2
        + [
            pltpu.VMEM((length + 2 * EDGE, width), F32),
            pltpu.SemaphoreType.DMA((len(small) + 2 * outer,)),
        ],
        compiler_params=params(),
        cost_estimate=cost(10**8, 2**20),
    )(*operands)
    blocks = blocks[::-1]

    def swap(array, axis, size, r):
        return lax.ppermute(array, axis, [(i, i ^ r) for i in range(size)])

    def exchange(arrays, axis, size):
        got = {r: swap(arrays[r], axis, size, r) for r in reversed(range(1, size))}
        return [got[r] for r in range(1, size)]

    blocks = [blocks[0], *exchange(blocks, "outer", outer)]
    line = 2 * channels + 512
    late_bucket, _ = lax.optimization_barrier((bucket, sums))
    near_rows, next_rows = pl.pallas_call(
        edges_kernel,
        name="edges",
        out_shape=[sds((EDGE, line), BF16)] * 2,
        compiler_params=params(),
        cost_estimate=cost(10**6, 2**18),
    )(signal, cotangent, in_t, out_t, late_bucket, segment)
    before = lax.ppermute(near_rows, "outer", [(i, i ^ 1) for i in range(outer)])
    weights, skips = pl.pallas_call(
        weights_kernel,
        name="weights",
        out_shape=[sds((heads, length, 2 * length), BF16), sds((2, channels), F32)],
        compiler_params=params(),
        cost_estimate=cost(10**8, 2**21),
    )(in_t, out_t, segment, skip_gain, sums, sums_t)
    blocks[0], weights = lax.optimization_barrier((blocks[0], weights))
    pairs = [(i, i + 1) for i in range(1, count - 1, 2)]
    after = lax.ppermute(next_rows, axes, pairs + [(j, i) for i, j in pairs])
    parts = 2

    def local(part):
        per = channels // parts
        both_rows = length + EDGE
        return pl.pallas_call(
            functools.partial(local_kernel, part=part, parts=parts),
            name=f"local{part}",
            out_shape=[
                sds((length, per), F32),
                sds((both_rows, per), F32),
                sds((both_rows, per), F32),
                sds((both_rows, per), F32),
                sds((both_rows, per), F32),
                sds((length, per), F32),
                sds((length, per), F32),
                sds((2 * nstate + EDGE, per), F32),
            ],
            scratch_shapes=[
                pltpu.VMEM((length + 2 * EDGE, channels), F32),
                pltpu.VMEM((2 * heads, channels), BF16),
            ],
            compiler_params=params(),
            cost_estimate=cost(4 * 10**8, 2**22),
        )(
            signal, cotangent, in_t, out_t, segment, conv_weight, conv_bias, decay_table, sums,
            weights, skips, before, after,
        )

    locals_ = [local(p) for p in range(parts)]
    totals = pl.pallas_call(
        functools.partial(totals_kernel, outer=outer, inner=inner, nstate=nstate),
        name="totals",
        out_shape=[sds((far, width), BF16)] * (inner - 1),
        scratch_shapes=[pltpu.VMEM((outer, pay, width), BF16)],
        compiler_params=params(),
        cost_estimate=cost(10**6, 2**19),
    )(*blocks, conv_weight, conv_bias)
    totals = exchange([None, *totals], "inner", inner)
    entries = pl.pallas_call(
        functools.partial(entries_kernel, outer=outer, inner=inner, nstate=nstate),
        name="entries",
        out_shape=[sds((4 * nstate, width), BF16)] * outer,
        scratch_shapes=[
            pltpu.VMEM((outer, pay, width), BF16),
            pltpu.VMEM((inner, far, width), F32),
            pltpu.VMEM((outer, 4 * nstate, width), BF16),
        ],
        compiler_params=params(),
        cost_estimate=cost(10**6, 2**19),
    )(*blocks, *totals, conv_weight, conv_bias)
    entries = [entries[0], *exchange(entries, "outer", outer)]
    return pl.pallas_call(
        functools.partial(finish_kernel, outer=outer, parts=parts),
        name="finish",
        out_shape=[sds((length, channels), BF16)] * 2,
        scratch_shapes=[
            pltpu.VMEM((4 * nstate, channels), BF16),
            pltpu.VMEM((length + EDGE, 256), F32),
            pltpu.VMEM((length + EDGE, 256), F32),
        ],
        compiler_params=params(),
        cost_estimate=cost(10**8, 2**22),
    )(*entries, *[a for group in locals_ for a in group], in_t, out_t, before, after, conv_weight)


def solution(mesh):
    rows = P(("groups", "inner", "outer"), None)
    flat = P(("groups", "inner", "outer"))
    return jax.shard_map(
        functools.partial(on_device, outer=mesh.shape["outer"], inner=mesh.shape["inner"]),
        mesh=mesh,
        in_specs=(rows, rows, rows, rows, P(), P(), P(), P(), flat, flat),
        out_specs=(rows, rows),
        check_vma=False,
    )
```

```python
import functools

import jax
import jax.numpy as jnp
from jax import lax
from jax.experimental import pallas as pl
from jax.experimental.pallas import tpu as pltpu
from jax.sharding import PartitionSpec as P

F32, BF16 = jnp.float32, jnp.bfloat16
EXACT = lax.Precision.HIGHEST
EDGE = 8
VMEM = 14 * 2**20
NEVER = -1e4
FIRST, SECOND, THIRD = (2, 1, 3), (3, 2, 1), (2, 1, 3)


def mm(a, b, precision=None):
    return lax.dot_general(
        a, b, (((1,), (0,)), ((), ())), precision=precision, preferred_element_type=F32
    )


def mm_tn(a, b, precision=None):
    return lax.dot_general(
        a, b, (((0,), (0,)), ((), ())), precision=precision, preferred_element_type=F32
    )


def mm_nt(a, b, precision=None):
    return lax.dot_general(
        a, b, (((1,), (1,)), ((), ())), precision=precision, preferred_element_type=F32
    )


def iota(shape, dim):
    return lax.broadcasted_iota(jnp.int32, shape, dim)


def twice(heads):
    col = iota((heads, 2 * heads), 1)
    col = jnp.where(col < heads, col, col - heads)
    return (iota((heads, 2 * heads), 0) == col).astype(F32)


def spread(heads, lanes, hdim, start=0):
    row = iota((2 * heads, lanes), 0)
    row = jnp.where(row < heads, row, row - heads)
    low = row * hdim
    col = iota((2 * heads, lanes), 1) + start
    return ((col >= low) & (col < low + hdim)).astype(BF16)


def high_low(x):
    high = x.astype(BF16).astype(F32)
    return jnp.where(iota(x.shape, 1) < x.shape[1] // 2, high, x - high).astype(BF16)


def three(x):
    high = x.astype(BF16)
    rest = x - high.astype(F32)
    mid = rest.astype(BF16)
    return jnp.concatenate([high, mid, (rest - mid.astype(F32)).astype(BF16)], axis=0)


def one_hot(column, size):
    return (column == iota((column.shape[0], size), 1).astype(column.dtype)).astype(F32)


def edges_kernel(sig, cot, in_t, out_t, bucket, segment, near, next_):
    length = bucket.shape[1]
    channels = sig.shape[1]

    bcol = jnp.transpose(jnp.broadcast_to(bucket[...].astype(F32), (length, length)))
    scol = jnp.transpose(jnp.broadcast_to(segment[...].astype(F32), (length, length)))
    j, t = iota((EDGE, length), 0), iota((EDGE, length), 1)
    even = lax.axis_index("outer") % 2 == 0

    def ends(place, value):
        final, first = value(length - EDGE), value(0)
        here = jnp.full(final.shape, even)
        columns = slice(place, place + final.shape[1])
        near[:, columns] = jnp.where(here, final, first).astype(BF16)
        next_[:, columns] = jnp.where(here, first, final).astype(BF16)

    def rows_of(ref):
        def get(row):
            start = row // 16 * 16
            return ref[start : start + 16].astype(F32)[row - start : row - start + EDGE]

        return get

    for k, ref in enumerate((sig, cot)):
        ends(k * channels, rows_of(ref))
    for k, ref in enumerate((in_t, out_t)):
        ends(2 * channels + 128 * k, lambda row: mm_nt((t == j + row).astype(BF16), ref[...]))
    for k, full in enumerate((bcol, scol)):
        ends(2 * channels + 256 + 128 * k, lambda row: full[row : row + EDGE, :128])


def neighbours(near, next_):
    a, b = near[...].astype(F32), next_[...].astype(F32)
    even = jnp.full(a.shape, lax.axis_index("outer") % 2 == 0)
    return jnp.where(even, b, a), jnp.where(even, a, b)


def edge_parts(x, channels, state):
    return (
        x[:, :channels].astype(F32),
        x[:, channels : 2 * channels].astype(F32),
        x[:, 2 * channels : 2 * channels + state].astype(F32),
        x[:, 2 * channels + 128 : 2 * channels + 128 + state].astype(F32),
        x[:, 2 * channels + 256 : 2 * channels + 257].astype(F32),
        x[:, 2 * channels + 384 : 2 * channels + 385].astype(F32),
    )


def conv(ext, start, rows, weight, bias, sl, step):
    total = bias
    for lag in range(weight.shape[0]):
        at = start + step * lag
        total = total + weight[lag : lag + 1, sl] * ext[at : at + rows, sl]
    return total


def begin_kernel(*refs, outer, steps):
    bucket_h, segment_h, table_h, cw_h, cb_h, in_h, out_h, sig_h, cot_h = refs[:9]
    count = len(steps)
    outs = refs[9 : 9 + count]
    sums, sums_t = refs[9 + count : 11 + count]
    bucket, segment, table, cw, cb, in_t, out_t, sig, cot, ext, sems = refs[11 + count :]
    near = (bucket, segment, table, cw, cb, in_t, out_t)
    me = lax.axis_index("outer")
    length = segment.shape[1]
    heads = table.shape[2]
    rows = table.shape[1]
    nstate = in_t.shape[0]
    width = sig.shape[2]
    channels = width * outer
    hdim = channels // heads
    margin = cw.shape[1] - 1
    starts = [pl.multiple_of((me ^ r) * width, 128) for r in steps]
    small_in = [
        pltpu.make_async_copy(a, b, sems.at[k]) for k, (a, b) in enumerate(zip(refs[:7], near))
    ]
    large_in = []
    for k, start in enumerate(starts):
        for n, (a, b) in enumerate(((sig_h, sig), (cot_h, cot))):
            large_in.append(
                pltpu.make_async_copy(
                    a.at[:, pl.ds(start, width)], b.at[k], sems.at[7 + 2 * k + n]
                )
            )
    for copy in small_in + large_in:
        copy.start()
    for copy in small_in[:3]:
        copy.wait()
    last, tail = length - 1, length - margin
    hot = (bucket[...] == iota((rows, length), 0)).astype(BF16)
    hot = jnp.concatenate([hot, hot, hot], axis=0)
    row, col = iota((length, length), 0), iota((length, length), 1)
    counts = mm_nt((row >= col).astype(BF16), hot).astype(BF16)
    parts_f, parts_r = three(table[0]), three(table[1])
    dup = twice(heads).astype(BF16)
    cf = mm(counts, mm(parts_f, dup).astype(BF16))
    ci = mm(counts, mm(parts_r, dup).astype(BF16))
    lanes4 = 8 * heads
    kind = iota((heads, lanes4), 1) // (2 * heads)
    same_head = iota((heads, lanes4), 0) == iota((heads, lanes4), 1) % heads
    sign = jnp.where(kind < 2, -1.0, 1.0)
    pick_f = jnp.where(same_head & ((kind == 0) | (kind == 3)), sign, 0.0).astype(BF16)
    pick_r = jnp.where(same_head & ((kind == 1) | (kind == 2)), sign, 0.0).astype(BF16)
    quad = mm(counts, (mm(parts_f, pick_f) + mm(parts_r, pick_r)).astype(BF16))
    t, kind = iota((length, lanes4), 0), iota((length, lanes4), 1) // (2 * heads)
    reverse = (kind == 1) | (kind == 2)
    before = jnp.where(t == 0, 0.0, pltpu.roll(quad, 1, 0))
    quad = jnp.where(reverse, before, quad)
    cr = jnp.where(iota(ci.shape, 0) == 0, 0.0, pltpu.roll(ci, 1, 0))
    sums[0], sums[1], sums[2] = cf, cr, ci
    counts_t = mm(hot, (row <= col).astype(BF16))
    sums_t[0:heads] = mm_tn(parts_f, counts_t.astype(BF16))
    sums_t[heads : 2 * heads] = mm_tn(parts_r, (counts_t - hot.astype(F32)).astype(BF16))
    seg = segment[...].astype(F32)
    seg_full = jnp.transpose(jnp.broadcast_to(seg, (length, length)))
    seg_col = seg_full[:, : 2 * heads]

    def at(place):
        return seg[:, place : place + 1]

    def by_kind(a, b, c, d, like):
        k = kind[: like.shape[0]] if like.shape[0] > 1 else kind[0:1]
        return jnp.where(k == 0, a, jnp.where(k == 1, b, jnp.where(k == 2, c, d)))

    line = quad[0:1]
    anchor = by_kind(quad[last:], quad[tail : tail + 1], line, quad[margin - 1 : margin], line)
    owner = by_kind(at(last), at(tail - 1), at(0), at(margin), line)
    first, end = jnp.where(reverse, 0, margin), jnp.where(reverse, tail, length)
    inside = (t >= first) & (t < end) & (seg_full[:, :lanes4] == owner)
    fades = jnp.where(inside, jnp.exp(quad - anchor), 0.0)
    high = fades.astype(BF16).astype(F32)
    upper_half = iota(fades.shape, 1) % (2 * heads) < heads
    fades = jnp.where(upper_half, high, fades - high).astype(BF16)
    total_f, total_r = cf[last:], ci[last:]
    j = iota((EDGE, 2 * heads), 0)
    early, late = j < margin, j >= EDGE - margin
    at_tail = cr[tail : tail + 1]
    logs = (
        total_f,
        at_tail,
        jnp.where(at(tail - 1) == at(last), total_r - at_tail, NEVER),
        total_r,
        total_f - cf[margin - 1 : margin],
        jnp.where(at(0) == at(margin), cf[margin - 1 : margin], NEVER),
    )
    keeps = jnp.zeros((EDGE, 2 * heads), F32)
    for k, value in enumerate(logs):
        keeps = jnp.where(j == k, value, keeps)
    cf_0, cr_l = cf[0:EDGE], cr[length - EDGE :]
    seg_0, seg_l = seg_col[0:EDGE], seg_col[length - EDGE :]
    act_fade = jnp.where(
        early & (seg_0 == at(last)),
        jnp.exp(total_f - cf_0),
        jnp.where(late & (seg_l == at(0)), jnp.exp(cr_l), 0.0),
    )
    cot_fade = jnp.where(
        early & (seg_0 == at(0)),
        jnp.exp(cf_0),
        jnp.where(late & (seg_l == at(last)), jnp.exp(total_r - cr_l), 0.0),
    )
    small = high_low(jnp.concatenate([keeps, act_fade, cot_fade], axis=0))
    for copy in small_in[3:]:
        copy.wait()
    keys, queries = in_t[...], out_t[...]
    k, s = iota((EDGE, length), 0), iota((EDGE, length), 1)
    lines = jnp.concatenate([keys, keys, queries, queries], axis=0)
    firsts = mm_nt(((k < margin) & (s == k)).astype(BF16), lines)
    finals = mm_nt(((k >= EDGE - margin) & (s == k + length - EDGE)).astype(BF16), lines)
    group = iota(firsts.shape, 1) // nstate
    coeff = jnp.where(group % 2 == 0, firsts, finals)
    coeff = jnp.where(
        k == 3,
        jnp.where(
            group == 0,
            at(0),
            jnp.where(group == 1, at(margin), jnp.where(group == 2, at(tail - 1), at(last))),
        ),
        coeff,
    )
    if width > coeff.shape[1]:
        coeff = jnp.concatenate(
            [coeff, jnp.zeros((EDGE, width - coeff.shape[1]), F32)], axis=1
        )
    ext[0:EDGE] = jnp.zeros((EDGE, width), F32)
    ext[EDGE + length :] = jnp.zeros((EDGE, width), F32)
    row = iota((EDGE, width), 0)
    base = 4 * nstate
    for n, start in enumerate(starts):
        lanes = pl.ds(start, width)
        widen = spread(heads, width, hdim, start)
        none = jnp.zeros_like(widen)
        factor = [
            mm(fades, jnp.concatenate([none] * k + [widen] + [none] * (3 - k), axis=0))
            for k in range(4)
        ]
        large_in[2 * n].wait()
        ext[EDGE : EDGE + length] = sig[n].astype(F32)
        for side in range(2):
            pre = cb[side : side + 1, lanes]
            for lag in range(margin + 1):
                first = EDGE + (lag if side else -lag)
                pre = pre + cw[side, lag : lag + 1, lanes] * ext[first : first + length]
            act = pre * jax.nn.sigmoid(pre)
            value = (act * factor[2 * side]).astype(BF16)
            to = 2 * side * nstate
            outs[n][to : to + nstate] = mm(keys, value).astype(BF16)
        large_in[2 * n + 1].wait()
        ct = cot[n].astype(F32)
        for side in range(2):
            value = (ct * factor[2 * side + 1]).astype(BF16)
            to = (2 * side + 1) * nstate
            outs[n][to : to + nstate] = mm(queries, value).astype(BF16)
        e = mm(small, widen)

        def tile(ref):
            top = ref[n, 0:16].astype(F32)[0:EDGE]
            return jnp.where(row < 4, top, ref[n, length - 16 :].astype(F32)[EDGE:])

        def spare(rows, first):
            filled = jnp.where(row == 3, e[first : first + 1], rows)
            return jnp.where(row == 4, e[first + 1 : first + 2], filled)

        outs[n][base : base + 16] = jnp.concatenate(
            [spare(tile(sig), 0), spare(e[EDGE : 2 * EDGE], 2)], axis=0
        ).astype(BF16)
        outs[n][base + 16 : base + 32] = jnp.concatenate(
            [spare(tile(cot) * e[2 * EDGE :], 4), coeff], axis=0
        ).astype(BF16)


def edge_sums(before, after, table, channels, state, heads, margin):
    dup = twice(heads)
    table_f = mm(table[0], dup, EXACT)
    table_r = mm(table[1], dup, EXACT)
    bs, bc, bi, bo, bb, bseg = edge_parts(before, channels, state)
    as_, ac, ai, ao, ab, aseg = edge_parts(after, channels, state)
    tri = (iota((EDGE, EDGE), 0) >= iota((EDGE, EDGE), 1)).astype(F32)
    rev = (iota((EDGE, EDGE), 0) <= iota((EDGE, EDGE), 1)).astype(F32)
    rows = table.shape[1]
    nf = mm(mm(tri, one_hot(ab, rows)), table_f, EXACT)
    pr = mm(mm(rev, one_hot(bb, rows)), table_r, EXACT)
    return (bs, bc, bi, bo, bseg), (as_, ac, ai, ao, aseg), nf, pr


class Block:
    def __init__(self, ref, nstate):
        x = ref.astype(F32)
        h = 4 * nstate
        self.f, self.br = x[0:nstate], x[nstate : 2 * nstate]
        self.r, self.bf = x[2 * nstate : 3 * nstate], x[3 * nstate : h]
        self.sig, self.fade = x[h : h + 8], x[h + 8 : h + 16]
        self.cot, self.coeff = x[h + 16 : h + 24], x[h + 24 : h + 32]
        self.keep_f, self.near_br = self.sig[3:4], self.sig[4:5]
        self.far_br, self.keep_r = self.fade[3:4], self.fade[4:5]
        self.near_bf, self.far_bf = self.cot[3:4], self.cot[4:5]
        self.seg_first, self.seg_early = self.coeff[3:4, 0:1], self.coeff[3:4, nstate : nstate + 1]
        self.seg_late = self.coeff[3:4, 2 * nstate : 2 * nstate + 1]
        self.seg_last = self.coeff[3:4, 3 * nstate : 3 * nstate + 1]


def alike(a, b):
    return jnp.where(a == b, 0.0, NEVER)


def act_rows(before, here, after, cw, cb, lanes):
    row = iota(here.shape, 0)
    pre_f = cb[0:1, lanes] + cw[0, 0:1, lanes] * here
    pre_r = cb[1:2, lanes] + cw[1, 0:1, lanes] * here
    for lag in range(1, cw.shape[1]):
        moved = pltpu.roll(jnp.where(row >= EDGE - lag, before, here), lag, 0)
        pre_f += cw[0, lag : lag + 1, lanes] * moved
        moved = pltpu.roll(jnp.where(row < lag, after, here), EDGE - lag, 0)
        pre_r += cw[1, lag : lag + 1, lanes] * moved
    pre = jnp.where(row < 4, pre_f, pre_r)
    return pre * jax.nn.sigmoid(pre)


def edge_states(act, fade, cot, coeff, nstate):
    coeff = coeff.astype(BF16)
    row = iota(cot.shape, 0)
    edge = (row < 3) | (row > 4)
    a = mm_tn(coeff[:, : 2 * nstate], jnp.where(edge, act * fade, 0.0).astype(BF16))
    b = mm_tn(coeff[:, 2 * nstate : 4 * nstate], jnp.where(edge, cot, 0.0).astype(BF16))
    return a[:nstate], a[nstate:], b[:nstate], b[nstate:]


def totals_kernel(*refs, outer, inner, nstate):
    blocks, (cw, cb), outs, held = in_order(refs[:outer], FIRST), refs[outer : outer + 2], refs[outer + 2 : -1], refs[-1]
    me = lax.axis_index("outer")
    place = lax.axis_index("inner")
    width = blocks[0].shape[1]
    lanes = pl.ds(pl.multiple_of(me * width, 128), width)
    for r in range(outer):
        held[me ^ r] = blocks[r][...]
    b = [Block(held[k], nstate) for k in range(outer)]
    none = jnp.zeros((EDGE, width), F32)
    low = []
    for k in range(outer):
        before = b[k - 1].sig if k else none
        after = b[k + 1].sig if k < outer - 1 else none
        act = act_rows(before, b[k].sig, after, cw, cb, lanes)
        low.append(edge_states(act, b[k].fade, b[k].cot, b[k].coeff, nstate))
    end = outer - 1
    f, x = b[0].f, b[0].br
    keep_f, keep_br = jnp.zeros((1, width), F32), b[0].near_br
    for k in range(1, outer):
        y = low[k - 1][3] + jnp.exp(b[k - 1].far_br) * x
        factor = b[k].near_br + alike(b[k - 1].seg_last, b[k].seg_late)
        x = b[k].br + jnp.exp(factor) * y
        keep_br = keep_br + b[k - 1].far_br + factor
        factor = b[k].keep_f + alike(b[k - 1].seg_last, b[k].seg_last)
        f = b[k].f + low[k][0] + jnp.exp(factor) * f
        keep_f = keep_f + factor
    r, z = b[end].r, b[end].bf
    keep_r, keep_bf = jnp.zeros((1, width), F32), b[end].near_bf
    for k in range(end - 1, -1, -1):
        y = low[k + 1][2] + jnp.exp(b[k + 1].far_bf) * z
        factor = b[k].near_bf + alike(b[k + 1].seg_first, b[k].seg_early)
        z = b[k].bf + jnp.exp(factor) * y
        keep_bf = keep_bf + b[k + 1].far_bf + factor
        factor = b[k].keep_r + alike(b[k + 1].seg_first, b[k].seg_first)
        r = b[k].r + low[k][1] + jnp.exp(factor) * r
        keep_r = keep_r + factor
    row = iota((EDGE, width), 0)
    half = row < 4

    def spare(rows, first, second):
        return jnp.where(row == 3, first, jnp.where(row == 4, second, rows))

    def named(rows, *values):
        group = iota(rows.shape, 1) // nstate
        for k, value in enumerate(values):
            rows = jnp.where((row == 3) & (group == k), value, rows)
        return rows

    sig = jnp.where(half, b[0].sig, b[end].sig)
    coeff = jnp.where(half, b[0].coeff, b[end].coeff)
    up = jnp.concatenate(
        [
            f,
            x,
            spare(sig, keep_f, b[0].keep_f),
            named(coeff, b[0].seg_last, b[0].seg_late, b[end].seg_last),
            spare(jnp.where(half, b[0].fade, b[end].cot), keep_br, b[end].far_br),
        ],
        axis=0,
    )
    down = jnp.concatenate(
        [
            r,
            z,
            spare(sig, keep_r, b[end].keep_r),
            named(coeff, b[end].seg_first, b[end].seg_early, b[0].seg_first),
            spare(jnp.where(half, b[0].cot, b[end].fade), keep_bf, b[0].far_bf),
        ],
        axis=0,
    )
    for r in range(1, inner):
        towards = jnp.full(up.shape, place ^ r, jnp.int32) > place
        outs[r - 1][...] = jnp.where(towards, up, down).astype(BF16)


def entries_kernel(*refs, outer, inner, nstate):
    blocks = in_order(refs[:outer], FIRST)
    others = in_order(refs[outer - 1 : outer + inner - 1], SECOND)[1:]
    cw, cb = refs[outer + inner - 1 : outer + inner + 1]
    outs = refs[outer + inner + 1 : -3]
    held, far, entry = refs[-3:]
    me = lax.axis_index("outer")
    place = lax.axis_index("inner")
    width = blocks[0].shape[1]
    lanes = pl.ds(pl.multiple_of(me * width, 128), width)
    for r in range(outer):
        held[me ^ r] = blocks[r][...]
    n, h = nstate, 2 * nstate
    far[place] = jnp.zeros(far.shape[1:], F32)
    for r in range(1, inner):
        far[place ^ r] = others[r - 1][...].astype(F32)
    zero = jnp.zeros((n, width), F32)
    none = jnp.zeros((EDGE, width), F32)
    line = jnp.zeros((1, 1), F32)

    def step(carry, index, wanted, upward):
        state, x, y, edge, seg = carry
        p = far[index]
        sig, coeff, rows = (p[h + k : h + k + EDGE] for k in (0, EDGE, 2 * EDGE))
        segs = [coeff[3:4, k * n : k * n + 1] for k in range(3)]
        if upward:
            act = act_rows(edge, sig, none, cw, cb, lanes)
            first, _, _, second = edge_states(act, rows, rows, coeff, n)
        else:
            act = act_rows(none, sig, edge, cw, cb, lanes)
            _, first, second, _ = edge_states(act, rows, rows, coeff, n)
        inside = jnp.exp(sig[4:5] + alike(seg, segs[0]))
        new = p[0:n] + jnp.exp(sig[3:4]) * (first + inside * state)
        new_x = p[n:h] + jnp.exp(rows[3:4] + alike(seg, segs[1])) * y
        new_y = second + jnp.exp(rows[4:5]) * new_x
        return tuple(
            jnp.where(jnp.full(b.shape, wanted), b, a)
            for a, b in zip(carry, (new, new_x, new_y, sig, segs[2]))
        )

    up = down = (zero, zero, zero, none, line)
    for k in range(inner - 1):
        up = step(up, k, k < place, True)
        back = inner - 1 - k
        down = step(down, back, back > place, False)
    f, x, y, edge_up, seg_up = up
    r, z, w, edge_down, seg_down = down
    b = [Block(held[k], nstate) for k in range(outer)]
    low = []
    for k in range(outer):
        before = b[k - 1].sig if k else edge_up
        after = b[k + 1].sig if k < outer - 1 else edge_down
        act = act_rows(before, b[k].sig, after, cw, cb, lanes)
        low.append(edge_states(act, b[k].fade, b[k].cot, b[k].coeff, nstate))
    for k in range(outer):
        entry[k, 0:h] = jnp.concatenate([f, x], axis=0).astype(BF16)
        if k == outer - 1:
            break
        before = b[k - 1].seg_last if k else seg_up
        f = b[k].f + low[k][0] + jnp.exp(b[k].keep_f + alike(before, b[k].seg_last)) * f
        x = b[k].br + jnp.exp(b[k].near_br + alike(before, b[k].seg_late)) * y
        y = low[k][3] + jnp.exp(b[k].far_br) * x
    for k in range(outer - 1, -1, -1):
        entry[k, h : 2 * h] = jnp.concatenate([r, z], axis=0).astype(BF16)
        if k == 0:
            break
        after = b[k + 1].seg_first if k < outer - 1 else seg_down
        r = b[k].r + low[k][1] + jnp.exp(b[k].keep_r + alike(after, b[k].seg_first)) * r
        z = b[k].bf + jnp.exp(b[k].near_bf + alike(after, b[k].seg_early)) * w
        w = low[k][2] + jnp.exp(b[k].far_bf) * z
    for r_ in range(outer):
        outs[r_][...] = entry[me ^ r_]


def weights_kernel(in_, out, segment, skip, sums, sums_t, weights, skips):
    length = segment.shape[1]
    heads = skip.shape[1]
    channels = skips.shape[1]
    seg = segment[...].astype(F32)
    same = jnp.transpose(jnp.broadcast_to(seg, (length, length))) == seg
    score = mm_tn(out[...], in_[...])
    t, s = iota((length, length), 0), iota((length, length), 1)
    score_f = jnp.where(same & (t >= s), score, 0.0)
    score_r = jnp.where(same & (t <= s), score, 0.0)
    lower = t >= s
    cf, cr = sums[0], sums[1]
    for h in range(heads):
        up = cf[:, h : h + 1] - sums_t[h : h + 1]
        down = sums_t[heads + h : heads + h + 1] - cr[:, h : h + 1]
        x = jnp.exp(jnp.minimum(jnp.where(lower, up, down), 0.0))
        weights[h, :, 0:length] = (x * score_f).astype(BF16)
        weights[h, :, length:] = (x * score_r).astype(BF16)
    wide = spread(heads, channels, channels // heads)[0:heads].astype(F32)
    skips[...] = mm(skip[...], wide, EXACT)


def local_kernel(
    sig, cot, in_, out, segment, cw, cb, table, sums, weights, skips, before, after,
    mixed, base_f, gate_f, base_r, gate_r, out_f, out_r, low, ext, widen,
    *, part, parts,
):
    length, channels = sig.shape
    heads = table.shape[2]
    nstate = in_.shape[0]
    hdim = channels // heads
    margin = cw.shape[1] - 1
    prev, nxt, nf, pr = edge_sums(*neighbours(before, after), table, channels, nstate, heads, margin)
    bs, bc, bi, bo, bseg = prev
    as_, ac, ai, ao, aseg = nxt
    seg = segment[...].astype(F32)
    col_full = jnp.transpose(jnp.broadcast_to(seg, (length, length)))
    col = col_full[:, : 2 * heads]
    cf, cr = sums[0], sums[1]
    total_f = cf[length - 1 : length]
    total_r = sums[2, length - EDGE :][EDGE - 1 : EDGE]
    j = iota((EDGE, 2 * heads), 0)
    early = j < margin
    late = j >= EDGE - margin
    s_first, s_last = aseg[0:1], bseg[EDGE - 1 : EDGE]
    s_beyond, s_ahead = aseg[margin : margin + 1], bseg[EDGE - margin - 1 : EDGE - margin]
    stack = [
        jnp.where(col == s_last, jnp.exp(cf), 0.0),
        jnp.where(col == s_first, jnp.exp(total_r - cr), 0.0),
        jnp.where(col == s_first, jnp.exp(total_f - cf), 0.0),
        jnp.where(col == s_last, jnp.exp(cr), 0.0),
        jnp.where(early & (aseg == s_beyond), jnp.exp(nf[margin - 1 : margin] - nf), 0.0),
        jnp.where(
            late & (bseg == s_ahead), jnp.exp(pr[EDGE - margin : EDGE - margin + 1] - pr), 0.0
        ),
        jnp.where(early & (aseg == s_first), jnp.exp(nf), 0.0),
        jnp.where(late & (bseg == s_last), jnp.exp(pr), 0.0),
        jnp.where(
            j < 4,
            jnp.where(s_first == s_beyond, jnp.exp(nf[margin - 1 : margin]), 0.0),
            jnp.where(s_last == s_ahead, jnp.exp(pr[EDGE - margin : EDGE - margin + 1]), 0.0),
        ),
    ]
    turned = []
    for d in range(margin):
        move = (EDGE - d) % EDGE
        later = pltpu.roll(nf, move, 0) if d else nf
        seg_j = jnp.broadcast_to(aseg, (EDGE, 2 * heads))
        seg_l = pltpu.roll(seg_j, move, 0) if d else seg_j
        ao_d = pltpu.roll(ao, move, 0) if d else ao
        dot = jnp.sum(ai * ao_d, axis=1, keepdims=True)
        stack.append(jnp.where((j + d < margin) & (seg_j == seg_l), jnp.exp(later - nf) * dot, 0.0))
        former = pltpu.roll(pr, d, 0) if d else pr
        seg_j = jnp.broadcast_to(bseg, (EDGE, 2 * heads))
        seg_l = pltpu.roll(seg_j, d, 0) if d else seg_j
        bo_d = pltpu.roll(bo, d, 0) if d else bo
        dot = jnp.sum(bi * bo_d, axis=1, keepdims=True)
        stack.append(
            jnp.where((j - d >= EDGE - margin) & (seg_j == seg_l), jnp.exp(former - pr) * dot, 0.0)
        )
    stack = high_low(jnp.concatenate(stack, axis=0))
    ext[0:EDGE] = bs
    ext[EDGE : EDGE + length] = sig[...].astype(F32)
    ext[EDGE + length :] = as_
    width = channels // parts
    start = part * width
    widen[...] = spread(heads, channels, hdim)
    wide = 128
    first = iota((length, wide), 1) < hdim
    ao_b, bo_b = ao.astype(BF16), bo.astype(BF16)
    for c in range(0, width, wide):
        sl = slice(start + c, start + c + wide)
        to = slice(c, c + wide)
        e = mm(stack, widen[:, sl])
        skip_f, skip_r = skips[0:1, sl], skips[1:2, sl]
        pre = conv(ext, EDGE, length + EDGE, cw[0], cb[0:1, sl], sl, -1)
        sg = jax.nn.sigmoid(pre)
        act_f = (pre * sg)[0:length]
        slope_f = sg * (1.0 + pre * (1.0 - sg))
        pre = conv(ext, 0, length + EDGE, cw[1], cb[1:2, sl], sl, 1)
        sg = jax.nn.sigmoid(pre)
        act_r = (pre * sg)[EDGE:]
        slope_r = sg * (1.0 + pre * (1.0 - sg))
        act = jnp.concatenate([act_f.astype(BF16), act_r.astype(BF16)], axis=0)
        ct16 = cot[:, sl]
        ct = ct16.astype(F32)
        forth, back = [], []
        for k in range(wide // hdim):
            h = (start + c) // hdim + k
            m = weights[h]
            forth.append(mm(m, act))
            back.append(mm_tn(m, ct16))
        mixed[:, to] = jnp.where(first, forth[0], forth[1]) + skip_f * act_f + skip_r * act_r
        here_f = jnp.where(first, back[0][0:length], back[1][0:length]) + skip_f * ct
        here_r = jnp.where(first, back[0][length:], back[1][length:]) + skip_r * ct
        at = 4 * length
        ac_c, bc_c = ac[:, sl], bc[:, sl]
        row = iota((EDGE, wide), 0)
        beyond = jnp.where(row < margin, skip_f * ac_c, 0.0)
        ahead = jnp.where(row >= EDGE - margin, skip_r * bc_c, 0.0)
        for d in range(margin):
            k = at + (5 + 2 * d) * EDGE
            moved = pltpu.roll(ac_c, (EDGE - d) % EDGE, 0) if d else ac_c
            beyond += e[k : k + EDGE] * moved
            moved = pltpu.roll(bc_c, d, 0) if d else bc_c
            ahead += e[k + EDGE : k + 2 * EDGE] * moved
        out_f[:, to] = e[0:length]
        out_r[:, to] = e[length : 2 * length]
        base_f[0:length, to] = here_f * slope_f[0:length]
        base_f[length:, to] = beyond * slope_f[length:]
        gate_f[0:length, to] = e[2 * length : 3 * length] * slope_f[0:length]
        gate_f[length:, to] = e[at : at + EDGE] * slope_f[length:]
        base_r[EDGE:, to] = here_r * slope_r[EDGE:]
        base_r[0:EDGE, to] = ahead * slope_r[0:EDGE]
        gate_r[EDGE:, to] = e[3 * length : 4 * length] * slope_r[EDGE:]
        gate_r[0:EDGE, to] = e[at + EDGE : at + 2 * EDGE] * slope_r[0:EDGE]
        low[0:nstate, to] = mm_tn(ao_b, (ac_c * e[at + 2 * EDGE : at + 3 * EDGE]).astype(BF16))
        low[nstate : 2 * nstate, to] = mm_tn(
            bo_b, (bc_c * e[at + 3 * EDGE : at + 4 * EDGE]).astype(BF16)
        )
        low[2 * nstate :, to] = e[at + 4 * EDGE : at + 5 * EDGE]


def finish_kernel(*refs, outer, parts):
    entries = in_order(refs[:outer], THIRD)
    locals_ = [refs[outer + 8 * p : outer + 8 * (p + 1)] for p in range(parts)]
    in_, out, before, after, cw, mixed, grad, state, df, dr = refs[outer + 8 * parts :]
    length, channels = mixed.shape
    nstate = in_.shape[0]
    me = lax.axis_index("outer")
    width = channels // outer
    for r in range(outer):
        state[:, pl.ds(pl.multiple_of((me ^ r) * width, 128), width)] = entries[r][...]
    per = channels // parts
    query, key = out[...], in_[...]
    at = 2 * channels
    ahead, beyond = neighbours(before.at[:, at : at + 128], after.at[:, at : at + 128])
    ahead, beyond = ahead[:, :nstate].astype(BF16), beyond[:, :nstate].astype(BF16)
    lags = cw.shape[1]
    wide = 256
    for c in range(0, channels, wide):
        p, off = divmod(c, per)
        loc, base_f, gate_f, base_r, gate_r, out_f, out_r, low = locals_[p]
        to = slice(off, off + wide)
        sl = slice(c, c + wide)
        s = state[:, sl]
        mixed[:, sl] = (
            loc[:, to]
            + out_f[:, to] * mm_tn(query, s[0:nstate])
            + out_r[:, to] * mm_tn(query, s[2 * nstate : 3 * nstate])
        ).astype(BF16)
        s_br, s_bf = s[nstate : 2 * nstate], s[3 * nstate :]
        h_f = low[0:nstate, to] + low[2 * nstate : 2 * nstate + 1, to] * s_bf.astype(F32)
        h_r = low[nstate : 2 * nstate, to] + low[2 * nstate + 4 : 2 * nstate + 5, to] * s_br.astype(F32)
        df[0:length] = base_f[0:length, to] + gate_f[0:length, to] * mm_tn(key, h_f.astype(BF16))
        df[length:] = base_f[length:, to] + gate_f[length:, to] * mm(beyond, s_bf)
        dr[EDGE:] = base_r[EDGE:, to] + gate_r[EDGE:, to] * mm_tn(key, h_r.astype(BF16))
        dr[0:EDGE] = base_r[0:EDGE, to] + gate_r[0:EDGE, to] * mm(ahead, s_br)
        total = jnp.zeros((length, wide), F32)
        for lag in range(lags):
            total += cw[0, lag : lag + 1, sl] * df[lag : lag + length]
            total += cw[1, lag : lag + 1, sl] * dr[EDGE - lag : EDGE - lag + length]
        grad[:, sl] = total.astype(BF16)


def order(size, head):
    first = [r for r in head if r < size]
    return first + [r for r in reversed(range(1, size)) if r not in first]


def lay(arrays, head):
    return [arrays[0]] + [arrays[r] for r in order(len(arrays), head)]


def in_order(refs, head):
    found = dict(zip([0] + order(len(refs), head), refs))
    return [found[r] for r in range(len(refs))]


def params():
    return pltpu.CompilerParams(vmem_limit_bytes=VMEM)


def cost(flops, size):
    return pl.CostEstimate(flops=flops, bytes_accessed=size, transcendentals=0)


def on_device(
    signal, in_coeff, out_coeff, cotangent, conv_weight, conv_bias, skip_gain, decay_table,
    bucket, segment, *, outer, inner,
):
    length, channels = signal.shape
    heads = skip_gain.shape[1]
    nstate = in_coeff.shape[1]
    axes = ("inner", "outer")
    count = outer * inner
    bucket = bucket.reshape(1, length)
    segment = segment.reshape(1, length)
    sds = jax.ShapeDtypeStruct
    width = channels // outer
    pay = 4 * nstate + 4 * EDGE
    far = 2 * nstate + 3 * EDGE
    in_t, out_t = in_coeff.T, out_coeff.T
    steps = tuple(reversed(range(outer)))
    small = (bucket, segment, decay_table, conv_weight, conv_bias, in_t, out_t)
    operands = [
        pltpu.with_memory_space_constraint(a, pltpu.HBM) for a in (*small, signal, cotangent)
    ]
    *blocks, sums, sums_t = pl.pallas_call(
        functools.partial(begin_kernel, outer=outer, steps=steps),
        name="begin",
        in_specs=[pl.BlockSpec(memory_space=pltpu.HBM)] * len(operands),
        out_shape=[sds((pay, width), BF16)] * outer
        + [sds((3, length, 2 * heads), F32), sds((2 * heads, length), F32)],
        scratch_shapes=[pltpu.VMEM(a.shape, a.dtype) for a in small]
        + [pltpu.VMEM((outer, length, width), BF16)] * 2
        + [
            pltpu.VMEM((length + 2 * EDGE, width), F32),
            pltpu.SemaphoreType.DMA((len(small) + 2 * outer,)),
        ],
        compiler_params=params(),
        cost_estimate=cost(10**8, 2**20),
    )(*operands)
    blocks = blocks[::-1]

    def swap(array, axis, size, r):
        return lax.ppermute(array, axis, [(i, i ^ r) for i in range(size)])

    def exchange(arrays, axis, size):
        got = {r: swap(arrays[r], axis, size, r) for r in reversed(range(1, size))}
        return [got[r] for r in range(1, size)]

    blocks = [blocks[0], *exchange(blocks, "outer", outer)]
    line = 2 * channels + 512
    late_bucket, _ = lax.optimization_barrier((bucket, sums))
    near_rows, next_rows = pl.pallas_call(
        edges_kernel,
        name="edges",
        out_shape=[sds((EDGE, line), BF16)] * 2,
        compiler_params=params(),
        cost_estimate=cost(10**6, 2**18),
    )(signal, cotangent, in_t, out_t, late_bucket, segment)
    before = lax.ppermute(near_rows, "outer", [(i, i ^ 1) for i in range(outer)])
    weights, skips = pl.pallas_call(
        weights_kernel,
        name="weights",
        out_shape=[sds((heads, length, 2 * length), BF16), sds((2, channels), F32)],
        compiler_params=params(),
        cost_estimate=cost(10**8, 2**21),
    )(in_t, out_t, segment, skip_gain, sums, sums_t)
    blocks[0], weights = lax.optimization_barrier((blocks[0], weights))
    pairs = [(i, i + 1) for i in range(1, count - 1, 2)]
    after = lax.ppermute(next_rows, axes, pairs + [(j, i) for i, j in pairs])
    parts = 2

    def local(part):
        per = channels // parts
        both_rows = length + EDGE
        return pl.pallas_call(
            functools.partial(local_kernel, part=part, parts=parts),
            name=f"local{part}",
            out_shape=[
                sds((length, per), F32),
                sds((both_rows, per), F32),
                sds((both_rows, per), F32),
                sds((both_rows, per), F32),
                sds((both_rows, per), F32),
                sds((length, per), F32),
                sds((length, per), F32),
                sds((2 * nstate + EDGE, per), F32),
            ],
            scratch_shapes=[
                pltpu.VMEM((length + 2 * EDGE, channels), F32),
                pltpu.VMEM((2 * heads, channels), BF16),
            ],
            compiler_params=params(),
            cost_estimate=cost(4 * 10**8, 2**22),
        )(
            signal, cotangent, in_t, out_t, segment, conv_weight, conv_bias, decay_table, sums,
            weights, skips, before, after,
        )

    locals_ = [local(p) for p in range(parts)]
    totals = pl.pallas_call(
        functools.partial(totals_kernel, outer=outer, inner=inner, nstate=nstate),
        name="totals",
        out_shape=[sds((far, width), BF16)] * (inner - 1),
        scratch_shapes=[pltpu.VMEM((outer, pay, width), BF16)],
        compiler_params=params(),
        cost_estimate=cost(10**6, 2**19),
    )(*lay(blocks, FIRST), conv_weight, conv_bias)
    totals = exchange([None, *totals], "inner", inner)
    entries = pl.pallas_call(
        functools.partial(entries_kernel, outer=outer, inner=inner, nstate=nstate),
        name="entries",
        out_shape=[sds((4 * nstate, width), BF16)] * outer,
        scratch_shapes=[
            pltpu.VMEM((outer, pay, width), BF16),
            pltpu.VMEM((inner, far, width), F32),
            pltpu.VMEM((outer, 4 * nstate, width), BF16),
        ],
        compiler_params=params(),
        cost_estimate=cost(10**6, 2**19),
    )(*lay(blocks, FIRST), *lay([None, *totals], SECOND)[1:], conv_weight, conv_bias)
    entries = [entries[0], *exchange(entries, "outer", outer)]
    return pl.pallas_call(
        functools.partial(finish_kernel, outer=outer, parts=parts),
        name="finish",
        out_shape=[sds((length, channels), BF16)] * 2,
        scratch_shapes=[
            pltpu.VMEM((4 * nstate, channels), BF16),
            pltpu.VMEM((length + EDGE, 256), F32),
            pltpu.VMEM((length + EDGE, 256), F32),
        ],
        compiler_params=params(),
        cost_estimate=cost(10**8, 2**22),
    )(*lay(entries, THIRD), *[a for group in locals_ for a in group], in_t, out_t, before, after, conv_weight)


def solution(mesh):
    rows = P(("groups", "inner", "outer"), None)
    flat = P(("groups", "inner", "outer"))
    return jax.shard_map(
        functools.partial(on_device, outer=mesh.shape["outer"], inner=mesh.shape["inner"]),
        mesh=mesh,
        in_specs=(rows, rows, rows, rows, P(), P(), P(), P(), flat, flat),
        out_specs=(rows, rows),
        check_vma=False,
    )
```

```python
import functools

import jax
import jax.numpy as jnp
from jax import lax
from jax.experimental import pallas as pl
from jax.experimental.pallas import tpu as pltpu
from jax.sharding import PartitionSpec as P

F32, BF16 = jnp.float32, jnp.bfloat16
EXACT = lax.Precision.HIGHEST
EDGE = 8
VMEM = 14 * 2**20
NEVER = -1e4
FIRST, SECOND, THIRD = (2, 1, 3), (3, 2, 1), (2, 1, 3)


def mm(a, b, precision=None):
    return lax.dot_general(
        a, b, (((1,), (0,)), ((), ())), precision=precision, preferred_element_type=F32
    )


def mm_tn(a, b, precision=None):
    return lax.dot_general(
        a, b, (((0,), (0,)), ((), ())), precision=precision, preferred_element_type=F32
    )


def mm_nt(a, b, precision=None):
    return lax.dot_general(
        a, b, (((1,), (1,)), ((), ())), precision=precision, preferred_element_type=F32
    )


def iota(shape, dim):
    return lax.broadcasted_iota(jnp.int32, shape, dim)


def twice(heads):
    col = iota((heads, 2 * heads), 1)
    col = jnp.where(col < heads, col, col - heads)
    return (iota((heads, 2 * heads), 0) == col).astype(F32)


def spread(heads, lanes, hdim, start=0):
    row = iota((2 * heads, lanes), 0)
    row = jnp.where(row < heads, row, row - heads)
    low = row * hdim
    col = iota((2 * heads, lanes), 1) + start
    return ((col >= low) & (col < low + hdim)).astype(BF16)


def high_low(x):
    high = x.astype(BF16).astype(F32)
    return jnp.where(iota(x.shape, 1) < x.shape[1] // 2, high, x - high).astype(BF16)


def three(x):
    high = x.astype(BF16)
    rest = x - high.astype(F32)
    mid = rest.astype(BF16)
    return jnp.concatenate([high, mid, (rest - mid.astype(F32)).astype(BF16)], axis=0)


def one_hot(column, size):
    return (column == iota((column.shape[0], size), 1).astype(column.dtype)).astype(F32)


def edges_kernel(sig, cot, in_t, out_t, bucket, segment, near, next_):
    length = bucket.shape[1]
    channels = sig.shape[1]

    bcol = jnp.transpose(jnp.broadcast_to(bucket[...].astype(F32), (length, length)))
    scol = jnp.transpose(jnp.broadcast_to(segment[...].astype(F32), (length, length)))
    j, t = iota((EDGE, length), 0), iota((EDGE, length), 1)
    even = lax.axis_index("outer") % 2 == 0

    def ends(place, value):
        final, first = value(length - EDGE), value(0)
        here = jnp.full(final.shape, even)
        columns = slice(place, place + final.shape[1])
        near[:, columns] = jnp.where(here, final, first).astype(BF16)
        next_[:, columns] = jnp.where(here, first, final).astype(BF16)

    def rows_of(ref):
        def get(row):
            start = row // 16 * 16
            return ref[start : start + 16].astype(F32)[row - start : row - start + EDGE]

        return get

    for k, ref in enumerate((sig, cot)):
        ends(k * channels, rows_of(ref))
    for k, ref in enumerate((in_t, out_t)):
        ends(2 * channels + 128 * k, lambda row: mm_nt((t == j + row).astype(BF16), ref[...]))
    for k, full in enumerate((bcol, scol)):
        ends(2 * channels + 256 + 128 * k, lambda row: full[row : row + EDGE, :128])


def neighbours(near, next_):
    a, b = near[...].astype(F32), next_[...].astype(F32)
    even = jnp.full(a.shape, lax.axis_index("outer") % 2 == 0)
    return jnp.where(even, b, a), jnp.where(even, a, b)


def edge_parts(x, channels, state):
    return (
        x[:, :channels].astype(F32),
        x[:, channels : 2 * channels].astype(F32),
        x[:, 2 * channels : 2 * channels + state].astype(F32),
        x[:, 2 * channels + 128 : 2 * channels + 128 + state].astype(F32),
        x[:, 2 * channels + 256 : 2 * channels + 257].astype(F32),
        x[:, 2 * channels + 384 : 2 * channels + 385].astype(F32),
    )


def conv(ext, start, rows, weight, bias, sl, step):
    total = bias
    for lag in range(weight.shape[0]):
        at = start + step * lag
        total = total + weight[lag : lag + 1, sl] * ext[at : at + rows, sl]
    return total


def begin_kernel(*refs, outer, steps):
    bucket_h, segment_h, table_h, cw_h, cb_h, in_h, out_h, sig_h, cot_h = refs[:9]
    count = len(steps)
    outs = refs[9 : 9 + count]
    sums, sums_t = refs[9 + count : 11 + count]
    bucket, segment, table, cw, cb, in_t, out_t, sig, cot, ext, fades_t, sems = refs[11 + count :]
    near = (bucket, segment, table, cw, cb, in_t, out_t)
    me = lax.axis_index("outer")
    length = segment.shape[1]
    heads = table.shape[2]
    rows = table.shape[1]
    nstate = in_t.shape[0]
    width = sig.shape[2]
    channels = width * outer
    hdim = channels // heads
    margin = cw.shape[1] - 1
    starts = [pl.multiple_of((me ^ r) * width, 128) for r in steps]
    small_in = [
        pltpu.make_async_copy(a, b, sems.at[k]) for k, (a, b) in enumerate(zip(refs[:7], near))
    ]
    large_in = []
    for k, start in enumerate(starts):
        for n, (a, b) in enumerate(((sig_h, sig), (cot_h, cot))):
            large_in.append(
                pltpu.make_async_copy(
                    a.at[:, pl.ds(start, width)], b.at[k], sems.at[7 + 2 * k + n]
                )
            )
    for copy in small_in + large_in:
        copy.start()
    for copy in small_in[:3]:
        copy.wait()
    last, tail = length - 1, length - margin
    hot = (bucket[...] == iota((rows, length), 0)).astype(BF16)
    hot = jnp.concatenate([hot, hot, hot], axis=0)
    row, col = iota((length, length), 0), iota((length, length), 1)
    counts = mm_nt((row >= col).astype(BF16), hot).astype(BF16)
    parts_f, parts_r = three(table[0]), three(table[1])
    dup = twice(heads).astype(BF16)
    cf = mm(counts, mm(parts_f, dup).astype(BF16))
    ci = mm(counts, mm(parts_r, dup).astype(BF16))
    lanes4 = 8 * heads
    kind = iota((heads, lanes4), 1) // (2 * heads)
    same_head = iota((heads, lanes4), 0) == iota((heads, lanes4), 1) % heads
    sign = jnp.where(kind < 2, -1.0, 1.0)
    pick_f = jnp.where(same_head & ((kind == 0) | (kind == 3)), sign, 0.0).astype(BF16)
    pick_r = jnp.where(same_head & ((kind == 1) | (kind == 2)), sign, 0.0).astype(BF16)
    quad = mm(counts, (mm(parts_f, pick_f) + mm(parts_r, pick_r)).astype(BF16))
    t, kind = iota((length, lanes4), 0), iota((length, lanes4), 1) // (2 * heads)
    reverse = (kind == 1) | (kind == 2)
    before = jnp.where(t == 0, 0.0, pltpu.roll(quad, 1, 0))
    quad = jnp.where(reverse, before, quad)
    cr = jnp.where(iota(ci.shape, 0) == 0, 0.0, pltpu.roll(ci, 1, 0))
    sums[0], sums[1], sums[2] = cf, cr, ci
    counts_t = mm(hot, (row <= col).astype(BF16))
    sums_t[0:heads] = mm_tn(parts_f, counts_t.astype(BF16))
    sums_t[heads : 2 * heads] = mm_tn(parts_r, (counts_t - hot.astype(F32)).astype(BF16))
    seg = segment[...].astype(F32)
    seg_full = jnp.transpose(jnp.broadcast_to(seg, (length, length)))
    seg_col = seg_full[:, : 2 * heads]

    def at(place):
        return seg[:, place : place + 1]

    def by_kind(a, b, c, d, like):
        k = kind[: like.shape[0]] if like.shape[0] > 1 else kind[0:1]
        return jnp.where(k == 0, a, jnp.where(k == 1, b, jnp.where(k == 2, c, d)))

    line = quad[0:1]
    anchor = by_kind(quad[last:], quad[tail : tail + 1], line, quad[margin - 1 : margin], line)
    owner = by_kind(at(last), at(tail - 1), at(0), at(margin), line)
    first, end = jnp.where(reverse, 0, margin), jnp.where(reverse, tail, length)
    inside = (t >= first) & (t < end) & (seg_full[:, :lanes4] == owner)
    fades = jnp.where(inside, jnp.exp(quad - anchor), 0.0)
    fades_t[...] = jnp.transpose(fades)
    total_f, total_r = cf[last:], ci[last:]
    j = iota((EDGE, 2 * heads), 0)
    early, late = j < margin, j >= EDGE - margin
    at_tail = cr[tail : tail + 1]
    logs = (
        total_f,
        at_tail,
        jnp.where(at(tail - 1) == at(last), total_r - at_tail, NEVER),
        total_r,
        total_f - cf[margin - 1 : margin],
        jnp.where(at(0) == at(margin), cf[margin - 1 : margin], NEVER),
    )
    keeps = jnp.zeros((EDGE, 2 * heads), F32)
    for k, value in enumerate(logs):
        keeps = jnp.where(j == k, value, keeps)
    cf_0, cr_l = cf[0:EDGE], cr[length - EDGE :]
    seg_0, seg_l = seg_col[0:EDGE], seg_col[length - EDGE :]
    act_fade = jnp.where(
        early & (seg_0 == at(last)),
        jnp.exp(total_f - cf_0),
        jnp.where(late & (seg_l == at(0)), jnp.exp(cr_l), 0.0),
    )
    cot_fade = jnp.where(
        early & (seg_0 == at(0)),
        jnp.exp(cf_0),
        jnp.where(late & (seg_l == at(last)), jnp.exp(total_r - cr_l), 0.0),
    )
    small = high_low(jnp.concatenate([keeps, act_fade, cot_fade], axis=0))
    for copy in small_in[3:]:
        copy.wait()
    keys, queries = in_t[...], out_t[...]
    keys_f, queries_f = keys.astype(F32), queries.astype(F32)
    k, s = iota((EDGE, length), 0), iota((EDGE, length), 1)
    lines = jnp.concatenate([keys, keys, queries, queries], axis=0)
    firsts = mm_nt(((k < margin) & (s == k)).astype(BF16), lines)
    finals = mm_nt(((k >= EDGE - margin) & (s == k + length - EDGE)).astype(BF16), lines)
    group = iota(firsts.shape, 1) // nstate
    coeff = jnp.where(group % 2 == 0, firsts, finals)
    coeff = jnp.where(
        k == 3,
        jnp.where(
            group == 0,
            at(0),
            jnp.where(group == 1, at(margin), jnp.where(group == 2, at(tail - 1), at(last))),
        ),
        coeff,
    )
    if width > coeff.shape[1]:
        coeff = jnp.concatenate(
            [coeff, jnp.zeros((EDGE, width - coeff.shape[1]), F32)], axis=1
        )
    ext[0:EDGE] = jnp.zeros((EDGE, width), F32)
    ext[EDGE + length :] = jnp.zeros((EDGE, width), F32)
    row = iota((EDGE, width), 0)
    base = 4 * nstate
    for n, start in enumerate(starts):
        lanes = pl.ds(start, width)
        widen = spread(heads, width, hdim, start)
        large_in[2 * n].wait()
        ext[EDGE : EDGE + length] = sig[n].astype(F32)
        acts = []
        for side in range(2):
            pre = cb[side : side + 1, lanes]
            for lag in range(margin + 1):
                first = EDGE + (lag if side else -lag)
                pre = pre + cw[side, lag : lag + 1, lanes] * ext[first : first + length]
            acts.append((pre * jax.nn.sigmoid(pre)).astype(BF16))
        large_in[2 * n + 1].wait()
        for c in range(0, width, 128):
            head = (me ^ steps[n]) * (width // hdim) + c // hdim
            pair = slice(c, c + 128)

            def faded(kind, rows):
                parts = [
                    rows * fades_t[pl.ds(2 * heads * kind + head + k, 1)]
                    for k in range(128 // hdim)
                ]
                return jnp.concatenate(parts, axis=0).astype(BF16)

            def own(rows):
                which = iota((nstate, 128), 1) // hdim
                total = rows[0:nstate]
                for k in range(1, 128 // hdim):
                    total = jnp.where(which == k, rows[k * nstate : (k + 1) * nstate], total)
                return total.astype(BF16)

            outs[n][0:nstate, pair] = own(mm(faded(0, keys_f), acts[0][:, pair]))
            outs[n][2 * nstate : 3 * nstate, pair] = own(mm(faded(2, keys_f), acts[1][:, pair]))
            two = jnp.concatenate([faded(1, queries_f), faded(3, queries_f)], axis=0)
            two = mm(two, cot[n, :, pair])
            half = two.shape[0] // 2
            outs[n][nstate : 2 * nstate, pair] = own(two[:half])
            outs[n][3 * nstate : 4 * nstate, pair] = own(two[half:])
        e = mm(small, widen)

        def tile(ref):
            top = ref[n, 0:16].astype(F32)[0:EDGE]
            return jnp.where(row < 4, top, ref[n, length - 16 :].astype(F32)[EDGE:])

        def spare(rows, first):
            filled = jnp.where(row == 3, e[first : first + 1], rows)
            return jnp.where(row == 4, e[first + 1 : first + 2], filled)

        outs[n][base : base + 16] = jnp.concatenate(
            [spare(tile(sig), 0), spare(e[EDGE : 2 * EDGE], 2)], axis=0
        ).astype(BF16)
        outs[n][base + 16 : base + 32] = jnp.concatenate(
            [spare(tile(cot) * e[2 * EDGE :], 4), coeff], axis=0
        ).astype(BF16)


def edge_sums(before, after, table, channels, state, heads, margin):
    dup = twice(heads)
    table_f = mm(table[0], dup, EXACT)
    table_r = mm(table[1], dup, EXACT)
    bs, bc, bi, bo, bb, bseg = edge_parts(before, channels, state)
    as_, ac, ai, ao, ab, aseg = edge_parts(after, channels, state)
    tri = (iota((EDGE, EDGE), 0) >= iota((EDGE, EDGE), 1)).astype(F32)
    rev = (iota((EDGE, EDGE), 0) <= iota((EDGE, EDGE), 1)).astype(F32)
    rows = table.shape[1]
    nf = mm(mm(tri, one_hot(ab, rows)), table_f, EXACT)
    pr = mm(mm(rev, one_hot(bb, rows)), table_r, EXACT)
    return (bs, bc, bi, bo, bseg), (as_, ac, ai, ao, aseg), nf, pr


class Block:
    def __init__(self, ref, nstate):
        x = ref.astype(F32)
        h = 4 * nstate
        self.f, self.br = x[0:nstate], x[nstate : 2 * nstate]
        self.r, self.bf = x[2 * nstate : 3 * nstate], x[3 * nstate : h]
        self.sig, self.fade = x[h : h + 8], x[h + 8 : h + 16]
        self.cot, self.coeff = x[h + 16 : h + 24], x[h + 24 : h + 32]
        self.keep_f, self.near_br = self.sig[3:4], self.sig[4:5]
        self.far_br, self.keep_r = self.fade[3:4], self.fade[4:5]
        self.near_bf, self.far_bf = self.cot[3:4], self.cot[4:5]
        self.seg_first, self.seg_early = self.coeff[3:4, 0:1], self.coeff[3:4, nstate : nstate + 1]
        self.seg_late = self.coeff[3:4, 2 * nstate : 2 * nstate + 1]
        self.seg_last = self.coeff[3:4, 3 * nstate : 3 * nstate + 1]


def alike(a, b):
    return jnp.where(a == b, 0.0, NEVER)


def act_rows(before, here, after, cw, cb, lanes):
    row = iota(here.shape, 0)
    pre_f = cb[0:1, lanes] + cw[0, 0:1, lanes] * here
    pre_r = cb[1:2, lanes] + cw[1, 0:1, lanes] * here
    for lag in range(1, cw.shape[1]):
        moved = pltpu.roll(jnp.where(row >= EDGE - lag, before, here), lag, 0)
        pre_f += cw[0, lag : lag + 1, lanes] * moved
        moved = pltpu.roll(jnp.where(row < lag, after, here), EDGE - lag, 0)
        pre_r += cw[1, lag : lag + 1, lanes] * moved
    pre = jnp.where(row < 4, pre_f, pre_r)
    return pre * jax.nn.sigmoid(pre)


def edge_states(act, fade, cot, coeff, nstate):
    coeff = coeff.astype(BF16)
    row = iota(cot.shape, 0)
    edge = (row < 3) | (row > 4)
    a = mm_tn(coeff[:, : 2 * nstate], jnp.where(edge, act * fade, 0.0).astype(BF16))
    b = mm_tn(coeff[:, 2 * nstate : 4 * nstate], jnp.where(edge, cot, 0.0).astype(BF16))
    return a[:nstate], a[nstate:], b[:nstate], b[nstate:]


def totals_kernel(*refs, outer, inner, nstate):
    blocks, (cw, cb), outs, held = in_order(refs[:outer], FIRST), refs[outer : outer + 2], refs[outer + 2 : -1], refs[-1]
    me = lax.axis_index("outer")
    place = lax.axis_index("inner")
    width = blocks[0].shape[1]
    lanes = pl.ds(pl.multiple_of(me * width, 128), width)
    for r in range(outer):
        held[me ^ r] = blocks[r][...]
    b = [Block(held[k], nstate) for k in range(outer)]
    none = jnp.zeros((EDGE, width), F32)
    low = []
    for k in range(outer):
        before = b[k - 1].sig if k else none
        after = b[k + 1].sig if k < outer - 1 else none
        act = act_rows(before, b[k].sig, after, cw, cb, lanes)
        low.append(edge_states(act, b[k].fade, b[k].cot, b[k].coeff, nstate))
    end = outer - 1
    f, x = b[0].f, b[0].br
    keep_f, keep_br = jnp.zeros((1, width), F32), b[0].near_br
    for k in range(1, outer):
        y = low[k - 1][3] + jnp.exp(b[k - 1].far_br) * x
        factor = b[k].near_br + alike(b[k - 1].seg_last, b[k].seg_late)
        x = b[k].br + jnp.exp(factor) * y
        keep_br = keep_br + b[k - 1].far_br + factor
        factor = b[k].keep_f + alike(b[k - 1].seg_last, b[k].seg_last)
        f = b[k].f + low[k][0] + jnp.exp(factor) * f
        keep_f = keep_f + factor
    r, z = b[end].r, b[end].bf
    keep_r, keep_bf = jnp.zeros((1, width), F32), b[end].near_bf
    for k in range(end - 1, -1, -1):
        y = low[k + 1][2] + jnp.exp(b[k + 1].far_bf) * z
        factor = b[k].near_bf + alike(b[k + 1].seg_first, b[k].seg_early)
        z = b[k].bf + jnp.exp(factor) * y
        keep_bf = keep_bf + b[k + 1].far_bf + factor
        factor = b[k].keep_r + alike(b[k + 1].seg_first, b[k].seg_first)
        r = b[k].r + low[k][1] + jnp.exp(factor) * r
        keep_r = keep_r + factor
    row = iota((EDGE, width), 0)
    half = row < 4

    def spare(rows, first, second):
        return jnp.where(row == 3, first, jnp.where(row == 4, second, rows))

    def named(rows, *values):
        group = iota(rows.shape, 1) // nstate
        for k, value in enumerate(values):
            rows = jnp.where((row == 3) & (group == k), value, rows)
        return rows

    sig = jnp.where(half, b[0].sig, b[end].sig)
    coeff = jnp.where(half, b[0].coeff, b[end].coeff)
    up = jnp.concatenate(
        [
            f,
            x,
            spare(sig, keep_f, b[0].keep_f),
            named(coeff, b[0].seg_last, b[0].seg_late, b[end].seg_last),
            spare(jnp.where(half, b[0].fade, b[end].cot), keep_br, b[end].far_br),
        ],
        axis=0,
    )
    down = jnp.concatenate(
        [
            r,
            z,
            spare(sig, keep_r, b[end].keep_r),
            named(coeff, b[end].seg_first, b[end].seg_early, b[0].seg_first),
            spare(jnp.where(half, b[0].cot, b[end].fade), keep_bf, b[0].far_bf),
        ],
        axis=0,
    )
    for r in range(1, inner):
        towards = jnp.full(up.shape, place ^ r, jnp.int32) > place
        outs[r - 1][...] = jnp.where(towards, up, down).astype(BF16)


def entries_kernel(*refs, outer, inner, nstate):
    blocks = in_order(refs[:outer], FIRST)
    others = in_order(refs[outer - 1 : outer + inner - 1], SECOND)[1:]
    cw, cb = refs[outer + inner - 1 : outer + inner + 1]
    outs = refs[outer + inner + 1 : -3]
    held, far, entry = refs[-3:]
    me = lax.axis_index("outer")
    place = lax.axis_index("inner")
    width = blocks[0].shape[1]
    lanes = pl.ds(pl.multiple_of(me * width, 128), width)
    for r in range(outer):
        held[me ^ r] = blocks[r][...]
    n, h = nstate, 2 * nstate
    far[place] = jnp.zeros(far.shape[1:], F32)
    for r in range(1, inner):
        far[place ^ r] = others[r - 1][...].astype(F32)
    zero = jnp.zeros((n, width), F32)
    none = jnp.zeros((EDGE, width), F32)
    line = jnp.zeros((1, 1), F32)

    def step(carry, index, wanted, upward):
        state, x, y, edge, seg = carry
        p = far[index]
        sig, coeff, rows = (p[h + k : h + k + EDGE] for k in (0, EDGE, 2 * EDGE))
        segs = [coeff[3:4, k * n : k * n + 1] for k in range(3)]
        if upward:
            act = act_rows(edge, sig, none, cw, cb, lanes)
            first, _, _, second = edge_states(act, rows, rows, coeff, n)
        else:
            act = act_rows(none, sig, edge, cw, cb, lanes)
            _, first, second, _ = edge_states(act, rows, rows, coeff, n)
        inside = jnp.exp(sig[4:5] + alike(seg, segs[0]))
        new = p[0:n] + jnp.exp(sig[3:4]) * (first + inside * state)
        new_x = p[n:h] + jnp.exp(rows[3:4] + alike(seg, segs[1])) * y
        new_y = second + jnp.exp(rows[4:5]) * new_x
        return tuple(
            jnp.where(jnp.full(b.shape, wanted), b, a)
            for a, b in zip(carry, (new, new_x, new_y, sig, segs[2]))
        )

    up = down = (zero, zero, zero, none, line)
    for k in range(inner - 1):
        up = step(up, k, k < place, True)
        back = inner - 1 - k
        down = step(down, back, back > place, False)
    f, x, y, edge_up, seg_up = up
    r, z, w, edge_down, seg_down = down
    b = [Block(held[k], nstate) for k in range(outer)]
    low = []
    for k in range(outer):
        before = b[k - 1].sig if k else edge_up
        after = b[k + 1].sig if k < outer - 1 else edge_down
        act = act_rows(before, b[k].sig, after, cw, cb, lanes)
        low.append(edge_states(act, b[k].fade, b[k].cot, b[k].coeff, nstate))
    for k in range(outer):
        entry[k, 0:h] = jnp.concatenate([f, x], axis=0).astype(BF16)
        if k == outer - 1:
            break
        before = b[k - 1].seg_last if k else seg_up
        f = b[k].f + low[k][0] + jnp.exp(b[k].keep_f + alike(before, b[k].seg_last)) * f
        x = b[k].br + jnp.exp(b[k].near_br + alike(before, b[k].seg_late)) * y
        y = low[k][3] + jnp.exp(b[k].far_br) * x
    for k in range(outer - 1, -1, -1):
        entry[k, h : 2 * h] = jnp.concatenate([r, z], axis=0).astype(BF16)
        if k == 0:
            break
        after = b[k + 1].seg_first if k < outer - 1 else seg_down
        r = b[k].r + low[k][1] + jnp.exp(b[k].keep_r + alike(after, b[k].seg_first)) * r
        z = b[k].bf + jnp.exp(b[k].near_bf + alike(after, b[k].seg_early)) * w
        w = low[k][2] + jnp.exp(b[k].far_bf) * z
    for r_ in range(outer):
        outs[r_][...] = entry[me ^ r_]


def weights_kernel(in_, out, segment, skip, sums, sums_t, weights, skips):
    length = segment.shape[1]
    heads = skip.shape[1]
    channels = skips.shape[1]
    seg = segment[...].astype(F32)
    same = jnp.transpose(jnp.broadcast_to(seg, (length, length))) == seg
    score = mm_tn(out[...], in_[...])
    t, s = iota((length, length), 0), iota((length, length), 1)
    score_f = jnp.where(same & (t >= s), score, 0.0)
    score_r = jnp.where(same & (t <= s), score, 0.0)
    lower = t >= s
    cf, cr = sums[0], sums[1]
    for h in range(heads):
        up = cf[:, h : h + 1] - sums_t[h : h + 1]
        down = sums_t[heads + h : heads + h + 1] - cr[:, h : h + 1]
        x = jnp.exp(jnp.minimum(jnp.where(lower, up, down), 0.0))
        weights[h, :, 0:length] = (x * score_f).astype(BF16)
        weights[h, :, length:] = (x * score_r).astype(BF16)
    wide = spread(heads, channels, channels // heads)[0:heads].astype(F32)
    skips[...] = mm(skip[...], wide, EXACT)


def local_kernel(
    sig, cot, in_, out, segment, cw, cb, table, sums, weights, skips, before, after,
    mixed, base_f, gate_f, base_r, gate_r, out_f, out_r, low, ext, widen,
    *, part, parts,
):
    length, channels = sig.shape
    heads = table.shape[2]
    nstate = in_.shape[0]
    hdim = channels // heads
    margin = cw.shape[1] - 1
    prev, nxt, nf, pr = edge_sums(*neighbours(before, after), table, channels, nstate, heads, margin)
    bs, bc, bi, bo, bseg = prev
    as_, ac, ai, ao, aseg = nxt
    seg = segment[...].astype(F32)
    col_full = jnp.transpose(jnp.broadcast_to(seg, (length, length)))
    col = col_full[:, : 2 * heads]
    cf, cr = sums[0], sums[1]
    total_f = cf[length - 1 : length]
    total_r = sums[2, length - EDGE :][EDGE - 1 : EDGE]
    j = iota((EDGE, 2 * heads), 0)
    early = j < margin
    late = j >= EDGE - margin
    s_first, s_last = aseg[0:1], bseg[EDGE - 1 : EDGE]
    s_beyond, s_ahead = aseg[margin : margin + 1], bseg[EDGE - margin - 1 : EDGE - margin]
    stack = [
        jnp.where(col == s_last, jnp.exp(cf), 0.0),
        jnp.where(col == s_first, jnp.exp(total_r - cr), 0.0),
        jnp.where(col == s_first, jnp.exp(total_f - cf), 0.0),
        jnp.where(col == s_last, jnp.exp(cr), 0.0),
        jnp.where(early & (aseg == s_beyond), jnp.exp(nf[margin - 1 : margin] - nf), 0.0),
        jnp.where(
            late & (bseg == s_ahead), jnp.exp(pr[EDGE - margin : EDGE - margin + 1] - pr), 0.0
        ),
        jnp.where(early & (aseg == s_first), jnp.exp(nf), 0.0),
        jnp.where(late & (bseg == s_last), jnp.exp(pr), 0.0),
        jnp.where(
            j < 4,
            jnp.where(s_first == s_beyond, jnp.exp(nf[margin - 1 : margin]), 0.0),
            jnp.where(s_last == s_ahead, jnp.exp(pr[EDGE - margin : EDGE - margin + 1]), 0.0),
        ),
    ]
    turned = []
    for d in range(margin):
        move = (EDGE - d) % EDGE
        later = pltpu.roll(nf, move, 0) if d else nf
        seg_j = jnp.broadcast_to(aseg, (EDGE, 2 * heads))
        seg_l = pltpu.roll(seg_j, move, 0) if d else seg_j
        ao_d = pltpu.roll(ao, move, 0) if d else ao
        dot = jnp.sum(ai * ao_d, axis=1, keepdims=True)
        stack.append(jnp.where((j + d < margin) & (seg_j == seg_l), jnp.exp(later - nf) * dot, 0.0))
        former = pltpu.roll(pr, d, 0) if d else pr
        seg_j = jnp.broadcast_to(bseg, (EDGE, 2 * heads))
        seg_l = pltpu.roll(seg_j, d, 0) if d else seg_j
        bo_d = pltpu.roll(bo, d, 0) if d else bo
        dot = jnp.sum(bi * bo_d, axis=1, keepdims=True)
        stack.append(
            jnp.where((j - d >= EDGE - margin) & (seg_j == seg_l), jnp.exp(former - pr) * dot, 0.0)
        )
    stack = high_low(jnp.concatenate(stack, axis=0))
    ext[0:EDGE] = bs
    ext[EDGE : EDGE + length] = sig[...].astype(F32)
    ext[EDGE + length :] = as_
    width = channels // parts
    start = part * width
    widen[...] = spread(heads, channels, hdim)
    wide = 128
    first = iota((length, wide), 1) < hdim
    ao_b, bo_b = ao.astype(BF16), bo.astype(BF16)
    for c in range(0, width, wide):
        sl = slice(start + c, start + c + wide)
        to = slice(c, c + wide)
        e = mm(stack, widen[:, sl])
        skip_f, skip_r = skips[0:1, sl], skips[1:2, sl]
        pre = conv(ext, EDGE, length + EDGE, cw[0], cb[0:1, sl], sl, -1)
        sg = jax.nn.sigmoid(pre)
        act_f = (pre * sg)[0:length]
        slope_f = sg * (1.0 + pre * (1.0 - sg))
        pre = conv(ext, 0, length + EDGE, cw[1], cb[1:2, sl], sl, 1)
        sg = jax.nn.sigmoid(pre)
        act_r = (pre * sg)[EDGE:]
        slope_r = sg * (1.0 + pre * (1.0 - sg))
        act = jnp.concatenate([act_f.astype(BF16), act_r.astype(BF16)], axis=0)
        ct16 = cot[:, sl]
        ct = ct16.astype(F32)
        forth, back = [], []
        for k in range(wide // hdim):
            h = (start + c) // hdim + k
            m = weights[h]
            forth.append(mm(m, act))
            back.append(mm_tn(m, ct16))
        mixed[:, to] = jnp.where(first, forth[0], forth[1]) + skip_f * act_f + skip_r * act_r
        here_f = jnp.where(first, back[0][0:length], back[1][0:length]) + skip_f * ct
        here_r = jnp.where(first, back[0][length:], back[1][length:]) + skip_r * ct
        at = 4 * length
        ac_c, bc_c = ac[:, sl], bc[:, sl]
        row = iota((EDGE, wide), 0)
        beyond = jnp.where(row < margin, skip_f * ac_c, 0.0)
        ahead = jnp.where(row >= EDGE - margin, skip_r * bc_c, 0.0)
        for d in range(margin):
            k = at + (5 + 2 * d) * EDGE
            moved = pltpu.roll(ac_c, (EDGE - d) % EDGE, 0) if d else ac_c
            beyond += e[k : k + EDGE] * moved
            moved = pltpu.roll(bc_c, d, 0) if d else bc_c
            ahead += e[k + EDGE : k + 2 * EDGE] * moved
        out_f[:, to] = e[0:length]
        out_r[:, to] = e[length : 2 * length]
        base_f[0:length, to] = here_f * slope_f[0:length]
        base_f[length:, to] = beyond * slope_f[length:]
        gate_f[0:length, to] = e[2 * length : 3 * length] * slope_f[0:length]
        gate_f[length:, to] = e[at : at + EDGE] * slope_f[length:]
        base_r[EDGE:, to] = here_r * slope_r[EDGE:]
        base_r[0:EDGE, to] = ahead * slope_r[0:EDGE]
        gate_r[EDGE:, to] = e[3 * length : 4 * length] * slope_r[EDGE:]
        gate_r[0:EDGE, to] = e[at + EDGE : at + 2 * EDGE] * slope_r[0:EDGE]
        low[0:nstate, to] = mm_tn(ao_b, (ac_c * e[at + 2 * EDGE : at + 3 * EDGE]).astype(BF16))
        low[nstate : 2 * nstate, to] = mm_tn(
            bo_b, (bc_c * e[at + 3 * EDGE : at + 4 * EDGE]).astype(BF16)
        )
        low[2 * nstate :, to] = e[at + 4 * EDGE : at + 5 * EDGE]


def finish_kernel(*refs, outer, parts):
    entries = in_order(refs[:outer], THIRD)
    locals_ = [refs[outer + 8 * p : outer + 8 * (p + 1)] for p in range(parts)]
    in_, out, before, after, cw, mixed, grad, state, df, dr = refs[outer + 8 * parts :]
    length, channels = mixed.shape
    nstate = in_.shape[0]
    me = lax.axis_index("outer")
    width = channels // outer
    for r in range(outer):
        state[:, pl.ds(pl.multiple_of((me ^ r) * width, 128), width)] = entries[r][...]
    per = channels // parts
    query, key = out[...], in_[...]
    at = 2 * channels
    ahead, beyond = neighbours(before.at[:, at : at + 128], after.at[:, at : at + 128])
    ahead, beyond = ahead[:, :nstate].astype(BF16), beyond[:, :nstate].astype(BF16)
    lags = cw.shape[1]
    wide = 256
    for c in range(0, channels, wide):
        p, off = divmod(c, per)
        loc, base_f, gate_f, base_r, gate_r, out_f, out_r, low = locals_[p]
        to = slice(off, off + wide)
        sl = slice(c, c + wide)
        s = state[:, sl]
        mixed[:, sl] = (
            loc[:, to]
            + out_f[:, to] * mm_tn(query, s[0:nstate])
            + out_r[:, to] * mm_tn(query, s[2 * nstate : 3 * nstate])
        ).astype(BF16)
        s_br, s_bf = s[nstate : 2 * nstate], s[3 * nstate :]
        h_f = low[0:nstate, to] + low[2 * nstate : 2 * nstate + 1, to] * s_bf.astype(F32)
        h_r = low[nstate : 2 * nstate, to] + low[2 * nstate + 4 : 2 * nstate + 5, to] * s_br.astype(F32)
        df[0:length] = base_f[0:length, to] + gate_f[0:length, to] * mm_tn(key, h_f.astype(BF16))
        df[length:] = base_f[length:, to] + gate_f[length:, to] * mm(beyond, s_bf)
        dr[EDGE:] = base_r[EDGE:, to] + gate_r[EDGE:, to] * mm_tn(key, h_r.astype(BF16))
        dr[0:EDGE] = base_r[0:EDGE, to] + gate_r[0:EDGE, to] * mm(ahead, s_br)
        total = jnp.zeros((length, wide), F32)
        for lag in range(lags):
            total += cw[0, lag : lag + 1, sl] * df[lag : lag + length]
            total += cw[1, lag : lag + 1, sl] * dr[EDGE - lag : EDGE - lag + length]
        grad[:, sl] = total.astype(BF16)


def order(size, head):
    first = [r for r in head if r < size]
    return first + [r for r in reversed(range(1, size)) if r not in first]


def lay(arrays, head):
    return [arrays[0]] + [arrays[r] for r in order(len(arrays), head)]


def in_order(refs, head):
    found = dict(zip([0] + order(len(refs), head), refs))
    return [found[r] for r in range(len(refs))]


def params():
    return pltpu.CompilerParams(vmem_limit_bytes=VMEM)


def cost(flops, size):
    return pl.CostEstimate(flops=flops, bytes_accessed=size, transcendentals=0)


def on_device(
    signal, in_coeff, out_coeff, cotangent, conv_weight, conv_bias, skip_gain, decay_table,
    bucket, segment, *, outer, inner,
):
    length, channels = signal.shape
    heads = skip_gain.shape[1]
    nstate = in_coeff.shape[1]
    axes = ("inner", "outer")
    count = outer * inner
    bucket = bucket.reshape(1, length)
    segment = segment.reshape(1, length)
    sds = jax.ShapeDtypeStruct
    width = channels // outer
    pay = 4 * nstate + 4 * EDGE
    far = 2 * nstate + 3 * EDGE
    in_t, out_t = in_coeff.T, out_coeff.T
    steps = tuple(reversed(range(outer)))
    small = (bucket, segment, decay_table, conv_weight, conv_bias, in_t, out_t)
    operands = [
        pltpu.with_memory_space_constraint(a, pltpu.HBM) for a in (*small, signal, cotangent)
    ]
    *blocks, sums, sums_t = pl.pallas_call(
        functools.partial(begin_kernel, outer=outer, steps=steps),
        name="begin",
        in_specs=[pl.BlockSpec(memory_space=pltpu.HBM)] * len(operands),
        out_shape=[sds((pay, width), BF16)] * outer
        + [sds((3, length, 2 * heads), F32), sds((2 * heads, length), F32)],
        scratch_shapes=[pltpu.VMEM(a.shape, a.dtype) for a in small]
        + [pltpu.VMEM((outer, length, width), BF16)] * 2
        + [
            pltpu.VMEM((length + 2 * EDGE, width), F32),
            pltpu.VMEM((8 * heads, length), F32),
            pltpu.SemaphoreType.DMA((len(small) + 2 * outer,)),
        ],
        compiler_params=params(),
        cost_estimate=cost(10**8, 2**20),
    )(*operands)
    blocks = blocks[::-1]

    def swap(array, axis, size, r):
        return lax.ppermute(array, axis, [(i, i ^ r) for i in range(size)])

    def exchange(arrays, axis, size):
        got = {r: swap(arrays[r], axis, size, r) for r in reversed(range(1, size))}
        return [got[r] for r in range(1, size)]

    blocks = [blocks[0], *exchange(blocks, "outer", outer)]
    line = 2 * channels + 512
    late_bucket, _ = lax.optimization_barrier((bucket, sums))
    near_rows, next_rows = pl.pallas_call(
        edges_kernel,
        name="edges",
        out_shape=[sds((EDGE, line), BF16)] * 2,
        compiler_params=params(),
        cost_estimate=cost(10**6, 2**18),
    )(signal, cotangent, in_t, out_t, late_bucket, segment)
    before = lax.ppermute(near_rows, "outer", [(i, i ^ 1) for i in range(outer)])
    weights, skips = pl.pallas_call(
        weights_kernel,
        name="weights",
        out_shape=[sds((heads, length, 2 * length), BF16), sds((2, channels), F32)],
        compiler_params=params(),
        cost_estimate=cost(10**8, 2**21),
    )(in_t, out_t, segment, skip_gain, sums, sums_t)
    blocks[0], weights = lax.optimization_barrier((blocks[0], weights))
    pairs = [(i, i + 1) for i in range(1, count - 1, 2)]
    after = lax.ppermute(next_rows, axes, pairs + [(j, i) for i, j in pairs])
    parts = 2

    def local(part):
        per = channels // parts
        both_rows = length + EDGE
        return pl.pallas_call(
            functools.partial(local_kernel, part=part, parts=parts),
            name=f"local{part}",
            out_shape=[
                sds((length, per), F32),
                sds((both_rows, per), F32),
                sds((both_rows, per), F32),
                sds((both_rows, per), F32),
                sds((both_rows, per), F32),
                sds((length, per), F32),
                sds((length, per), F32),
                sds((2 * nstate + EDGE, per), F32),
            ],
            scratch_shapes=[
                pltpu.VMEM((length + 2 * EDGE, channels), F32),
                pltpu.VMEM((2 * heads, channels), BF16),
            ],
            compiler_params=params(),
            cost_estimate=cost(4 * 10**8, 2**22),
        )(
            signal, cotangent, in_t, out_t, segment, conv_weight, conv_bias, decay_table, sums,
            weights, skips, before, after,
        )

    locals_ = [local(p) for p in range(parts)]
    totals = pl.pallas_call(
        functools.partial(totals_kernel, outer=outer, inner=inner, nstate=nstate),
        name="totals",
        out_shape=[sds((far, width), BF16)] * (inner - 1),
        scratch_shapes=[pltpu.VMEM((outer, pay, width), BF16)],
        compiler_params=params(),
        cost_estimate=cost(10**6, 2**19),
    )(*lay(blocks, FIRST), conv_weight, conv_bias)
    totals = exchange([None, *totals], "inner", inner)
    entries = pl.pallas_call(
        functools.partial(entries_kernel, outer=outer, inner=inner, nstate=nstate),
        name="entries",
        out_shape=[sds((4 * nstate, width), BF16)] * outer,
        scratch_shapes=[
            pltpu.VMEM((outer, pay, width), BF16),
            pltpu.VMEM((inner, far, width), F32),
            pltpu.VMEM((outer, 4 * nstate, width), BF16),
        ],
        compiler_params=params(),
        cost_estimate=cost(10**6, 2**19),
    )(*lay(blocks, FIRST), *lay([None, *totals], SECOND)[1:], conv_weight, conv_bias)
    entries = [entries[0], *exchange(entries, "outer", outer)]
    return pl.pallas_call(
        functools.partial(finish_kernel, outer=outer, parts=parts),
        name="finish",
        out_shape=[sds((length, channels), BF16)] * 2,
        scratch_shapes=[
            pltpu.VMEM((4 * nstate, channels), BF16),
            pltpu.VMEM((length + EDGE, 256), F32),
            pltpu.VMEM((length + EDGE, 256), F32),
        ],
        compiler_params=params(),
        cost_estimate=cost(10**8, 2**22),
    )(*lay(entries, THIRD), *[a for group in locals_ for a in group], in_t, out_t, before, after, conv_weight)


def solution(mesh):
    rows = P(("groups", "inner", "outer"), None)
    flat = P(("groups", "inner", "outer"))
    return jax.shard_map(
        functools.partial(on_device, outer=mesh.shape["outer"], inner=mesh.shape["inner"]),
        mesh=mesh,
        in_specs=(rows, rows, rows, rows, P(), P(), P(), P(), flat, flat),
        out_specs=(rows, rows),
        check_vma=False,
    )
```

```python
import functools

import jax
import jax.numpy as jnp
from jax import lax
from jax.experimental import pallas as pl
from jax.experimental.pallas import tpu as pltpu
from jax.sharding import PartitionSpec as P

F32, BF16 = jnp.float32, jnp.bfloat16
EXACT = lax.Precision.HIGHEST
EDGE = 8
VMEM = 14 * 2**20
NEVER = -1e4
FIRST, SECOND, THIRD = (2, 1, 3), (3, 2, 1), (2, 1, 3)


def mm(a, b, precision=None):
    return lax.dot_general(
        a, b, (((1,), (0,)), ((), ())), precision=precision, preferred_element_type=F32
    )


def mm_tn(a, b, precision=None):
    return lax.dot_general(
        a, b, (((0,), (0,)), ((), ())), precision=precision, preferred_element_type=F32
    )


def mm_nt(a, b, precision=None):
    return lax.dot_general(
        a, b, (((1,), (1,)), ((), ())), precision=precision, preferred_element_type=F32
    )


def iota(shape, dim):
    return lax.broadcasted_iota(jnp.int32, shape, dim)


def twice(heads):
    col = iota((heads, 2 * heads), 1)
    col = jnp.where(col < heads, col, col - heads)
    return (iota((heads, 2 * heads), 0) == col).astype(F32)


def spread(heads, lanes, hdim, start=0):
    row = iota((2 * heads, lanes), 0)
    row = jnp.where(row < heads, row, row - heads)
    low = row * hdim
    col = iota((2 * heads, lanes), 1) + start
    return ((col >= low) & (col < low + hdim)).astype(BF16)


def high_low(x):
    high = x.astype(BF16).astype(F32)
    return jnp.where(iota(x.shape, 1) < x.shape[1] // 2, high, x - high).astype(BF16)


def three(x):
    high = x.astype(BF16)
    rest = x - high.astype(F32)
    mid = rest.astype(BF16)
    return jnp.concatenate([high, mid, (rest - mid.astype(F32)).astype(BF16)], axis=0)


def one_hot(column, size):
    return (column == iota((column.shape[0], size), 1).astype(column.dtype)).astype(F32)


def edges_kernel(sig, cot, in_t, out_t, bucket, segment, near, next_):
    length = bucket.shape[1]
    channels = sig.shape[1]

    bcol = jnp.transpose(jnp.broadcast_to(bucket[...].astype(F32), (length, length)))
    scol = jnp.transpose(jnp.broadcast_to(segment[...].astype(F32), (length, length)))
    j, t = iota((EDGE, length), 0), iota((EDGE, length), 1)
    even = lax.axis_index("outer") % 2 == 0

    def ends(place, value):
        final, first = value(length - EDGE), value(0)
        here = jnp.full(final.shape, even)
        columns = slice(place, place + final.shape[1])
        near[:, columns] = jnp.where(here, final, first).astype(BF16)
        next_[:, columns] = jnp.where(here, first, final).astype(BF16)

    def rows_of(ref):
        def get(row):
            start = row // 16 * 16
            return ref[start : start + 16].astype(F32)[row - start : row - start + EDGE]

        return get

    for k, ref in enumerate((sig, cot)):
        ends(k * channels, rows_of(ref))
    for k, ref in enumerate((in_t, out_t)):
        ends(2 * channels + 128 * k, lambda row: mm_nt((t == j + row).astype(BF16), ref[...]))
    for k, full in enumerate((bcol, scol)):
        ends(2 * channels + 256 + 128 * k, lambda row: full[row : row + EDGE, :128])


def neighbours(near, next_):
    a, b = near[...].astype(F32), next_[...].astype(F32)
    even = jnp.full(a.shape, lax.axis_index("outer") % 2 == 0)
    return jnp.where(even, b, a), jnp.where(even, a, b)


def edge_parts(x, channels, state):
    return (
        x[:, :channels].astype(F32),
        x[:, channels : 2 * channels].astype(F32),
        x[:, 2 * channels : 2 * channels + state].astype(F32),
        x[:, 2 * channels + 128 : 2 * channels + 128 + state].astype(F32),
        x[:, 2 * channels + 256 : 2 * channels + 257].astype(F32),
        x[:, 2 * channels + 384 : 2 * channels + 385].astype(F32),
    )


def conv(ext, start, rows, weight, bias, sl, step):
    total = bias
    for lag in range(weight.shape[0]):
        at = start + step * lag
        total = total + weight[lag : lag + 1, sl] * ext[at : at + rows, sl]
    return total


def begin_kernel(*refs, outer, steps):
    bucket_h, segment_h, table_h, cw_h, cb_h, in_h, out_h, sig_h, cot_h = refs[:9]
    count = len(steps)
    outs = refs[9 : 9 + count]
    sums, sums_t = refs[9 + count : 11 + count]
    bucket, segment, table, cw, cb, in_t, out_t, sig, cot, ext, fades_t, sems = refs[11 + count :]
    near = (bucket, segment, table, cw, cb, in_t, out_t)
    me = lax.axis_index("outer")
    length = segment.shape[1]
    heads = table.shape[2]
    rows = table.shape[1]
    nstate = in_t.shape[0]
    channels = sig.shape[1]
    width = channels // outer
    hdim = channels // heads
    margin = cw.shape[1] - 1
    starts = [pl.multiple_of((me ^ r) * width, 128) for r in steps]
    small_in = [
        pltpu.make_async_copy(a, b, sems.at[k]) for k, (a, b) in enumerate(zip(refs[:7], near))
    ]
    large_in = []
    for n, (a, b) in enumerate(((sig_h, sig), (cot_h, cot))):
        large_in.append(pltpu.make_async_copy(a, b, sems.at[7 + n]))
    for copy in small_in + large_in:
        copy.start()
    for copy in small_in + large_in:
        copy.wait()
    last, tail = length - 1, length - margin
    hot = (bucket[...] == iota((rows, length), 0)).astype(BF16)
    hot = jnp.concatenate([hot, hot, hot], axis=0)
    row, col = iota((length, length), 0), iota((length, length), 1)
    counts = mm_nt((row >= col).astype(BF16), hot).astype(BF16)
    parts_f, parts_r = three(table[0]), three(table[1])
    dup = twice(heads).astype(BF16)
    cf = mm(counts, mm(parts_f, dup).astype(BF16))
    ci = mm(counts, mm(parts_r, dup).astype(BF16))
    lanes4 = 8 * heads
    kind = iota((heads, lanes4), 1) // (2 * heads)
    same_head = iota((heads, lanes4), 0) == iota((heads, lanes4), 1) % heads
    sign = jnp.where(kind < 2, -1.0, 1.0)
    pick_f = jnp.where(same_head & ((kind == 0) | (kind == 3)), sign, 0.0).astype(BF16)
    pick_r = jnp.where(same_head & ((kind == 1) | (kind == 2)), sign, 0.0).astype(BF16)
    quad = mm(counts, (mm(parts_f, pick_f) + mm(parts_r, pick_r)).astype(BF16))
    t, kind = iota((length, lanes4), 0), iota((length, lanes4), 1) // (2 * heads)
    reverse = (kind == 1) | (kind == 2)
    before = jnp.where(t == 0, 0.0, pltpu.roll(quad, 1, 0))
    quad = jnp.where(reverse, before, quad)
    cr = jnp.where(iota(ci.shape, 0) == 0, 0.0, pltpu.roll(ci, 1, 0))
    sums[0], sums[1], sums[2] = cf, cr, ci
    counts_t = mm(hot, (row <= col).astype(BF16))
    sums_t[0:heads] = mm_tn(parts_f, counts_t.astype(BF16))
    sums_t[heads : 2 * heads] = mm_tn(parts_r, (counts_t - hot.astype(F32)).astype(BF16))
    seg = segment[...].astype(F32)
    seg_full = jnp.transpose(jnp.broadcast_to(seg, (length, length)))
    seg_col = seg_full[:, : 2 * heads]

    def at(place):
        return seg[:, place : place + 1]

    def by_kind(a, b, c, d, like):
        k = kind[: like.shape[0]] if like.shape[0] > 1 else kind[0:1]
        return jnp.where(k == 0, a, jnp.where(k == 1, b, jnp.where(k == 2, c, d)))

    line = quad[0:1]
    anchor = by_kind(quad[last:], quad[tail : tail + 1], line, quad[margin - 1 : margin], line)
    owner = by_kind(at(last), at(tail - 1), at(0), at(margin), line)
    first, end = jnp.where(reverse, 0, margin), jnp.where(reverse, tail, length)
    inside = (t >= first) & (t < end) & (seg_full[:, :lanes4] == owner)
    fades = jnp.where(inside, jnp.exp(quad - anchor), 0.0)
    fades_t[...] = jnp.transpose(fades)
    total_f, total_r = cf[last:], ci[last:]
    j = iota((EDGE, 2 * heads), 0)
    early, late = j < margin, j >= EDGE - margin
    at_tail = cr[tail : tail + 1]
    logs = (
        total_f,
        at_tail,
        jnp.where(at(tail - 1) == at(last), total_r - at_tail, NEVER),
        total_r,
        total_f - cf[margin - 1 : margin],
        jnp.where(at(0) == at(margin), cf[margin - 1 : margin], NEVER),
    )
    keeps = jnp.zeros((EDGE, 2 * heads), F32)
    for k, value in enumerate(logs):
        keeps = jnp.where(j == k, value, keeps)
    cf_0, cr_l = cf[0:EDGE], cr[length - EDGE :]
    seg_0, seg_l = seg_col[0:EDGE], seg_col[length - EDGE :]
    act_fade = jnp.where(
        early & (seg_0 == at(last)),
        jnp.exp(total_f - cf_0),
        jnp.where(late & (seg_l == at(0)), jnp.exp(cr_l), 0.0),
    )
    cot_fade = jnp.where(
        early & (seg_0 == at(0)),
        jnp.exp(cf_0),
        jnp.where(late & (seg_l == at(last)), jnp.exp(total_r - cr_l), 0.0),
    )
    small = high_low(jnp.concatenate([keeps, act_fade, cot_fade], axis=0))
    keys, queries = in_t[...], out_t[...]
    keys_f, queries_f = keys.astype(F32), queries.astype(F32)
    k, s = iota((EDGE, length), 0), iota((EDGE, length), 1)
    lines = jnp.concatenate([keys, keys, queries, queries], axis=0)
    firsts = mm_nt(((k < margin) & (s == k)).astype(BF16), lines)
    finals = mm_nt(((k >= EDGE - margin) & (s == k + length - EDGE)).astype(BF16), lines)
    group = iota(firsts.shape, 1) // nstate
    coeff = jnp.where(group % 2 == 0, firsts, finals)
    coeff = jnp.where(
        k == 3,
        jnp.where(
            group == 0,
            at(0),
            jnp.where(group == 1, at(margin), jnp.where(group == 2, at(tail - 1), at(last))),
        ),
        coeff,
    )
    if width > coeff.shape[1]:
        coeff = jnp.concatenate(
            [coeff, jnp.zeros((EDGE, width - coeff.shape[1]), F32)], axis=1
        )
    ext[0:EDGE] = jnp.zeros((EDGE, width), F32)
    ext[EDGE + length :] = jnp.zeros((EDGE, width), F32)
    row = iota((EDGE, width), 0)
    base = 4 * nstate
    for n, start in enumerate(starts):
        lanes = pl.ds(start, width)
        widen = spread(heads, width, hdim, start)
        ext[EDGE : EDGE + length] = sig[:, lanes].astype(F32)
        acts = []
        for side in range(2):
            pre = cb[side : side + 1, lanes]
            for lag in range(margin + 1):
                first = EDGE + (lag if side else -lag)
                pre = pre + cw[side, lag : lag + 1, lanes] * ext[first : first + length]
            acts.append((pre * jax.nn.sigmoid(pre)).astype(BF16))
        for c in range(0, width, 128):
            head = (me ^ steps[n]) * (width // hdim) + c // hdim
            pair = slice(c, c + 128)

            def faded(kind, rows):
                parts = [
                    rows * fades_t[pl.ds(2 * heads * kind + head + k, 1)]
                    for k in range(128 // hdim)
                ]
                return jnp.concatenate(parts, axis=0).astype(BF16)

            def own(rows):
                which = iota((nstate, 128), 1) // hdim
                total = rows[0:nstate]
                for k in range(1, 128 // hdim):
                    total = jnp.where(which == k, rows[k * nstate : (k + 1) * nstate], total)
                return total.astype(BF16)

            outs[n][0:nstate, pair] = own(mm(faded(0, keys_f), acts[0][:, pair]))
            outs[n][2 * nstate : 3 * nstate, pair] = own(mm(faded(2, keys_f), acts[1][:, pair]))
            two = jnp.concatenate([faded(1, queries_f), faded(3, queries_f)], axis=0)
            two = mm(two, cot[:, pl.ds(start + c, 128)])
            half = two.shape[0] // 2
            outs[n][nstate : 2 * nstate, pair] = own(two[:half])
            outs[n][3 * nstate : 4 * nstate, pair] = own(two[half:])
        e = mm(small, widen)

        def tile(ref):
            top = ref[0:16, lanes].astype(F32)[0:EDGE]
            return jnp.where(row < 4, top, ref[length - 16 :, lanes].astype(F32)[EDGE:])

        def spare(rows, first):
            filled = jnp.where(row == 3, e[first : first + 1], rows)
            return jnp.where(row == 4, e[first + 1 : first + 2], filled)

        outs[n][base : base + 16] = jnp.concatenate(
            [spare(tile(sig), 0), spare(e[EDGE : 2 * EDGE], 2)], axis=0
        ).astype(BF16)
        outs[n][base + 16 : base + 32] = jnp.concatenate(
            [spare(tile(cot) * e[2 * EDGE :], 4), coeff], axis=0
        ).astype(BF16)


def edge_sums(before, after, table, channels, state, heads, margin):
    dup = twice(heads)
    table_f = mm(table[0], dup, EXACT)
    table_r = mm(table[1], dup, EXACT)
    bs, bc, bi, bo, bb, bseg = edge_parts(before, channels, state)
    as_, ac, ai, ao, ab, aseg = edge_parts(after, channels, state)
    tri = (iota((EDGE, EDGE), 0) >= iota((EDGE, EDGE), 1)).astype(F32)
    rev = (iota((EDGE, EDGE), 0) <= iota((EDGE, EDGE), 1)).astype(F32)
    rows = table.shape[1]
    nf = mm(mm(tri, one_hot(ab, rows)), table_f, EXACT)
    pr = mm(mm(rev, one_hot(bb, rows)), table_r, EXACT)
    return (bs, bc, bi, bo, bseg), (as_, ac, ai, ao, aseg), nf, pr


class Block:
    def __init__(self, ref, nstate):
        x = ref.astype(F32)
        h = 4 * nstate
        self.f, self.br = x[0:nstate], x[nstate : 2 * nstate]
        self.r, self.bf = x[2 * nstate : 3 * nstate], x[3 * nstate : h]
        self.sig, self.fade = x[h : h + 8], x[h + 8 : h + 16]
        self.cot, self.coeff = x[h + 16 : h + 24], x[h + 24 : h + 32]
        self.keep_f, self.near_br = self.sig[3:4], self.sig[4:5]
        self.far_br, self.keep_r = self.fade[3:4], self.fade[4:5]
        self.near_bf, self.far_bf = self.cot[3:4], self.cot[4:5]
        self.seg_first, self.seg_early = self.coeff[3:4, 0:1], self.coeff[3:4, nstate : nstate + 1]
        self.seg_late = self.coeff[3:4, 2 * nstate : 2 * nstate + 1]
        self.seg_last = self.coeff[3:4, 3 * nstate : 3 * nstate + 1]


def alike(a, b):
    return jnp.where(a == b, 0.0, NEVER)


def act_rows(before, here, after, cw, cb, lanes):
    row = iota(here.shape, 0)
    pre_f = cb[0:1, lanes] + cw[0, 0:1, lanes] * here
    pre_r = cb[1:2, lanes] + cw[1, 0:1, lanes] * here
    for lag in range(1, cw.shape[1]):
        moved = pltpu.roll(jnp.where(row >= EDGE - lag, before, here), lag, 0)
        pre_f += cw[0, lag : lag + 1, lanes] * moved
        moved = pltpu.roll(jnp.where(row < lag, after, here), EDGE - lag, 0)
        pre_r += cw[1, lag : lag + 1, lanes] * moved
    pre = jnp.where(row < 4, pre_f, pre_r)
    return pre * jax.nn.sigmoid(pre)


def edge_states(act, fade, cot, coeff, nstate):
    coeff = coeff.astype(BF16)
    row = iota(cot.shape, 0)
    edge = (row < 3) | (row > 4)
    a = mm_tn(coeff[:, : 2 * nstate], jnp.where(edge, act * fade, 0.0).astype(BF16))
    b = mm_tn(coeff[:, 2 * nstate : 4 * nstate], jnp.where(edge, cot, 0.0).astype(BF16))
    return a[:nstate], a[nstate:], b[:nstate], b[nstate:]


def totals_kernel(*refs, outer, inner, nstate):
    blocks, (cw, cb), outs, held = in_order(refs[:outer], FIRST), refs[outer : outer + 2], refs[outer + 2 : -1], refs[-1]
    me = lax.axis_index("outer")
    place = lax.axis_index("inner")
    width = blocks[0].shape[1]
    lanes = pl.ds(pl.multiple_of(me * width, 128), width)
    for r in range(outer):
        held[me ^ r] = blocks[r][...]
    b = [Block(held[k], nstate) for k in range(outer)]
    none = jnp.zeros((EDGE, width), F32)
    low = []
    for k in range(outer):
        before = b[k - 1].sig if k else none
        after = b[k + 1].sig if k < outer - 1 else none
        act = act_rows(before, b[k].sig, after, cw, cb, lanes)
        low.append(edge_states(act, b[k].fade, b[k].cot, b[k].coeff, nstate))
    end = outer - 1
    f, x = b[0].f, b[0].br
    keep_f, keep_br = jnp.zeros((1, width), F32), b[0].near_br
    for k in range(1, outer):
        y = low[k - 1][3] + jnp.exp(b[k - 1].far_br) * x
        factor = b[k].near_br + alike(b[k - 1].seg_last, b[k].seg_late)
        x = b[k].br + jnp.exp(factor) * y
        keep_br = keep_br + b[k - 1].far_br + factor
        factor = b[k].keep_f + alike(b[k - 1].seg_last, b[k].seg_last)
        f = b[k].f + low[k][0] + jnp.exp(factor) * f
        keep_f = keep_f + factor
    r, z = b[end].r, b[end].bf
    keep_r, keep_bf = jnp.zeros((1, width), F32), b[end].near_bf
    for k in range(end - 1, -1, -1):
        y = low[k + 1][2] + jnp.exp(b[k + 1].far_bf) * z
        factor = b[k].near_bf + alike(b[k + 1].seg_first, b[k].seg_early)
        z = b[k].bf + jnp.exp(factor) * y
        keep_bf = keep_bf + b[k + 1].far_bf + factor
        factor = b[k].keep_r + alike(b[k + 1].seg_first, b[k].seg_first)
        r = b[k].r + low[k][1] + jnp.exp(factor) * r
        keep_r = keep_r + factor
    row = iota((EDGE, width), 0)
    half = row < 4

    def spare(rows, first, second):
        return jnp.where(row == 3, first, jnp.where(row == 4, second, rows))

    def named(rows, *values):
        group = iota(rows.shape, 1) // nstate
        for k, value in enumerate(values):
            rows = jnp.where((row == 3) & (group == k), value, rows)
        return rows

    sig = jnp.where(half, b[0].sig, b[end].sig)
    coeff = jnp.where(half, b[0].coeff, b[end].coeff)
    up = jnp.concatenate(
        [
            f,
            x,
            spare(sig, keep_f, b[0].keep_f),
            named(coeff, b[0].seg_last, b[0].seg_late, b[end].seg_last),
            spare(jnp.where(half, b[0].fade, b[end].cot), keep_br, b[end].far_br),
        ],
        axis=0,
    )
    down = jnp.concatenate(
        [
            r,
            z,
            spare(sig, keep_r, b[end].keep_r),
            named(coeff, b[end].seg_first, b[end].seg_early, b[0].seg_first),
            spare(jnp.where(half, b[0].cot, b[end].fade), keep_bf, b[0].far_bf),
        ],
        axis=0,
    )
    for r in range(1, inner):
        towards = jnp.full(up.shape, place ^ r, jnp.int32) > place
        outs[r - 1][...] = jnp.where(towards, up, down).astype(BF16)


def entries_kernel(*refs, outer, inner, nstate):
    blocks = in_order(refs[:outer], FIRST)
    others = in_order(refs[outer - 1 : outer + inner - 1], SECOND)[1:]
    cw, cb = refs[outer + inner - 1 : outer + inner + 1]
    outs = refs[outer + inner + 1 : -3]
    held, far, entry = refs[-3:]
    me = lax.axis_index("outer")
    place = lax.axis_index("inner")
    width = blocks[0].shape[1]
    lanes = pl.ds(pl.multiple_of(me * width, 128), width)
    for r in range(outer):
        held[me ^ r] = blocks[r][...]
    n, h = nstate, 2 * nstate
    far[place] = jnp.zeros(far.shape[1:], F32)
    for r in range(1, inner):
        far[place ^ r] = others[r - 1][...].astype(F32)
    zero = jnp.zeros((n, width), F32)
    none = jnp.zeros((EDGE, width), F32)
    line = jnp.zeros((1, 1), F32)

    def step(carry, index, wanted, upward):
        state, x, y, edge, seg = carry
        p = far[index]
        sig, coeff, rows = (p[h + k : h + k + EDGE] for k in (0, EDGE, 2 * EDGE))
        segs = [coeff[3:4, k * n : k * n + 1] for k in range(3)]
        if upward:
            act = act_rows(edge, sig, none, cw, cb, lanes)
            first, _, _, second = edge_states(act, rows, rows, coeff, n)
        else:
            act = act_rows(none, sig, edge, cw, cb, lanes)
            _, first, second, _ = edge_states(act, rows, rows, coeff, n)
        inside = jnp.exp(sig[4:5] + alike(seg, segs[0]))
        new = p[0:n] + jnp.exp(sig[3:4]) * (first + inside * state)
        new_x = p[n:h] + jnp.exp(rows[3:4] + alike(seg, segs[1])) * y
        new_y = second + jnp.exp(rows[4:5]) * new_x
        return tuple(
            jnp.where(jnp.full(b.shape, wanted), b, a)
            for a, b in zip(carry, (new, new_x, new_y, sig, segs[2]))
        )

    up = down = (zero, zero, zero, none, line)
    for k in range(inner - 1):
        up = step(up, k, k < place, True)
        back = inner - 1 - k
        down = step(down, back, back > place, False)
    f, x, y, edge_up, seg_up = up
    r, z, w, edge_down, seg_down = down
    b = [Block(held[k], nstate) for k in range(outer)]
    low = []
    for k in range(outer):
        before = b[k - 1].sig if k else edge_up
        after = b[k + 1].sig if k < outer - 1 else edge_down
        act = act_rows(before, b[k].sig, after, cw, cb, lanes)
        low.append(edge_states(act, b[k].fade, b[k].cot, b[k].coeff, nstate))
    for k in range(outer):
        entry[k, 0:h] = jnp.concatenate([f, x], axis=0).astype(BF16)
        if k == outer - 1:
            break
        before = b[k - 1].seg_last if k else seg_up
        f = b[k].f + low[k][0] + jnp.exp(b[k].keep_f + alike(before, b[k].seg_last)) * f
        x = b[k].br + jnp.exp(b[k].near_br + alike(before, b[k].seg_late)) * y
        y = low[k][3] + jnp.exp(b[k].far_br) * x
    for k in range(outer - 1, -1, -1):
        entry[k, h : 2 * h] = jnp.concatenate([r, z], axis=0).astype(BF16)
        if k == 0:
            break
        after = b[k + 1].seg_first if k < outer - 1 else seg_down
        r = b[k].r + low[k][1] + jnp.exp(b[k].keep_r + alike(after, b[k].seg_first)) * r
        z = b[k].bf + jnp.exp(b[k].near_bf + alike(after, b[k].seg_early)) * w
        w = low[k][2] + jnp.exp(b[k].far_bf) * z
    for r_ in range(outer):
        outs[r_][...] = entry[me ^ r_]


def weights_kernel(in_, out, segment, skip, sums, sums_t, weights, skips):
    length = segment.shape[1]
    heads = skip.shape[1]
    channels = skips.shape[1]
    seg = segment[...].astype(F32)
    same = jnp.transpose(jnp.broadcast_to(seg, (length, length))) == seg
    score = mm_tn(out[...], in_[...])
    t, s = iota((length, length), 0), iota((length, length), 1)
    score_f = jnp.where(same & (t >= s), score, 0.0)
    score_r = jnp.where(same & (t <= s), score, 0.0)
    lower = t >= s
    cf, cr = sums[0], sums[1]
    for h in range(heads):
        up = cf[:, h : h + 1] - sums_t[h : h + 1]
        down = sums_t[heads + h : heads + h + 1] - cr[:, h : h + 1]
        x = jnp.exp(jnp.minimum(jnp.where(lower, up, down), 0.0))
        weights[h, :, 0:length] = (x * score_f).astype(BF16)
        weights[h, :, length:] = (x * score_r).astype(BF16)
    wide = spread(heads, channels, channels // heads)[0:heads].astype(F32)
    skips[...] = mm(skip[...], wide, EXACT)


def local_kernel(
    sig, cot, in_, out, segment, cw, cb, table, sums, weights, skips, before, after,
    mixed, base_f, gate_f, base_r, gate_r, out_f, out_r, low, ext, widen,
    *, part, parts,
):
    length, channels = sig.shape
    heads = table.shape[2]
    nstate = in_.shape[0]
    hdim = channels // heads
    margin = cw.shape[1] - 1
    prev, nxt, nf, pr = edge_sums(*neighbours(before, after), table, channels, nstate, heads, margin)
    bs, bc, bi, bo, bseg = prev
    as_, ac, ai, ao, aseg = nxt
    seg = segment[...].astype(F32)
    col_full = jnp.transpose(jnp.broadcast_to(seg, (length, length)))
    col = col_full[:, : 2 * heads]
    cf, cr = sums[0], sums[1]
    total_f = cf[length - 1 : length]
    total_r = sums[2, length - EDGE :][EDGE - 1 : EDGE]
    j = iota((EDGE, 2 * heads), 0)
    early = j < margin
    late = j >= EDGE - margin
    s_first, s_last = aseg[0:1], bseg[EDGE - 1 : EDGE]
    s_beyond, s_ahead = aseg[margin : margin + 1], bseg[EDGE - margin - 1 : EDGE - margin]
    stack = [
        jnp.where(col == s_last, jnp.exp(cf), 0.0),
        jnp.where(col == s_first, jnp.exp(total_r - cr), 0.0),
        jnp.where(col == s_first, jnp.exp(total_f - cf), 0.0),
        jnp.where(col == s_last, jnp.exp(cr), 0.0),
        jnp.where(early & (aseg == s_beyond), jnp.exp(nf[margin - 1 : margin] - nf), 0.0),
        jnp.where(
            late & (bseg == s_ahead), jnp.exp(pr[EDGE - margin : EDGE - margin + 1] - pr), 0.0
        ),
        jnp.where(early & (aseg == s_first), jnp.exp(nf), 0.0),
        jnp.where(late & (bseg == s_last), jnp.exp(pr), 0.0),
        jnp.where(
            j < 4,
            jnp.where(s_first == s_beyond, jnp.exp(nf[margin - 1 : margin]), 0.0),
            jnp.where(s_last == s_ahead, jnp.exp(pr[EDGE - margin : EDGE - margin + 1]), 0.0),
        ),
    ]
    turned = []
    for d in range(margin):
        move = (EDGE - d) % EDGE
        later = pltpu.roll(nf, move, 0) if d else nf
        seg_j = jnp.broadcast_to(aseg, (EDGE, 2 * heads))
        seg_l = pltpu.roll(seg_j, move, 0) if d else seg_j
        ao_d = pltpu.roll(ao, move, 0) if d else ao
        dot = jnp.sum(ai * ao_d, axis=1, keepdims=True)
        stack.append(jnp.where((j + d < margin) & (seg_j == seg_l), jnp.exp(later - nf) * dot, 0.0))
        former = pltpu.roll(pr, d, 0) if d else pr
        seg_j = jnp.broadcast_to(bseg, (EDGE, 2 * heads))
        seg_l = pltpu.roll(seg_j, d, 0) if d else seg_j
        bo_d = pltpu.roll(bo, d, 0) if d else bo
        dot = jnp.sum(bi * bo_d, axis=1, keepdims=True)
        stack.append(
            jnp.where((j - d >= EDGE - margin) & (seg_j == seg_l), jnp.exp(former - pr) * dot, 0.0)
        )
    stack = high_low(jnp.concatenate(stack, axis=0))
    ext[0:EDGE] = bs
    ext[EDGE : EDGE + length] = sig[...].astype(F32)
    ext[EDGE + length :] = as_
    width = channels // parts
    start = part * width
    widen[...] = spread(heads, channels, hdim)
    wide = 128
    first = iota((length, wide), 1) < hdim
    ao_b, bo_b = ao.astype(BF16), bo.astype(BF16)
    for c in range(0, width, wide):
        sl = slice(start + c, start + c + wide)
        to = slice(c, c + wide)
        e = mm(stack, widen[:, sl])
        skip_f, skip_r = skips[0:1, sl], skips[1:2, sl]
        pre = conv(ext, EDGE, length + EDGE, cw[0], cb[0:1, sl], sl, -1)
        sg = jax.nn.sigmoid(pre)
        act_f = (pre * sg)[0:length]
        slope_f = sg * (1.0 + pre * (1.0 - sg))
        pre = conv(ext, 0, length + EDGE, cw[1], cb[1:2, sl], sl, 1)
        sg = jax.nn.sigmoid(pre)
        act_r = (pre * sg)[EDGE:]
        slope_r = sg * (1.0 + pre * (1.0 - sg))
        act = jnp.concatenate([act_f.astype(BF16), act_r.astype(BF16)], axis=0)
        ct16 = cot[:, sl]
        ct = ct16.astype(F32)
        forth, back = [], []
        for k in range(wide // hdim):
            h = (start + c) // hdim + k
            m = weights[h]
            forth.append(mm(m, act))
            back.append(mm_tn(m, ct16))
        mixed[:, to] = jnp.where(first, forth[0], forth[1]) + skip_f * act_f + skip_r * act_r
        here_f = jnp.where(first, back[0][0:length], back[1][0:length]) + skip_f * ct
        here_r = jnp.where(first, back[0][length:], back[1][length:]) + skip_r * ct
        at = 4 * length
        ac_c, bc_c = ac[:, sl], bc[:, sl]
        row = iota((EDGE, wide), 0)
        beyond = jnp.where(row < margin, skip_f * ac_c, 0.0)
        ahead = jnp.where(row >= EDGE - margin, skip_r * bc_c, 0.0)
        for d in range(margin):
            k = at + (5 + 2 * d) * EDGE
            moved = pltpu.roll(ac_c, (EDGE - d) % EDGE, 0) if d else ac_c
            beyond += e[k : k + EDGE] * moved
            moved = pltpu.roll(bc_c, d, 0) if d else bc_c
            ahead += e[k + EDGE : k + 2 * EDGE] * moved
        out_f[:, to] = e[0:length]
        out_r[:, to] = e[length : 2 * length]
        base_f[0:length, to] = here_f * slope_f[0:length]
        base_f[length:, to] = beyond * slope_f[length:]
        gate_f[0:length, to] = e[2 * length : 3 * length] * slope_f[0:length]
        gate_f[length:, to] = e[at : at + EDGE] * slope_f[length:]
        base_r[EDGE:, to] = here_r * slope_r[EDGE:]
        base_r[0:EDGE, to] = ahead * slope_r[0:EDGE]
        gate_r[EDGE:, to] = e[3 * length : 4 * length] * slope_r[EDGE:]
        gate_r[0:EDGE, to] = e[at + EDGE : at + 2 * EDGE] * slope_r[0:EDGE]
        low[0:nstate, to] = mm_tn(ao_b, (ac_c * e[at + 2 * EDGE : at + 3 * EDGE]).astype(BF16))
        low[nstate : 2 * nstate, to] = mm_tn(
            bo_b, (bc_c * e[at + 3 * EDGE : at + 4 * EDGE]).astype(BF16)
        )
        low[2 * nstate :, to] = e[at + 4 * EDGE : at + 5 * EDGE]


def finish_kernel(*refs, outer, parts):
    entries = in_order(refs[:outer], THIRD)
    locals_ = [refs[outer + 8 * p : outer + 8 * (p + 1)] for p in range(parts)]
    in_, out, before, after, cw, mixed, grad, state, df, dr = refs[outer + 8 * parts :]
    length, channels = mixed.shape
    nstate = in_.shape[0]
    me = lax.axis_index("outer")
    width = channels // outer
    for r in range(outer):
        state[:, pl.ds(pl.multiple_of((me ^ r) * width, 128), width)] = entries[r][...]
    per = channels // parts
    query, key = out[...], in_[...]
    at = 2 * channels
    ahead, beyond = neighbours(before.at[:, at : at + 128], after.at[:, at : at + 128])
    ahead, beyond = ahead[:, :nstate].astype(BF16), beyond[:, :nstate].astype(BF16)
    lags = cw.shape[1]
    wide = 256
    for c in range(0, channels, wide):
        p, off = divmod(c, per)
        loc, base_f, gate_f, base_r, gate_r, out_f, out_r, low = locals_[p]
        to = slice(off, off + wide)
        sl = slice(c, c + wide)
        s = state[:, sl]
        mixed[:, sl] = (
            loc[:, to]
            + out_f[:, to] * mm_tn(query, s[0:nstate])
            + out_r[:, to] * mm_tn(query, s[2 * nstate : 3 * nstate])
        ).astype(BF16)
        s_br, s_bf = s[nstate : 2 * nstate], s[3 * nstate :]
        h_f = low[0:nstate, to] + low[2 * nstate : 2 * nstate + 1, to] * s_bf.astype(F32)
        h_r = low[nstate : 2 * nstate, to] + low[2 * nstate + 4 : 2 * nstate + 5, to] * s_br.astype(F32)
        df[0:length] = base_f[0:length, to] + gate_f[0:length, to] * mm_tn(key, h_f.astype(BF16))
        df[length:] = base_f[length:, to] + gate_f[length:, to] * mm(beyond, s_bf)
        dr[EDGE:] = base_r[EDGE:, to] + gate_r[EDGE:, to] * mm_tn(key, h_r.astype(BF16))
        dr[0:EDGE] = base_r[0:EDGE, to] + gate_r[0:EDGE, to] * mm(ahead, s_br)
        total = jnp.zeros((length, wide), F32)
        for lag in range(lags):
            total += cw[0, lag : lag + 1, sl] * df[lag : lag + length]
            total += cw[1, lag : lag + 1, sl] * dr[EDGE - lag : EDGE - lag + length]
        grad[:, sl] = total.astype(BF16)


def order(size, head):
    first = [r for r in head if r < size]
    return first + [r for r in reversed(range(1, size)) if r not in first]


def lay(arrays, head):
    return [arrays[0]] + [arrays[r] for r in order(len(arrays), head)]


def in_order(refs, head):
    found = dict(zip([0] + order(len(refs), head), refs))
    return [found[r] for r in range(len(refs))]


def params():
    return pltpu.CompilerParams(vmem_limit_bytes=VMEM)


def cost(flops, size):
    return pl.CostEstimate(flops=flops, bytes_accessed=size, transcendentals=0)


def on_device(
    signal, in_coeff, out_coeff, cotangent, conv_weight, conv_bias, skip_gain, decay_table,
    bucket, segment, *, outer, inner,
):
    length, channels = signal.shape
    heads = skip_gain.shape[1]
    nstate = in_coeff.shape[1]
    axes = ("inner", "outer")
    count = outer * inner
    bucket = bucket.reshape(1, length)
    segment = segment.reshape(1, length)
    sds = jax.ShapeDtypeStruct
    width = channels // outer
    pay = 4 * nstate + 4 * EDGE
    far = 2 * nstate + 3 * EDGE
    in_t, out_t = in_coeff.T, out_coeff.T
    steps = tuple(reversed(range(outer)))
    small = (bucket, segment, decay_table, conv_weight, conv_bias, in_t, out_t)
    operands = [
        pltpu.with_memory_space_constraint(a, pltpu.HBM) for a in (*small, signal, cotangent)
    ]
    *blocks, sums, sums_t = pl.pallas_call(
        functools.partial(begin_kernel, outer=outer, steps=steps),
        name="begin",
        in_specs=[pl.BlockSpec(memory_space=pltpu.HBM)] * len(operands),
        out_shape=[sds((pay, width), BF16)] * outer
        + [sds((3, length, 2 * heads), F32), sds((2 * heads, length), F32)],
        scratch_shapes=[pltpu.VMEM(a.shape, a.dtype) for a in small]
        + [pltpu.VMEM((length, channels), BF16)] * 2
        + [
            pltpu.VMEM((length + 2 * EDGE, width), F32),
            pltpu.VMEM((8 * heads, length), F32),
            pltpu.SemaphoreType.DMA((len(small) + 2 * outer,)),
        ],
        compiler_params=params(),
        cost_estimate=cost(10**8, 2**20),
    )(*operands)
    blocks = blocks[::-1]

    def swap(array, axis, size, r):
        return lax.ppermute(array, axis, [(i, i ^ r) for i in range(size)])

    def exchange(arrays, axis, size):
        got = {r: swap(arrays[r], axis, size, r) for r in reversed(range(1, size))}
        return [got[r] for r in range(1, size)]

    blocks = [blocks[0], *exchange(blocks, "outer", outer)]
    line = 2 * channels + 512
    late_bucket, _ = lax.optimization_barrier((bucket, sums))
    near_rows, next_rows = pl.pallas_call(
        edges_kernel,
        name="edges",
        out_shape=[sds((EDGE, line), BF16)] * 2,
        compiler_params=params(),
        cost_estimate=cost(10**6, 2**18),
    )(signal, cotangent, in_t, out_t, late_bucket, segment)
    before = lax.ppermute(near_rows, "outer", [(i, i ^ 1) for i in range(outer)])
    weights, skips = pl.pallas_call(
        weights_kernel,
        name="weights",
        out_shape=[sds((heads, length, 2 * length), BF16), sds((2, channels), F32)],
        compiler_params=params(),
        cost_estimate=cost(10**8, 2**21),
    )(in_t, out_t, segment, skip_gain, sums, sums_t)
    blocks[0], weights = lax.optimization_barrier((blocks[0], weights))
    pairs = [(i, i + 1) for i in range(1, count - 1, 2)]
    after = lax.ppermute(next_rows, axes, pairs + [(j, i) for i, j in pairs])
    parts = 2

    def local(part):
        per = channels // parts
        both_rows = length + EDGE
        return pl.pallas_call(
            functools.partial(local_kernel, part=part, parts=parts),
            name=f"local{part}",
            out_shape=[
                sds((length, per), F32),
                sds((both_rows, per), F32),
                sds((both_rows, per), F32),
                sds((both_rows, per), F32),
                sds((both_rows, per), F32),
                sds((length, per), F32),
                sds((length, per), F32),
                sds((2 * nstate + EDGE, per), F32),
            ],
            scratch_shapes=[
                pltpu.VMEM((length + 2 * EDGE, channels), F32),
                pltpu.VMEM((2 * heads, channels), BF16),
            ],
            compiler_params=params(),
            cost_estimate=cost(4 * 10**8, 2**22),
        )(
            signal, cotangent, in_t, out_t, segment, conv_weight, conv_bias, decay_table, sums,
            weights, skips, before, after,
        )

    locals_ = [local(p) for p in range(parts)]
    totals = pl.pallas_call(
        functools.partial(totals_kernel, outer=outer, inner=inner, nstate=nstate),
        name="totals",
        out_shape=[sds((far, width), BF16)] * (inner - 1),
        scratch_shapes=[pltpu.VMEM((outer, pay, width), BF16)],
        compiler_params=params(),
        cost_estimate=cost(10**6, 2**19),
    )(*lay(blocks, FIRST), conv_weight, conv_bias)
    totals = exchange([None, *totals], "inner", inner)
    entries = pl.pallas_call(
        functools.partial(entries_kernel, outer=outer, inner=inner, nstate=nstate),
        name="entries",
        out_shape=[sds((4 * nstate, width), BF16)] * outer,
        scratch_shapes=[
            pltpu.VMEM((outer, pay, width), BF16),
            pltpu.VMEM((inner, far, width), F32),
            pltpu.VMEM((outer, 4 * nstate, width), BF16),
        ],
        compiler_params=params(),
        cost_estimate=cost(10**6, 2**19),
    )(*lay(blocks, FIRST), *lay([None, *totals], SECOND)[1:], conv_weight, conv_bias)
    entries = [entries[0], *exchange(entries, "outer", outer)]
    return pl.pallas_call(
        functools.partial(finish_kernel, outer=outer, parts=parts),
        name="finish",
        out_shape=[sds((length, channels), BF16)] * 2,
        scratch_shapes=[
            pltpu.VMEM((4 * nstate, channels), BF16),
            pltpu.VMEM((length + EDGE, 256), F32),
            pltpu.VMEM((length + EDGE, 256), F32),
        ],
        compiler_params=params(),
        cost_estimate=cost(10**8, 2**22),
    )(*lay(entries, THIRD), *[a for group in locals_ for a in group], in_t, out_t, before, after, conv_weight)


def solution(mesh):
    rows = P(("groups", "inner", "outer"), None)
    flat = P(("groups", "inner", "outer"))
    return jax.shard_map(
        functools.partial(on_device, outer=mesh.shape["outer"], inner=mesh.shape["inner"]),
        mesh=mesh,
        in_specs=(rows, rows, rows, rows, P(), P(), P(), P(), flat, flat),
        out_specs=(rows, rows),
        check_vma=False,
    )
```

```python
import functools

import jax
import jax.numpy as jnp
from jax import lax
from jax.experimental import pallas as pl
from jax.experimental.pallas import tpu as pltpu
from jax.sharding import PartitionSpec as P

F32, BF16 = jnp.float32, jnp.bfloat16
EXACT = lax.Precision.HIGHEST
EDGE = 8
VMEM = 14 * 2**20
NEVER = -1e4
FIRST, SECOND, THIRD = (2, 1, 3), (3, 2, 1), (2, 1, 3)


def mm(a, b, precision=None):
    return lax.dot_general(
        a, b, (((1,), (0,)), ((), ())), precision=precision, preferred_element_type=F32
    )


def mm_tn(a, b, precision=None):
    return lax.dot_general(
        a, b, (((0,), (0,)), ((), ())), precision=precision, preferred_element_type=F32
    )


def mm_nt(a, b, precision=None):
    return lax.dot_general(
        a, b, (((1,), (1,)), ((), ())), precision=precision, preferred_element_type=F32
    )


def iota(shape, dim):
    return lax.broadcasted_iota(jnp.int32, shape, dim)


def twice(heads):
    col = iota((heads, 2 * heads), 1)
    col = jnp.where(col < heads, col, col - heads)
    return (iota((heads, 2 * heads), 0) == col).astype(F32)


def spread(heads, lanes, hdim, start=0):
    row = iota((2 * heads, lanes), 0)
    row = jnp.where(row < heads, row, row - heads)
    low = row * hdim
    col = iota((2 * heads, lanes), 1) + start
    return ((col >= low) & (col < low + hdim)).astype(BF16)


def high_low(x):
    high = x.astype(BF16).astype(F32)
    return jnp.where(iota(x.shape, 1) < x.shape[1] // 2, high, x - high).astype(BF16)


def three(x):
    high = x.astype(BF16)
    rest = x - high.astype(F32)
    mid = rest.astype(BF16)
    return jnp.concatenate([high, mid, (rest - mid.astype(F32)).astype(BF16)], axis=0)


def one_hot(column, size):
    return (column == iota((column.shape[0], size), 1).astype(column.dtype)).astype(F32)


def edges_kernel(sig, cot, in_t, out_t, bucket, segment, near, next_):
    length = bucket.shape[1]
    channels = sig.shape[1]

    bcol = jnp.transpose(jnp.broadcast_to(bucket[...].astype(F32), (length, length)))
    scol = jnp.transpose(jnp.broadcast_to(segment[...].astype(F32), (length, length)))
    j, t = iota((EDGE, length), 0), iota((EDGE, length), 1)
    even = lax.axis_index("outer") % 2 == 0

    def ends(place, value):
        final, first = value(length - EDGE), value(0)
        here = jnp.full(final.shape, even)
        columns = slice(place, place + final.shape[1])
        near[:, columns] = jnp.where(here, final, first).astype(BF16)
        next_[:, columns] = jnp.where(here, first, final).astype(BF16)

    def rows_of(ref):
        def get(row):
            start = row // 16 * 16
            return ref[start : start + 16].astype(F32)[row - start : row - start + EDGE]

        return get

    for k, ref in enumerate((sig, cot)):
        ends(k * channels, rows_of(ref))
    for k, ref in enumerate((in_t, out_t)):
        ends(2 * channels + 128 * k, lambda row: mm_nt((t == j + row).astype(BF16), ref[...]))
    for k, full in enumerate((bcol, scol)):
        ends(2 * channels + 256 + 128 * k, lambda row: full[row : row + EDGE, :128])


def neighbours(near, next_):
    a, b = near[...].astype(F32), next_[...].astype(F32)
    even = jnp.full(a.shape, lax.axis_index("outer") % 2 == 0)
    return jnp.where(even, b, a), jnp.where(even, a, b)


def edge_parts(x, channels, state):
    return (
        x[:, :channels].astype(F32),
        x[:, channels : 2 * channels].astype(F32),
        x[:, 2 * channels : 2 * channels + state].astype(F32),
        x[:, 2 * channels + 128 : 2 * channels + 128 + state].astype(F32),
        x[:, 2 * channels + 256 : 2 * channels + 257].astype(F32),
        x[:, 2 * channels + 384 : 2 * channels + 385].astype(F32),
    )


def conv(ext, start, rows, weight, bias, sl, step):
    total = bias
    for lag in range(weight.shape[0]):
        at = start + step * lag
        total = total + weight[lag : lag + 1, sl] * ext[at : at + rows, sl]
    return total


def begin_kernel(*refs, outer, steps):
    bucket_h, segment_h, table_h, cw_h, cb_h, in_h, out_h, sig_h, cot_h = refs[:9]
    count = len(steps)
    outs = refs[9 : 9 + count]
    sums, sums_t = refs[9 + count : 11 + count]
    bucket, segment, table, cw, cb, in_t, out_t, sig, cot, ext, fades_t, sems = refs[11 + count :]
    near = (bucket, segment, table, cw, cb, in_t, out_t)
    me = lax.axis_index("outer")
    length = segment.shape[1]
    heads = table.shape[2]
    rows = table.shape[1]
    nstate = in_t.shape[0]
    channels = sig.shape[1]
    width = channels // outer
    hdim = channels // heads
    margin = cw.shape[1] - 1
    starts = [pl.multiple_of((me ^ r) * width, 128) for r in steps]
    small_in = [
        pltpu.make_async_copy(a, b, sems.at[k]) for k, (a, b) in enumerate(zip(refs[:7], near))
    ]
    large_in = []
    for n, (a, b) in enumerate(((sig_h, sig), (cot_h, cot))):
        large_in.append(pltpu.make_async_copy(a, b, sems.at[7 + n]))
    for copy in large_in + small_in:
        copy.start()
    for copy in small_in + large_in:
        copy.wait()
    last, tail = length - 1, length - margin
    hot = (bucket[...] == iota((rows, length), 0)).astype(BF16)
    hot = jnp.concatenate([hot, hot, hot], axis=0)
    row, col = iota((length, length), 0), iota((length, length), 1)
    counts = mm_nt((row >= col).astype(BF16), hot).astype(BF16)
    parts_f, parts_r = three(table[0]), three(table[1])
    dup = twice(heads).astype(BF16)
    cf = mm(counts, mm(parts_f, dup).astype(BF16))
    ci = mm(counts, mm(parts_r, dup).astype(BF16))
    lanes4 = 8 * heads
    kind = iota((heads, lanes4), 1) // (2 * heads)
    same_head = iota((heads, lanes4), 0) == iota((heads, lanes4), 1) % heads
    sign = jnp.where(kind < 2, -1.0, 1.0)
    pick_f = jnp.where(same_head & ((kind == 0) | (kind == 3)), sign, 0.0).astype(BF16)
    pick_r = jnp.where(same_head & ((kind == 1) | (kind == 2)), sign, 0.0).astype(BF16)
    quad = mm(counts, (mm(parts_f, pick_f) + mm(parts_r, pick_r)).astype(BF16))
    t, kind = iota((length, lanes4), 0), iota((length, lanes4), 1) // (2 * heads)
    reverse = (kind == 1) | (kind == 2)
    before = jnp.where(t == 0, 0.0, pltpu.roll(quad, 1, 0))
    quad = jnp.where(reverse, before, quad)
    cr = jnp.where(iota(ci.shape, 0) == 0, 0.0, pltpu.roll(ci, 1, 0))
    sums[0], sums[1], sums[2] = cf, cr, ci
    counts_t = mm(hot, (row <= col).astype(BF16))
    sums_t[0:heads] = mm_tn(parts_f, counts_t.astype(BF16))
    sums_t[heads : 2 * heads] = mm_tn(parts_r, (counts_t - hot.astype(F32)).astype(BF16))
    seg = segment[...].astype(F32)
    seg_full = jnp.transpose(jnp.broadcast_to(seg, (length, length)))
    seg_col = seg_full[:, : 2 * heads]

    def at(place):
        return seg[:, place : place + 1]

    def by_kind(a, b, c, d, like):
        k = kind[: like.shape[0]] if like.shape[0] > 1 else kind[0:1]
        return jnp.where(k == 0, a, jnp.where(k == 1, b, jnp.where(k == 2, c, d)))

    line = quad[0:1]
    anchor = by_kind(quad[last:], quad[tail : tail + 1], line, quad[margin - 1 : margin], line)
    owner = by_kind(at(last), at(tail - 1), at(0), at(margin), line)
    first, end = jnp.where(reverse, 0, margin), jnp.where(reverse, tail, length)
    inside = (t >= first) & (t < end) & (seg_full[:, :lanes4] == owner)
    fades = jnp.where(inside, jnp.exp(quad - anchor), 0.0)
    fades_t[...] = jnp.transpose(fades)
    total_f, total_r = cf[last:], ci[last:]
    j = iota((EDGE, 2 * heads), 0)
    early, late = j < margin, j >= EDGE - margin
    at_tail = cr[tail : tail + 1]
    logs = (
        total_f,
        at_tail,
        jnp.where(at(tail - 1) == at(last), total_r - at_tail, NEVER),
        total_r,
        total_f - cf[margin - 1 : margin],
        jnp.where(at(0) == at(margin), cf[margin - 1 : margin], NEVER),
    )
    keeps = jnp.zeros((EDGE, 2 * heads), F32)
    for k, value in enumerate(logs):
        keeps = jnp.where(j == k, value, keeps)
    cf_0, cr_l = cf[0:EDGE], cr[length - EDGE :]
    seg_0, seg_l = seg_col[0:EDGE], seg_col[length - EDGE :]
    act_fade = jnp.where(
        early & (seg_0 == at(last)),
        jnp.exp(total_f - cf_0),
        jnp.where(late & (seg_l == at(0)), jnp.exp(cr_l), 0.0),
    )
    cot_fade = jnp.where(
        early & (seg_0 == at(0)),
        jnp.exp(cf_0),
        jnp.where(late & (seg_l == at(last)), jnp.exp(total_r - cr_l), 0.0),
    )
    small = high_low(jnp.concatenate([keeps, act_fade, cot_fade], axis=0))
    keys, queries = in_t[...], out_t[...]
    keys_f, queries_f = keys.astype(F32), queries.astype(F32)
    k, s = iota((EDGE, length), 0), iota((EDGE, length), 1)
    lines = jnp.concatenate([keys, keys, queries, queries], axis=0)
    firsts = mm_nt(((k < margin) & (s == k)).astype(BF16), lines)
    finals = mm_nt(((k >= EDGE - margin) & (s == k + length - EDGE)).astype(BF16), lines)
    group = iota(firsts.shape, 1) // nstate
    coeff = jnp.where(group % 2 == 0, firsts, finals)
    coeff = jnp.where(
        k == 3,
        jnp.where(
            group == 0,
            at(0),
            jnp.where(group == 1, at(margin), jnp.where(group == 2, at(tail - 1), at(last))),
        ),
        coeff,
    )
    if width > coeff.shape[1]:
        coeff = jnp.concatenate(
            [coeff, jnp.zeros((EDGE, width - coeff.shape[1]), F32)], axis=1
        )
    ext[0:EDGE] = jnp.zeros((EDGE, width), F32)
    ext[EDGE + length :] = jnp.zeros((EDGE, width), F32)
    row = iota((EDGE, width), 0)
    base = 4 * nstate
    for n, start in enumerate(starts):
        lanes = pl.ds(start, width)
        widen = spread(heads, width, hdim, start)
        ext[EDGE : EDGE + length] = sig[:, lanes].astype(F32)
        acts = []
        for side in range(2):
            pre = cb[side : side + 1, lanes]
            for lag in range(margin + 1):
                first = EDGE + (lag if side else -lag)
                pre = pre + cw[side, lag : lag + 1, lanes] * ext[first : first + length]
            acts.append((pre * jax.nn.sigmoid(pre)).astype(BF16))
        for c in range(0, width, 128):
            head = (me ^ steps[n]) * (width // hdim) + c // hdim
            pair = slice(c, c + 128)

            def faded(kind, rows):
                parts = [
                    rows * fades_t[pl.ds(2 * heads * kind + head + k, 1)]
                    for k in range(128 // hdim)
                ]
                return jnp.concatenate(parts, axis=0).astype(BF16)

            def own(rows):
                which = iota((nstate, 128), 1) // hdim
                total = rows[0:nstate]
                for k in range(1, 128 // hdim):
                    total = jnp.where(which == k, rows[k * nstate : (k + 1) * nstate], total)
                return total.astype(BF16)

            outs[n][0:nstate, pair] = own(mm(faded(0, keys_f), acts[0][:, pair]))
            outs[n][2 * nstate : 3 * nstate, pair] = own(mm(faded(2, keys_f), acts[1][:, pair]))
            two = jnp.concatenate([faded(1, queries_f), faded(3, queries_f)], axis=0)
            two = mm(two, cot[:, pl.ds(start + c, 128)])
            half = two.shape[0] // 2
            outs[n][nstate : 2 * nstate, pair] = own(two[:half])
            outs[n][3 * nstate : 4 * nstate, pair] = own(two[half:])
        e = mm(small, widen)

        def tile(ref):
            top = ref[0:16, lanes].astype(F32)[0:EDGE]
            return jnp.where(row < 4, top, ref[length - 16 :, lanes].astype(F32)[EDGE:])

        def spare(rows, first):
            filled = jnp.where(row == 3, e[first : first + 1], rows)
            return jnp.where(row == 4, e[first + 1 : first + 2], filled)

        outs[n][base : base + 16] = jnp.concatenate(
            [spare(tile(sig), 0), spare(e[EDGE : 2 * EDGE], 2)], axis=0
        ).astype(BF16)
        outs[n][base + 16 : base + 32] = jnp.concatenate(
            [spare(tile(cot) * e[2 * EDGE :], 4), coeff], axis=0
        ).astype(BF16)


def edge_sums(before, after, table, channels, state, heads, margin):
    dup = twice(heads)
    table_f = mm(table[0], dup, EXACT)
    table_r = mm(table[1], dup, EXACT)
    bs, bc, bi, bo, bb, bseg = edge_parts(before, channels, state)
    as_, ac, ai, ao, ab, aseg = edge_parts(after, channels, state)
    tri = (iota((EDGE, EDGE), 0) >= iota((EDGE, EDGE), 1)).astype(F32)
    rev = (iota((EDGE, EDGE), 0) <= iota((EDGE, EDGE), 1)).astype(F32)
    rows = table.shape[1]
    nf = mm(mm(tri, one_hot(ab, rows)), table_f, EXACT)
    pr = mm(mm(rev, one_hot(bb, rows)), table_r, EXACT)
    return (bs, bc, bi, bo, bseg), (as_, ac, ai, ao, aseg), nf, pr


class Block:
    def __init__(self, ref, nstate):
        x = ref.astype(F32)
        h = 4 * nstate
        self.f, self.br = x[0:nstate], x[nstate : 2 * nstate]
        self.r, self.bf = x[2 * nstate : 3 * nstate], x[3 * nstate : h]
        self.sig, self.fade = x[h : h + 8], x[h + 8 : h + 16]
        self.cot, self.coeff = x[h + 16 : h + 24], x[h + 24 : h + 32]
        self.keep_f, self.near_br = self.sig[3:4], self.sig[4:5]
        self.far_br, self.keep_r = self.fade[3:4], self.fade[4:5]
        self.near_bf, self.far_bf = self.cot[3:4], self.cot[4:5]
        self.seg_first, self.seg_early = self.coeff[3:4, 0:1], self.coeff[3:4, nstate : nstate + 1]
        self.seg_late = self.coeff[3:4, 2 * nstate : 2 * nstate + 1]
        self.seg_last = self.coeff[3:4, 3 * nstate : 3 * nstate + 1]


def alike(a, b):
    return jnp.where(a == b, 0.0, NEVER)


def act_rows(before, here, after, cw, cb, lanes):
    row = iota(here.shape, 0)
    pre_f = cb[0:1, lanes] + cw[0, 0:1, lanes] * here
    pre_r = cb[1:2, lanes] + cw[1, 0:1, lanes] * here
    for lag in range(1, cw.shape[1]):
        moved = pltpu.roll(jnp.where(row >= EDGE - lag, before, here), lag, 0)
        pre_f += cw[0, lag : lag + 1, lanes] * moved
        moved = pltpu.roll(jnp.where(row < lag, after, here), EDGE - lag, 0)
        pre_r += cw[1, lag : lag + 1, lanes] * moved
    pre = jnp.where(row < 4, pre_f, pre_r)
    return pre * jax.nn.sigmoid(pre)


def edge_states(act, fade, cot, coeff, nstate):
    coeff = coeff.astype(BF16)
    row = iota(cot.shape, 0)
    edge = (row < 3) | (row > 4)
    a = mm_tn(coeff[:, : 2 * nstate], jnp.where(edge, act * fade, 0.0).astype(BF16))
    b = mm_tn(coeff[:, 2 * nstate : 4 * nstate], jnp.where(edge, cot, 0.0).astype(BF16))
    return a[:nstate], a[nstate:], b[:nstate], b[nstate:]


def totals_kernel(*refs, outer, inner, nstate):
    blocks, (cw, cb), outs, held = in_order(refs[:outer], FIRST), refs[outer : outer + 2], refs[outer + 2 : -1], refs[-1]
    me = lax.axis_index("outer")
    place = lax.axis_index("inner")
    width = blocks[0].shape[1]
    lanes = pl.ds(pl.multiple_of(me * width, 128), width)
    for r in range(outer):
        held[me ^ r] = blocks[r][...]
    b = [Block(held[k], nstate) for k in range(outer)]
    none = jnp.zeros((EDGE, width), F32)
    low = []
    for k in range(outer):
        before = b[k - 1].sig if k else none
        after = b[k + 1].sig if k < outer - 1 else none
        act = act_rows(before, b[k].sig, after, cw, cb, lanes)
        low.append(edge_states(act, b[k].fade, b[k].cot, b[k].coeff, nstate))
    end = outer - 1
    f, x = b[0].f, b[0].br
    keep_f, keep_br = jnp.zeros((1, width), F32), b[0].near_br
    for k in range(1, outer):
        y = low[k - 1][3] + jnp.exp(b[k - 1].far_br) * x
        factor = b[k].near_br + alike(b[k - 1].seg_last, b[k].seg_late)
        x = b[k].br + jnp.exp(factor) * y
        keep_br = keep_br + b[k - 1].far_br + factor
        factor = b[k].keep_f + alike(b[k - 1].seg_last, b[k].seg_last)
        f = b[k].f + low[k][0] + jnp.exp(factor) * f
        keep_f = keep_f + factor
    r, z = b[end].r, b[end].bf
    keep_r, keep_bf = jnp.zeros((1, width), F32), b[end].near_bf
    for k in range(end - 1, -1, -1):
        y = low[k + 1][2] + jnp.exp(b[k + 1].far_bf) * z
        factor = b[k].near_bf + alike(b[k + 1].seg_first, b[k].seg_early)
        z = b[k].bf + jnp.exp(factor) * y
        keep_bf = keep_bf + b[k + 1].far_bf + factor
        factor = b[k].keep_r + alike(b[k + 1].seg_first, b[k].seg_first)
        r = b[k].r + low[k][1] + jnp.exp(factor) * r
        keep_r = keep_r + factor
    row = iota((EDGE, width), 0)
    half = row < 4

    def spare(rows, first, second):
        return jnp.where(row == 3, first, jnp.where(row == 4, second, rows))

    def named(rows, *values):
        group = iota(rows.shape, 1) // nstate
        for k, value in enumerate(values):
            rows = jnp.where((row == 3) & (group == k), value, rows)
        return rows

    sig = jnp.where(half, b[0].sig, b[end].sig)
    coeff = jnp.where(half, b[0].coeff, b[end].coeff)
    up = jnp.concatenate(
        [
            f,
            x,
            spare(sig, keep_f, b[0].keep_f),
            named(coeff, b[0].seg_last, b[0].seg_late, b[end].seg_last),
            spare(jnp.where(half, b[0].fade, b[end].cot), keep_br, b[end].far_br),
        ],
        axis=0,
    )
    down = jnp.concatenate(
        [
            r,
            z,
            spare(sig, keep_r, b[end].keep_r),
            named(coeff, b[end].seg_first, b[end].seg_early, b[0].seg_first),
            spare(jnp.where(half, b[0].cot, b[end].fade), keep_bf, b[0].far_bf),
        ],
        axis=0,
    )
    for r in range(1, inner):
        towards = jnp.full(up.shape, place ^ r, jnp.int32) > place
        outs[r - 1][...] = jnp.where(towards, up, down).astype(BF16)


def entries_kernel(*refs, outer, inner, nstate):
    blocks = in_order(refs[:outer], FIRST)
    others = in_order(refs[outer - 1 : outer + inner - 1], SECOND)[1:]
    cw, cb = refs[outer + inner - 1 : outer + inner + 1]
    outs = refs[outer + inner + 1 : -3]
    held, far, entry = refs[-3:]
    me = lax.axis_index("outer")
    place = lax.axis_index("inner")
    width = blocks[0].shape[1]
    lanes = pl.ds(pl.multiple_of(me * width, 128), width)
    for r in range(outer):
        held[me ^ r] = blocks[r][...]
    n, h = nstate, 2 * nstate
    far[place] = jnp.zeros(far.shape[1:], F32)
    for r in range(1, inner):
        far[place ^ r] = others[r - 1][...].astype(F32)
    zero = jnp.zeros((n, width), F32)
    none = jnp.zeros((EDGE, width), F32)
    line = jnp.zeros((1, 1), F32)

    def step(carry, index, wanted, upward):
        state, x, y, edge, seg = carry
        p = far[index]
        sig, coeff, rows = (p[h + k : h + k + EDGE] for k in (0, EDGE, 2 * EDGE))
        segs = [coeff[3:4, k * n : k * n + 1] for k in range(3)]
        if upward:
            act = act_rows(edge, sig, none, cw, cb, lanes)
            first, _, _, second = edge_states(act, rows, rows, coeff, n)
        else:
            act = act_rows(none, sig, edge, cw, cb, lanes)
            _, first, second, _ = edge_states(act, rows, rows, coeff, n)
        inside = jnp.exp(sig[4:5] + alike(seg, segs[0]))
        new = p[0:n] + jnp.exp(sig[3:4]) * (first + inside * state)
        new_x = p[n:h] + jnp.exp(rows[3:4] + alike(seg, segs[1])) * y
        new_y = second + jnp.exp(rows[4:5]) * new_x
        return tuple(
            jnp.where(jnp.full(b.shape, wanted), b, a)
            for a, b in zip(carry, (new, new_x, new_y, sig, segs[2]))
        )

    up = down = (zero, zero, zero, none, line)
    for k in range(inner - 1):
        up = step(up, k, k < place, True)
        back = inner - 1 - k
        down = step(down, back, back > place, False)
    f, x, y, edge_up, seg_up = up
    r, z, w, edge_down, seg_down = down
    b = [Block(held[k], nstate) for k in range(outer)]
    low = []
    for k in range(outer):
        before = b[k - 1].sig if k else edge_up
        after = b[k + 1].sig if k < outer - 1 else edge_down
        act = act_rows(before, b[k].sig, after, cw, cb, lanes)
        low.append(edge_states(act, b[k].fade, b[k].cot, b[k].coeff, nstate))
    for k in range(outer):
        entry[k, 0:h] = jnp.concatenate([f, x], axis=0).astype(BF16)
        if k == outer - 1:
            break
        before = b[k - 1].seg_last if k else seg_up
        f = b[k].f + low[k][0] + jnp.exp(b[k].keep_f + alike(before, b[k].seg_last)) * f
        x = b[k].br + jnp.exp(b[k].near_br + alike(before, b[k].seg_late)) * y
        y = low[k][3] + jnp.exp(b[k].far_br) * x
    for k in range(outer - 1, -1, -1):
        entry[k, h : 2 * h] = jnp.concatenate([r, z], axis=0).astype(BF16)
        if k == 0:
            break
        after = b[k + 1].seg_first if k < outer - 1 else seg_down
        r = b[k].r + low[k][1] + jnp.exp(b[k].keep_r + alike(after, b[k].seg_first)) * r
        z = b[k].bf + jnp.exp(b[k].near_bf + alike(after, b[k].seg_early)) * w
        w = low[k][2] + jnp.exp(b[k].far_bf) * z
    for r_ in range(outer):
        outs[r_][...] = entry[me ^ r_]


def weights_kernel(in_, out, segment, skip, sums, sums_t, weights, skips):
    length = segment.shape[1]
    heads = skip.shape[1]
    channels = skips.shape[1]
    seg = segment[...].astype(F32)
    same = jnp.transpose(jnp.broadcast_to(seg, (length, length))) == seg
    score = mm_tn(out[...], in_[...])
    t, s = iota((length, length), 0), iota((length, length), 1)
    score_f = jnp.where(same & (t >= s), score, 0.0)
    score_r = jnp.where(same & (t <= s), score, 0.0)
    lower = t >= s
    cf, cr = sums[0], sums[1]
    for h in range(heads):
        up = cf[:, h : h + 1] - sums_t[h : h + 1]
        down = sums_t[heads + h : heads + h + 1] - cr[:, h : h + 1]
        x = jnp.exp(jnp.minimum(jnp.where(lower, up, down), 0.0))
        weights[h, :, 0:length] = (x * score_f).astype(BF16)
        weights[h, :, length:] = (x * score_r).astype(BF16)
    wide = spread(heads, channels, channels // heads)[0:heads].astype(F32)
    skips[...] = mm(skip[...], wide, EXACT)


def local_kernel(
    sig, cot, in_, out, segment, cw, cb, table, sums, weights, skips, before, after,
    mixed, base_f, gate_f, base_r, gate_r, out_f, out_r, low, ext, widen,
    *, part, parts,
):
    length, channels = sig.shape
    heads = table.shape[2]
    nstate = in_.shape[0]
    hdim = channels // heads
    margin = cw.shape[1] - 1
    prev, nxt, nf, pr = edge_sums(*neighbours(before, after), table, channels, nstate, heads, margin)
    bs, bc, bi, bo, bseg = prev
    as_, ac, ai, ao, aseg = nxt
    seg = segment[...].astype(F32)
    col_full = jnp.transpose(jnp.broadcast_to(seg, (length, length)))
    col = col_full[:, : 2 * heads]
    cf, cr = sums[0], sums[1]
    total_f = cf[length - 1 : length]
    total_r = sums[2, length - EDGE :][EDGE - 1 : EDGE]
    j = iota((EDGE, 2 * heads), 0)
    early = j < margin
    late = j >= EDGE - margin
    s_first, s_last = aseg[0:1], bseg[EDGE - 1 : EDGE]
    s_beyond, s_ahead = aseg[margin : margin + 1], bseg[EDGE - margin - 1 : EDGE - margin]
    stack = [
        jnp.where(col == s_last, jnp.exp(cf), 0.0),
        jnp.where(col == s_first, jnp.exp(total_r - cr), 0.0),
        jnp.where(col == s_first, jnp.exp(total_f - cf), 0.0),
        jnp.where(col == s_last, jnp.exp(cr), 0.0),
        jnp.where(early & (aseg == s_beyond), jnp.exp(nf[margin - 1 : margin] - nf), 0.0),
        jnp.where(
            late & (bseg == s_ahead), jnp.exp(pr[EDGE - margin : EDGE - margin + 1] - pr), 0.0
        ),
        jnp.where(early & (aseg == s_first), jnp.exp(nf), 0.0),
        jnp.where(late & (bseg == s_last), jnp.exp(pr), 0.0),
        jnp.where(
            j < 4,
            jnp.where(s_first == s_beyond, jnp.exp(nf[margin - 1 : margin]), 0.0),
            jnp.where(s_last == s_ahead, jnp.exp(pr[EDGE - margin : EDGE - margin + 1]), 0.0),
        ),
    ]
    turned = []
    for d in range(margin):
        move = (EDGE - d) % EDGE
        later = pltpu.roll(nf, move, 0) if d else nf
        seg_j = jnp.broadcast_to(aseg, (EDGE, 2 * heads))
        seg_l = pltpu.roll(seg_j, move, 0) if d else seg_j
        ao_d = pltpu.roll(ao, move, 0) if d else ao
        dot = jnp.sum(ai * ao_d, axis=1, keepdims=True)
        stack.append(jnp.where((j + d < margin) & (seg_j == seg_l), jnp.exp(later - nf) * dot, 0.0))
        former = pltpu.roll(pr, d, 0) if d else pr
        seg_j = jnp.broadcast_to(bseg, (EDGE, 2 * heads))
        seg_l = pltpu.roll(seg_j, d, 0) if d else seg_j
        bo_d = pltpu.roll(bo, d, 0) if d else bo
        dot = jnp.sum(bi * bo_d, axis=1, keepdims=True)
        stack.append(
            jnp.where((j - d >= EDGE - margin) & (seg_j == seg_l), jnp.exp(former - pr) * dot, 0.0)
        )
    stack = high_low(jnp.concatenate(stack, axis=0))
    ext[0:EDGE] = bs
    ext[EDGE : EDGE + length] = sig[...].astype(F32)
    ext[EDGE + length :] = as_
    width = channels // parts
    start = part * width
    widen[...] = spread(heads, channels, hdim)
    wide = 128
    first = iota((length, wide), 1) < hdim
    ao_b, bo_b = ao.astype(BF16), bo.astype(BF16)
    for c in range(0, width, wide):
        sl = slice(start + c, start + c + wide)
        to = slice(c, c + wide)
        e = mm(stack, widen[:, sl])
        skip_f, skip_r = skips[0:1, sl], skips[1:2, sl]
        pre = conv(ext, EDGE, length + EDGE, cw[0], cb[0:1, sl], sl, -1)
        sg = jax.nn.sigmoid(pre)
        act_f = (pre * sg)[0:length]
        slope_f = sg * (1.0 + pre * (1.0 - sg))
        pre = conv(ext, 0, length + EDGE, cw[1], cb[1:2, sl], sl, 1)
        sg = jax.nn.sigmoid(pre)
        act_r = (pre * sg)[EDGE:]
        slope_r = sg * (1.0 + pre * (1.0 - sg))
        act = jnp.concatenate([act_f.astype(BF16), act_r.astype(BF16)], axis=0)
        ct16 = cot[:, sl]
        ct = ct16.astype(F32)
        forth, back = [], []
        for k in range(wide // hdim):
            h = (start + c) // hdim + k
            m = weights[h]
            forth.append(mm(m, act))
            back.append(mm_tn(m, ct16))
        mixed[:, to] = jnp.where(first, forth[0], forth[1]) + skip_f * act_f + skip_r * act_r
        here_f = jnp.where(first, back[0][0:length], back[1][0:length]) + skip_f * ct
        here_r = jnp.where(first, back[0][length:], back[1][length:]) + skip_r * ct
        at = 4 * length
        ac_c, bc_c = ac[:, sl], bc[:, sl]
        row = iota((EDGE, wide), 0)
        beyond = jnp.where(row < margin, skip_f * ac_c, 0.0)
        ahead = jnp.where(row >= EDGE - margin, skip_r * bc_c, 0.0)
        for d in range(margin):
            k = at + (5 + 2 * d) * EDGE
            moved = pltpu.roll(ac_c, (EDGE - d) % EDGE, 0) if d else ac_c
            beyond += e[k : k + EDGE] * moved
            moved = pltpu.roll(bc_c, d, 0) if d else bc_c
            ahead += e[k + EDGE : k + 2 * EDGE] * moved
        out_f[:, to] = e[0:length]
        out_r[:, to] = e[length : 2 * length]
        base_f[0:length, to] = here_f * slope_f[0:length]
        base_f[length:, to] = beyond * slope_f[length:]
        gate_f[0:length, to] = e[2 * length : 3 * length] * slope_f[0:length]
        gate_f[length:, to] = e[at : at + EDGE] * slope_f[length:]
        base_r[EDGE:, to] = here_r * slope_r[EDGE:]
        base_r[0:EDGE, to] = ahead * slope_r[0:EDGE]
        gate_r[EDGE:, to] = e[3 * length : 4 * length] * slope_r[EDGE:]
        gate_r[0:EDGE, to] = e[at + EDGE : at + 2 * EDGE] * slope_r[0:EDGE]
        low[0:nstate, to] = mm_tn(ao_b, (ac_c * e[at + 2 * EDGE : at + 3 * EDGE]).astype(BF16))
        low[nstate : 2 * nstate, to] = mm_tn(
            bo_b, (bc_c * e[at + 3 * EDGE : at + 4 * EDGE]).astype(BF16)
        )
        low[2 * nstate :, to] = e[at + 4 * EDGE : at + 5 * EDGE]


def finish_kernel(*refs, outer, parts):
    entries = in_order(refs[:outer], THIRD)
    locals_ = [refs[outer + 8 * p : outer + 8 * (p + 1)] for p in range(parts)]
    in_, out, before, after, cw, mixed, grad, state, df, dr = refs[outer + 8 * parts :]
    length, channels = mixed.shape
    nstate = in_.shape[0]
    me = lax.axis_index("outer")
    width = channels // outer
    for r in range(outer):
        state[:, pl.ds(pl.multiple_of((me ^ r) * width, 128), width)] = entries[r][...]
    per = channels // parts
    query, key = out[...], in_[...]
    at = 2 * channels
    ahead, beyond = neighbours(before.at[:, at : at + 128], after.at[:, at : at + 128])
    ahead, beyond = ahead[:, :nstate].astype(BF16), beyond[:, :nstate].astype(BF16)
    lags = cw.shape[1]
    wide = 256
    for c in range(0, channels, wide):
        p, off = divmod(c, per)
        loc, base_f, gate_f, base_r, gate_r, out_f, out_r, low = locals_[p]
        to = slice(off, off + wide)
        sl = slice(c, c + wide)
        s = state[:, sl]
        mixed[:, sl] = (
            loc[:, to]
            + out_f[:, to] * mm_tn(query, s[0:nstate])
            + out_r[:, to] * mm_tn(query, s[2 * nstate : 3 * nstate])
        ).astype(BF16)
        s_br, s_bf = s[nstate : 2 * nstate], s[3 * nstate :]
        h_f = low[0:nstate, to] + low[2 * nstate : 2 * nstate + 1, to] * s_bf.astype(F32)
        h_r = low[nstate : 2 * nstate, to] + low[2 * nstate + 4 : 2 * nstate + 5, to] * s_br.astype(F32)
        df[0:length] = base_f[0:length, to] + gate_f[0:length, to] * mm_tn(key, h_f.astype(BF16))
        df[length:] = base_f[length:, to] + gate_f[length:, to] * mm(beyond, s_bf)
        dr[EDGE:] = base_r[EDGE:, to] + gate_r[EDGE:, to] * mm_tn(key, h_r.astype(BF16))
        dr[0:EDGE] = base_r[0:EDGE, to] + gate_r[0:EDGE, to] * mm(ahead, s_br)
        total = jnp.zeros((length, wide), F32)
        for lag in range(lags):
            total += cw[0, lag : lag + 1, sl] * df[lag : lag + length]
            total += cw[1, lag : lag + 1, sl] * dr[EDGE - lag : EDGE - lag + length]
        grad[:, sl] = total.astype(BF16)


def order(size, head):
    first = [r for r in head if r < size]
    return first + [r for r in reversed(range(1, size)) if r not in first]


def lay(arrays, head):
    return [arrays[0]] + [arrays[r] for r in order(len(arrays), head)]


def in_order(refs, head):
    found = dict(zip([0] + order(len(refs), head), refs))
    return [found[r] for r in range(len(refs))]


def params():
    return pltpu.CompilerParams(vmem_limit_bytes=VMEM)


def cost(flops, size):
    return pl.CostEstimate(flops=flops, bytes_accessed=size, transcendentals=0)


def on_device(
    signal, in_coeff, out_coeff, cotangent, conv_weight, conv_bias, skip_gain, decay_table,
    bucket, segment, *, outer, inner,
):
    length, channels = signal.shape
    heads = skip_gain.shape[1]
    nstate = in_coeff.shape[1]
    axes = ("inner", "outer")
    count = outer * inner
    bucket = bucket.reshape(1, length)
    segment = segment.reshape(1, length)
    sds = jax.ShapeDtypeStruct
    width = channels // outer
    pay = 4 * nstate + 4 * EDGE
    far = 2 * nstate + 3 * EDGE
    in_t, out_t = in_coeff.T, out_coeff.T
    steps = tuple(reversed(range(outer)))
    small = (bucket, segment, decay_table, conv_weight, conv_bias, in_t, out_t)
    operands = [
        pltpu.with_memory_space_constraint(a, pltpu.HBM) for a in (*small, signal, cotangent)
    ]
    *blocks, sums, sums_t = pl.pallas_call(
        functools.partial(begin_kernel, outer=outer, steps=steps),
        name="begin",
        in_specs=[pl.BlockSpec(memory_space=pltpu.HBM)] * len(operands),
        out_shape=[sds((pay, width), BF16)] * outer
        + [sds((3, length, 2 * heads), F32), sds((2 * heads, length), F32)],
        scratch_shapes=[pltpu.VMEM(a.shape, a.dtype) for a in small]
        + [pltpu.VMEM((length, channels), BF16)] * 2
        + [
            pltpu.VMEM((length + 2 * EDGE, width), F32),
            pltpu.VMEM((8 * heads, length), F32),
            pltpu.SemaphoreType.DMA((len(small) + 2 * outer,)),
        ],
        compiler_params=params(),
        cost_estimate=cost(10**8, 2**20),
    )(*operands)
    blocks = blocks[::-1]

    def swap(array, axis, size, r):
        return lax.ppermute(array, axis, [(i, i ^ r) for i in range(size)])

    def exchange(arrays, axis, size):
        got = {r: swap(arrays[r], axis, size, r) for r in reversed(range(1, size))}
        return [got[r] for r in range(1, size)]

    blocks = [blocks[0], *exchange(blocks, "outer", outer)]
    line = 2 * channels + 512
    late_bucket, _ = lax.optimization_barrier((bucket, sums))
    near_rows, next_rows = pl.pallas_call(
        edges_kernel,
        name="edges",
        out_shape=[sds((EDGE, line), BF16)] * 2,
        compiler_params=params(),
        cost_estimate=cost(10**6, 2**18),
    )(signal, cotangent, in_t, out_t, late_bucket, segment)
    before = lax.ppermute(near_rows, "outer", [(i, i ^ 1) for i in range(outer)])
    weights, skips = pl.pallas_call(
        weights_kernel,
        name="weights",
        out_shape=[sds((heads, length, 2 * length), BF16), sds((2, channels), F32)],
        compiler_params=params(),
        cost_estimate=cost(10**8, 2**21),
    )(in_t, out_t, segment, skip_gain, sums, sums_t)
    blocks[0], weights = lax.optimization_barrier((blocks[0], weights))
    pairs = [(i, i + 1) for i in range(1, count - 1, 2)]
    after = lax.ppermute(next_rows, axes, pairs + [(j, i) for i, j in pairs])
    parts = 2

    def local(part):
        per = channels // parts
        both_rows = length + EDGE
        return pl.pallas_call(
            functools.partial(local_kernel, part=part, parts=parts),
            name=f"local{part}",
            out_shape=[
                sds((length, per), F32),
                sds((both_rows, per), F32),
                sds((both_rows, per), F32),
                sds((both_rows, per), F32),
                sds((both_rows, per), F32),
                sds((length, per), F32),
                sds((length, per), F32),
                sds((2 * nstate + EDGE, per), F32),
            ],
            scratch_shapes=[
                pltpu.VMEM((length + 2 * EDGE, channels), F32),
                pltpu.VMEM((2 * heads, channels), BF16),
            ],
            compiler_params=params(),
            cost_estimate=cost(4 * 10**8, 2**22),
        )(
            signal, cotangent, in_t, out_t, segment, conv_weight, conv_bias, decay_table, sums,
            weights, skips, before, after,
        )

    locals_ = [local(p) for p in range(parts)]
    totals = pl.pallas_call(
        functools.partial(totals_kernel, outer=outer, inner=inner, nstate=nstate),
        name="totals",
        out_shape=[sds((far, width), BF16)] * (inner - 1),
        scratch_shapes=[pltpu.VMEM((outer, pay, width), BF16)],
        compiler_params=params(),
        cost_estimate=cost(10**6, 2**19),
    )(*lay(blocks, FIRST), conv_weight, conv_bias)
    totals = exchange([None, *totals], "inner", inner)
    entries = pl.pallas_call(
        functools.partial(entries_kernel, outer=outer, inner=inner, nstate=nstate),
        name="entries",
        out_shape=[sds((4 * nstate, width), BF16)] * outer,
        scratch_shapes=[
            pltpu.VMEM((outer, pay, width), BF16),
            pltpu.VMEM((inner, far, width), F32),
            pltpu.VMEM((outer, 4 * nstate, width), BF16),
        ],
        compiler_params=params(),
        cost_estimate=cost(10**6, 2**19),
    )(*lay(blocks, FIRST), *lay([None, *totals], SECOND)[1:], conv_weight, conv_bias)
    entries = [entries[0], *exchange(entries, "outer", outer)]
    return pl.pallas_call(
        functools.partial(finish_kernel, outer=outer, parts=parts),
        name="finish",
        out_shape=[sds((length, channels), BF16)] * 2,
        scratch_shapes=[
            pltpu.VMEM((4 * nstate, channels), BF16),
            pltpu.VMEM((length + EDGE, 256), F32),
            pltpu.VMEM((length + EDGE, 256), F32),
        ],
        compiler_params=params(),
        cost_estimate=cost(10**8, 2**22),
    )(*lay(entries, THIRD), *[a for group in locals_ for a in group], in_t, out_t, before, after, conv_weight)


def solution(mesh):
    rows = P(("groups", "inner", "outer"), None)
    flat = P(("groups", "inner", "outer"))
    return jax.shard_map(
        functools.partial(on_device, outer=mesh.shape["outer"], inner=mesh.shape["inner"]),
        mesh=mesh,
        in_specs=(rows, rows, rows, rows, P(), P(), P(), P(), flat, flat),
        out_specs=(rows, rows),
        check_vma=False,
    )
```
